128 devices in a mesh: role: 2 (over z_hi), gx: 8 (over y, z_lo), gy: 8 (over x, core).
Axes of the slice: x: 4, y: 4, z: 4 (z_hi: 2, z_lo: 2; z = z_hi * 2 + z_lo), core: 2. Of those that a mesh axis runs over, the one named last changes fastest.
Arguments:
- design: float32 [256, 256, 256], P(('gx', 'gy'), None, 'role'), may hold values from 0 to 1
- force: float32 [3, 128, 128, 256], P(None, 'gx', 'gy', 'role'), may hold values from -6 to 6
- clamped_dof_mask: int32 [3, 128, 128, 256], P(None, 'gx', 'gy', 'role'), may hold values 0 or 1
- stiffness: float32 [81, 81], replicated, may hold values from -1 to 70, as said below
Outputs:
- sensitivity: float32 [256, 256, 256], P(('gx', 'gy'), None, 'role')
- displacement: float32 [3, 128, 128, 256], P(None, 'gx', 'gy', 'role')
The draws below stay inside these ranges and needn't reach their ends.
Inputs may be any that keep to these rules, and one draw needn't show every extreme that they name: `stiffness`: symmetric, and each diagonal entry exceeds the sum of the magnitudes of the other entries of its row.
All inputs are finite; a program needn't handle non-finite values. No bound on the sum of `clamped_dof_mask` on one device may be relied on, other than what follows from the above.
Results may differ from the reference program's by a relative error of at most 0.00013.
Values sent between devices are 32-bit elements; how exact they have to be, the bound alone decides.
A program may use at most 64 MiB of HBM per device.

```python
import jax
import jax.numpy as jnp
from jax import lax

ITERS = 3
RADIUS = 2
ELEMENTS_X = 64
ELEMENTS_Y = 64
ELEMENTS_Z = 128
FX = 256
FY = 256
FZ = 256


def draw_stiffness(key, part):
    first_key, second_key = jax.random.split(jax.random.fold_in(key, 11))
    raw = jnp.clip(jax.random.normal(first_key, (81, 81), jnp.float32), -4.0, 4.0) / 9.0
    identity = jnp.eye(81, dtype=jnp.float32)
    symmetric = (raw + raw.T) * 0.7071
    offdiag = symmetric * (1.0 - identity)
    diagonal = 1.25 * jnp.sum(jnp.abs(offdiag), axis=1) + jax.random.uniform(second_key, (81,), jnp.float32, 0.5, 2.0)
    return offdiag + diagonal[:, None] * identity


def plant(values, key, smallest, high):
    longest = values.shape.index(max(values.shape))
    spots = []
    for shift in (0, 1):
        where = [jax.random.randint(jax.random.fold_in(key, axis), (), 0, length) for axis, length in enumerate(values.shape)]
        where[longest] = (where[longest] + shift) % values.shape[longest]
        spots.append(tuple(where))
    return values.at[spots[0]].set(smallest).at[spots[1]].set(high)


def level_of(key, shape, cuts, least, top_value):
    def one(dim, shards_of):
        heights = jax.random.uniform(jax.random.fold_in(jax.random.fold_in(key, 6), dim), (shards_of,), jnp.float32, least / len(cuts), top_value / len(cuts))
        return jnp.repeat(jnp.exp(heights), shape[dim] // shards_of).reshape((-1,) + (1,) * (len(shape) - dim - 1))

    loudness = one(*cuts[0])
    for cut in cuts[1:]:
        loudness = loudness * one(*cut)
    return loudness


def normal_values(own_key, shape, scale, bound, cuts=(), kind=jnp.bfloat16):
    drawn = jax.random.normal(own_key, shape, jnp.float32) * scale
    if len(cuts) > 0:
        drawn = level_of(own_key, shape, cuts, -0.22, 0.18) * drawn
    return jnp.clip(drawn, min=-bound, max=bound).astype(kind)


def setup_inputs(seed: int = 0) -> dict:
    arg_keys = jax.random.split(jax.random.key(seed), 5)
    design = jnp.clip(1.0 * jax.random.uniform(arg_keys[0], (FX, FY, FZ), jnp.float32) ** level_of(arg_keys[0], (FX, FY, FZ), ((0, 64), (2, 2)), -0.2, 0.2), 0.0, 1.0)
    force = normal_values(arg_keys[1], (3, 2 * ELEMENTS_X, 2 * ELEMENTS_Y, 2 * ELEMENTS_Z), 1.0, 6.0, ((1, 8), (2, 8), (3, 2)), jnp.float32)
    clamped_dof_mask = plant((jax.random.randint(arg_keys[2], (3, 2 * ELEMENTS_X, 2 * ELEMENTS_Y, 2 * ELEMENTS_Z), 0, 8) < 1).astype(jnp.int32), jax.random.fold_in(arg_keys[2], 1), 0, 1)
    stiffness = draw_stiffness(jax.random.fold_in(arg_keys[4], 71), 0)
    return {"design": design, "force": force, "clamped_dof_mask": clamped_dof_mask, "stiffness": stiffness}


sharpness = 4.0
threshold = 0.5
floor_stiff = 0.001


def hat_list():
    return [float(RADIUS + 1 - abs(shift_idx - RADIUS)) for shift_idx in range(2 * RADIUS + 1)]


def smooth_axis(padded, axis_num, length):
    result = None
    for offset_idx, weight in enumerate(hat_list()):
        portion = weight * lax.slice_in_dim(padded, offset_idx, offset_idx + length, axis=axis_num)
        result = portion if result is None else result + portion
    return result


def axis_count(start, length, extent):
    places = start + jnp.arange(length, dtype=jnp.int32)
    counted = jnp.zeros((length,), jnp.float32)
    for offset_idx, weight in enumerate(hat_list()):
        target = places + (offset_idx - RADIUS)
        inside = jnp.logical_and(target >= 0, target < extent)
        counted = counted + weight * inside.astype(jnp.float32)
    return counted


def smooth_all(field):
    extent_x, extent_y, extent_z = field.shape
    padded = jnp.pad(field, RADIUS)
    return smooth_axis(smooth_axis(smooth_axis(padded, 2, extent_z), 1, extent_y), 0, extent_x)


def heaviside_projection(values):
    scaled = jnp.tanh(sharpness * threshold) + jnp.tanh(sharpness * (1.0 - threshold))
    return (jnp.tanh(sharpness * threshold) + jnp.tanh(sharpness * (values - threshold))) / scaled


def slope(values):
    scaled = jnp.tanh(sharpness * threshold) + jnp.tanh(sharpness * (1.0 - threshold))
    bent = jnp.tanh(sharpness * (values - threshold))
    return sharpness * (1.0 - bent * bent) / scaled


def element_mean(fine):
    count_x = fine.shape[0] // 4
    count_y = fine.shape[1] // 4
    count_z = fine.shape[2] // 2
    return fine.reshape(count_x, 4, count_y, 4, count_z, 2).mean(axis=(1, 3, 5))


def spread(elements):
    count_x, count_y, count_z = elements.shape
    widened = jnp.broadcast_to(elements[:, None, :, None, :, None], (count_x, 4, count_y, 4, count_z, 2))
    return widened.reshape(4 * count_x, 4 * count_y, 2 * count_z)


def split_axis(values, axis_num):
    half_len = (values.shape[axis_num] - 1) // 2
    pieces = [lax.slice_in_dim(values, corner, corner + 2 * half_len - 1, stride=2, axis=axis_num) for corner in range(3)]
    return jnp.stack(pieces, axis=0)


def split_nodes(values):
    stacked = split_axis(values, 1)
    stacked = split_axis(stacked, 3)
    stacked = split_axis(stacked, 5)
    return stacked.reshape(81, -1)


def merge_axis(parts, axis_num):
    opening = parts[0]
    middle = parts[1]
    closing = parts[2]
    length = opening.shape[axis_num]
    before = [(0, 0)] * opening.ndim
    before[axis_num] = (0, 1)
    behind = [(0, 0)] * opening.ndim
    behind[axis_num] = (1, 0)
    evens = jnp.pad(opening, before) + jnp.pad(closing, behind)
    leading = lax.slice_in_dim(evens, 0, length, axis=axis_num)
    ending = lax.slice_in_dim(evens, length, length + 1, axis=axis_num)
    braided = jnp.stack([leading, middle], axis=axis_num + 1)
    new_shape = list(leading.shape)
    new_shape[axis_num] = 2 * length
    return jnp.concatenate([braided.reshape(new_shape), ending], axis=axis_num)


def merge_nodes(stiffness_product, element_shape):
    reshaped = stiffness_product.reshape((3, 3, 3, 3) + tuple(element_shape))
    merged = merge_axis(reshaped, 5)
    merged = merge_axis(merged, 3)
    return merge_axis(merged, 1)


def conjugate_gradient_solve(operate, inner_sum, rhs):
    solution = jnp.zeros_like(rhs)
    residual = rhs
    direction = rhs
    current = inner_sum(residual, residual)
    for sweep in range(ITERS):
        applied = operate(direction)
        step_len = current / inner_sum(direction, applied)
        solution = solution + step_len * direction
        residual = residual - step_len * applied
        updated = inner_sum(residual, residual)
        direction = residual + (updated / current) * direction
        current = updated
    return solution


def reference(design, force, clamped_dof_mask, stiffness):
    extent_x, extent_y, extent_z = design.shape
    filter_weight_grid = (axis_count(0, extent_x, extent_x)[:, None, None]
                   * axis_count(0, extent_y, extent_y)[None, :, None]
                   * axis_count(0, extent_z, extent_z)[None, None, :])
    filtered = smooth_all(design) / filter_weight_grid
    density = element_mean(heaviside_projection(filtered))
    factor = floor_stiff + (1.0 - floor_stiff) * density ** 3
    behind = ((0, 0), (0, 1), (0, 1), (0, 1))
    free = jnp.pad((1 - clamped_dof_mask).astype(jnp.float32), behind)
    rhs = free * jnp.pad(force, behind)
    scales = factor.reshape(-1)

    def operate(values):
        columns = split_nodes(free * values)
        stiffness_product = jnp.dot(stiffness, columns, precision=lax.Precision.HIGHEST,
                          preferred_element_type=jnp.float32) * scales[None, :]
        return free * merge_nodes(stiffness_product, factor.shape)

    def inner_sum(left, right):
        return jnp.sum(left * right)

    solution = conjugate_gradient_solve(operate, inner_sum, rhs)
    columns = split_nodes(solution)
    energy = jnp.sum(columns * jnp.dot(stiffness, columns, precision=lax.Precision.HIGHEST,
                                       preferred_element_type=jnp.float32), axis=0).reshape(factor.shape)
    element_grad = -3.0 * density ** 2 * (1.0 - floor_stiff) * energy / 32.0
    voxel_grad = spread(element_grad) * slope(filtered)
    sensitivity = smooth_all(voxel_grad / filter_weight_grid)
    return sensitivity, solution[:, :-1, :-1, :-1]
```

```python
import jax
import jax.numpy as jnp
import numpy as np
from jax import lax
from jax.experimental import pallas as pl
from jax.experimental.pallas import tpu as pltpu
from jax.sharding import PartitionSpec as P

ITERS = 3
RADIUS = 2
GX_GY = ("gx", "gy")


sharpness = 4.0
threshold = 0.5
floor_stiff = 0.001


def with_halo(block, sides, width):
    for axis, dim in sides:
        count = lax.axis_size(axis)
        forward = [(i, i + 1) for i in range(count - 1)]
        backward = [(target, source) for source, target in forward]
        low = lax.ppermute(
            lax.slice_in_dim(block, block.shape[dim] - width, None, axis=dim), axis, forward
        )
        high = lax.ppermute(lax.slice_in_dim(block, 0, width, axis=dim), axis, backward)
        block = jnp.concatenate([low, block, high], axis=dim)
    return block


def hat_list():
    return [float(RADIUS + 1 - abs(shift_idx - RADIUS)) for shift_idx in range(2 * RADIUS + 1)]


def smooth_axis(padded, axis_num, length):
    result = None
    for offset_idx, weight in enumerate(hat_list()):
        portion = weight * lax.slice_in_dim(padded, offset_idx, offset_idx + length, axis=axis_num)
        result = portion if result is None else result + portion
    return result


def axis_count(start, length, extent):
    places = start + jnp.arange(length, dtype=jnp.int32)
    counted = jnp.zeros((length,), jnp.float32)
    for offset_idx, weight in enumerate(hat_list()):
        target = places + (offset_idx - RADIUS)
        inside = jnp.logical_and(target >= 0, target < extent)
        counted = counted + weight * inside.astype(jnp.float32)
    return counted


def slab_weight(shape):
    extent_x, extent_y, extent_z = shape
    along_x = axis_count(
        lax.axis_index(GX_GY) * extent_x, extent_x, extent_x * lax.axis_size(GX_GY)
    )
    along_y = axis_count(0, extent_y, extent_y)
    along_z = axis_count(
        lax.axis_index("role") * extent_z, extent_z, extent_z * lax.axis_size("role")
    )
    return along_x[:, None, None] * along_y[None, :, None] * along_z[None, None, :]


def slab_smooth(field):
    extent_x, extent_y, extent_z = field.shape
    padded = with_halo(field, (("role", 2), (GX_GY, 0)), RADIUS)
    padded = jnp.pad(padded, ((0, 0), (RADIUS, RADIUS), (0, 0)))
    return smooth_axis(smooth_axis(smooth_axis(padded, 2, extent_z), 1, extent_y), 0, extent_x)


def heaviside_projection(values):
    scaled = jnp.tanh(sharpness * threshold) + jnp.tanh(sharpness * (1.0 - threshold))
    return (jnp.tanh(sharpness * threshold) + jnp.tanh(sharpness * (values - threshold))) / scaled


def slope(values):
    scaled = jnp.tanh(sharpness * threshold) + jnp.tanh(sharpness * (1.0 - threshold))
    bent = jnp.tanh(sharpness * (values - threshold))
    return sharpness * (1.0 - bent * bent) / scaled


def element_mean(fine):
    count_x = fine.shape[0] // 4
    count_y = fine.shape[1] // 4
    count_z = fine.shape[2] // 2
    return fine.reshape(count_x, 4, count_y, 4, count_z, 2).mean(axis=(1, 3, 5))


def spread(elements):
    count_x, count_y, count_z = elements.shape
    widened = jnp.broadcast_to(
        elements[:, None, :, None, :, None], (count_x, 4, count_y, 4, count_z, 2)
    )
    return widened.reshape(4 * count_x, 4 * count_y, 2 * count_z)


MESH = pl.DeviceIdType.MESH
VMEM = pl.BlockSpec(memory_space=pltpu.VMEM)
ANY = pl.BlockSpec(memory_space=pl.ANY)
F32 = jnp.float32
ROWS = 112
LANES = 128
GXN = 8
YN = 16
CHUNKS = (
    (0, 0, 0), (0, 0, 1), (0, 0, 2), (0, 0, 3), (0, 0, 4), (0, 0, 5),
    (1, 0, 0), (1, 0, 1), (1, 0, 4),
    (0, 1, 0), (0, 1, 2), (0, 1, 6),
    (1, 1, 0), (1, 1, 4),
)
PAIRS = {4: ((0, 0), (0, 1)), 5: ((1, 0), (1, 1)), 6: ((0, 0), (1, 0))}


def row_table():
    table = np.zeros((ROWS, 81), np.float32)
    seen = set()
    for place, (dx, dy, kind) in enumerate(CHUNKS):
        for half in range(2):
            if kind < 4:
                px, py, c = kind // 2, kind % 2, half
            else:
                (px, py), c = PAIRS[kind][half], 2
            if (dx and px) or (dy and py):
                continue
            a, b = px + 2 * dx, py + 2 * dy
            for q in range(3):
                index = ((c * 3 + b) * 3 + a) * 3 + q
                assert index not in seen
                seen.add(index)
                table[place * 8 + half * 4 + q, index] = 1.0
    assert len(seen) == 81
    return table


def place_of():
    role, gx, gy = lax.axis_index("role"), lax.axis_index("gx"), lax.axis_index("gy")
    return role, gx, gy, 2 * gy + role


def device_at(gx, row):
    gx = lax.rem(gx + GXN, GXN)
    row = lax.rem(row + YN, YN)
    return {"role": lax.rem(row, 2), "gx": gx, "gy": lax.div(row, 2)}


def greet(devices):
    barrier = pltpu.get_barrier_semaphore()
    for device in devices:
        pl.semaphore_signal(barrier, inc=1, device_id=device, device_id_type=MESH)
    pl.semaphore_wait(barrier, len(devices))


def remote(src, dst, send, recv, device):
    return pltpu.make_async_remote_copy(
        src_ref=src, dst_ref=dst, send_sem=send, recv_sem=recv, device_id=device, device_id_type=MESH
    )


def params(ident=None):
    if ident is None:
        return pltpu.CompilerParams(vmem_limit_bytes=48 * 1024 * 1024)
    return pltpu.CompilerParams(collective_id=ident, has_side_effects=True, vmem_limit_bytes=32 * 1024 * 1024)


def parity_matrix(role, natural_own):
    rows = lax.broadcasted_iota(jnp.int32, (256, 256), 0)
    cols = lax.broadcasted_iota(jnp.int32, (256, 256), 1)
    half = jnp.where(rows < LANES, role, 1 - role)
    spot = half * LANES + lax.rem(rows, LANES)
    want = 2 * lax.rem(cols, LANES) + lax.div(cols, LANES)
    return (spot == want).astype(F32)


def pack_kernel(force_ref, free_ref, out_ref):
    role = lax.axis_index("role")
    matrix = parity_matrix(role, True)
    upper = lax.broadcasted_iota(jnp.int32, (8, LANES), 0) < 4

    def body(e, _):
        for px in range(2):
            x = 2 * e + px
            both = []
            for ref, precision in ((force_ref, lax.Precision.HIGHEST), (free_ref, None)):
                wide = jnp.dot(
                    ref[x].reshape(64, 256), matrix, precision=precision, preferred_element_type=F32
                )
                both.append(wide)
            for f in range(4):
                for py in range(2):
                    y = 2 * f + py
                    vals = [
                        jnp.where(upper, w[8 * y : 8 * y + 8, :LANES], w[8 * y : 8 * y + 8, LANES:])
                        for w in both
                    ]
                    out_ref[0, e, f, px, py] = vals[0] * vals[1]
                    out_ref[1, e, f, px, py] = vals[1]
        return 0

    lax.fori_loop(0, 8, body, 0)


def start_exchange_kernel(vf_ref, dens_ref, xhi_ref, yhi_ref, corner_ref, dall_ref, send, recv, own):
    role, gx, gy, row = place_of()
    group = [device_at(gx, row + k) for k in range(1, YN)]
    greet(
        group
        + [device_at(gx + 1, row), device_at(gx - 1, row), device_at(gx + 1, row + 1), device_at(gx - 1, row - 1)]
    )
    copies = []
    for k in range(1, YN):
        target = lax.rem(row + k, YN)
        copies.append(
            remote(dens_ref.at[target], dall_ref.at[row], send.at[k], recv.at[k], group[k - 1])
        )
    copies.append(remote(vf_ref.at[:, 0, :, 0], xhi_ref, send.at[16], recv.at[16], device_at(gx - 1, row)))
    copies.append(remote(vf_ref.at[:, :, 0, :, 0], yhi_ref, send.at[17], recv.at[17], device_at(gx, row - 1)))
    copies.append(
        remote(vf_ref.at[:, 0, 0, 0, 0], corner_ref, send.at[18], recv.at[18], device_at(gx - 1, row - 1))
    )
    for copy in copies:
        copy.start()
    mine = pltpu.make_async_copy(dens_ref.at[row], dall_ref.at[row], own)
    mine.start()
    mine.wait()
    for copy in copies:
        copy.wait()


def start_exchange(vf, dens):
    return pl.pallas_call(
        start_exchange_kernel,
        out_shape=(
            jax.ShapeDtypeStruct((2, 4, 2, 8, LANES), F32),
            jax.ShapeDtypeStruct((2, 8, 2, 8, LANES), F32),
            jax.ShapeDtypeStruct((2, 8, LANES), F32),
            jax.ShapeDtypeStruct((YN, 8, LANES), F32),
        ),
        in_specs=[ANY, ANY],
        out_specs=(ANY,) * 4,
        scratch_shapes=[pltpu.SemaphoreType.DMA((19,)), pltpu.SemaphoreType.DMA((19,)), pltpu.SemaphoreType.DMA],
        compiler_params=params(1),
        name="start_exchange",
    )(vf, dens)


def reduce_parts(tile_ref, slots, second, total, send, recv, gx, row, base):
    slots[row] = tile_ref[...]
    copies = []
    for k in range(1, YN):
        copies.append(
            remote(tile_ref, slots.at[row], send.at[base + k], recv.at[base + k], device_at(gx, row + k))
        )
    for copy in copies:
        copy.start()
    for copy in copies:
        copy.wait()
    part = slots[0]
    for k in range(1, YN):
        part = part + slots[k]
    total[...] = part
    second[gx] = part
    base = base + YN
    copies = []
    for k in range(1, GXN):
        copies.append(
            remote(total, second.at[gx], send.at[base + k], recv.at[base + k], device_at(gx + k, row))
        )
    for copy in copies:
        copy.start()
    for copy in copies:
        copy.wait()
    part = second[0]
    for k in range(1, GXN):
        part = part + second[k]
    return part


def face_moves():
    return (
        (1, 0), (-1, 0), (0, 1), (0, -1), (1, 1), (1, -1), (-1, 1), (-1, -1),
    )


def face_exchange_kernel(
    image_ref, tile_ref, xlo, xhi, ylo, yhi, corners, sum_ref, slots, second, total, send, recv
):
    role, gx, gy, row = place_of()
    greet(
        [device_at(gx, row + k) for k in range(1, YN)]
        + [device_at(gx + k, row) for k in range(1, GXN)]
        + [device_at(gx + dx, row + dy) for dx, dy in face_moves()[4:]]
    )
    ends = (
        (image_ref.at[8, :, 0], xlo),
        (image_ref.at[0, :, 0], xhi),
        (image_ref.at[:, 4, :, 0], ylo),
        (image_ref.at[:, 0, :, 0], yhi),
        (image_ref.at[8, 4, 0, 0], corners.at[0]),
        (image_ref.at[8, 0, 0, 0], corners.at[1]),
        (image_ref.at[0, 4, 0, 0], corners.at[2]),
        (image_ref.at[0, 0, 0, 0], corners.at[3]),
    )
    copies = []
    for k, ((dx, dy), (src, dst)) in enumerate(zip(face_moves(), ends)):
        copies.append(remote(src, dst, send.at[k], recv.at[k], device_at(gx + dx, row + dy)))
    for copy in copies:
        copy.start()
    sum_ref[...] = reduce_parts(tile_ref, slots, second, total, send, recv, gx, row, 8)
    for copy in copies:
        copy.wait()


REDUCE_SCRATCH = [
    pltpu.VMEM((YN, 8, LANES), F32),
    pltpu.VMEM((GXN, 8, LANES), F32),
    pltpu.VMEM((8, LANES), F32),
]


def face_exchange(image, tile, ident):
    return pl.pallas_call(
        face_exchange_kernel,
        out_shape=(
            jax.ShapeDtypeStruct((5, 2, 8, LANES), F32),
            jax.ShapeDtypeStruct((5, 2, 8, LANES), F32),
            jax.ShapeDtypeStruct((9, 2, 8, LANES), F32),
            jax.ShapeDtypeStruct((9, 2, 8, LANES), F32),
            jax.ShapeDtypeStruct((4, 8, LANES), F32),
            jax.ShapeDtypeStruct((8, LANES), F32),
        ),
        in_specs=[ANY, VMEM],
        out_specs=(ANY,) * 5 + (VMEM,),
        scratch_shapes=REDUCE_SCRATCH
        + [pltpu.SemaphoreType.DMA((32,)), pltpu.SemaphoreType.DMA((32,))],
        compiler_params=params(ident),
        name="face_exchange",
    )(image, tile)


def reduce_kernel(tile_ref, sum_ref, slots, second, total, send, recv):
    role, gx, gy, row = place_of()
    greet(
        [device_at(gx, row + k) for k in range(1, YN)] + [device_at(gx + k, row) for k in range(1, GXN)]
    )
    sum_ref[...] = reduce_parts(tile_ref, slots, second, total, send, recv, gx, row, 0)


def reduce_all(tile, ident):
    return pl.pallas_call(
        reduce_kernel,
        out_shape=jax.ShapeDtypeStruct((8, LANES), F32),
        in_specs=[VMEM],
        out_specs=VMEM,
        scratch_shapes=REDUCE_SCRATCH
        + [pltpu.SemaphoreType.DMA((24,)), pltpu.SemaphoreType.DMA((24,))],
        compiler_params=params(ident),
        name="reduce_all",
    )(tile)


def gradient_exchange_kernel(grad_ref, all_ref, send, recv, own):
    role, gx, gy, row = place_of()
    greet([device_at(gx, row + k) for k in range(1, YN)])
    copies = []
    for k in range(1, YN):
        target = lax.rem(row + k, YN)
        copies.append(
            remote(
                grad_ref.at[lax.div(target, 2)], all_ref.at[row], send.at[k], recv.at[k], device_at(gx, row + k)
            )
        )
    for copy in copies:
        copy.start()
    mine = pltpu.make_async_copy(grad_ref.at[gy], all_ref.at[row], own)
    mine.start()
    mine.wait()
    for copy in copies:
        copy.wait()


def gradient_exchange(grad):
    return pl.pallas_call(
        gradient_exchange_kernel,
        out_shape=jax.ShapeDtypeStruct((YN, 8, LANES), F32),
        in_specs=[ANY],
        out_specs=ANY,
        scratch_shapes=[pltpu.SemaphoreType.DMA((16,)), pltpu.SemaphoreType.DMA((16,)), pltpu.SemaphoreType.DMA],
        compiler_params=params(5),
        name="gradient_exchange",
    )(grad)


def matrix_pieces(table_ref):
    whole = table_ref[...]
    high = whole.astype(jnp.bfloat16)
    low = (whole - high.astype(F32)).astype(jnp.bfloat16)
    return jnp.concatenate(
        [
            jnp.concatenate([high, high], axis=1),
            jnp.concatenate([low, jnp.zeros_like(low)], axis=1),
        ],
        axis=0,
    )


def build_store(field, store):
    sub = lax.broadcasted_iota(jnp.int32, (8, LANES), 0) < 4
    inside = lax.broadcasted_iota(jnp.int32, (8, LANES), 1) < LANES - 1

    def body(e, _):
        for f in range(5):
            held = [field[e, f, k // 2, k % 2] for k in range(4)]
            shifted = [jnp.where(inside, pltpu.roll(v, LANES - 1, 1), 0.0) for v in held]
            turned = [None] + [pltpu.roll(v, 4, 0) for v in shifted[1:]]
            for k in range(4):
                store[e, f, k] = held[k]
            store[e, f, 4] = jnp.where(sub, shifted[0], turned[1])
            store[e, f, 5] = jnp.where(sub, shifted[2], turned[3])
            store[e, f, 6] = jnp.where(sub, shifted[0], turned[2])
        return 0

    lax.fori_loop(0, 9, body, 0)


def element_product(store, pieces, e):
    columns = []
    for f in range(4):
        columns.append(jnp.concatenate([store[e + dx, f + dy, kind] for dx, dy, kind in CHUNKS], axis=0))
    wide = jnp.concatenate(columns, axis=1)
    high = wide.astype(jnp.bfloat16)
    low = (wide - high.astype(F32)).astype(jnp.bfloat16)
    out = jnp.dot(pieces, jnp.concatenate([high, low], axis=0), preferred_element_type=F32)
    product = out[:ROWS] + out[ROWS:]
    return columns, [product[:, f * LANES : (f + 1) * LANES] for f in range(4)]


def chunk_sum(left, right):
    both = left * right
    total = both[:8]
    for k in range(1, len(CHUNKS)):
        total = total + both[8 * k : 8 * k + 8]
    return total


def density_rows(dall_ref, e):
    return dall_ref[2 * e] + dall_ref[2 * e + 1]


def apply_operator(store, acc, pieces, dall_ref, image_ref):
    acc[...] = jnp.zeros_like(acc)

    def body(e, energy):
        columns, products = element_product(store, pieces, e)
        rho = density_rows(dall_ref, e)
        factor = floor_stiff + (1.0 - floor_stiff) * rho * rho * rho
        for f in range(4):
            scaled = products[f] * factor[f : f + 1, :]
            energy = energy + chunk_sum(columns[f], scaled)
            for place, (dx, dy, kind) in enumerate(CHUNKS):
                acc[e + dx, f + dy, kind] += scaled[8 * place : 8 * place + 8]
        return energy

    energy = lax.fori_loop(0, 8, body, jnp.zeros((8, LANES), F32))
    sub = lax.broadcasted_iota(jnp.int32, (8, LANES), 0) < 4
    inside = lax.broadcasted_iota(jnp.int32, (8, LANES), 1) > 0

    def fold(e, _):
        for f in range(5):
            z0, z1, z2 = acc[e, f, 4], acc[e, f, 5], acc[e, f, 6]
            t0, t1, t2 = (pltpu.roll(v, 4, 0) for v in (z0, z1, z2))
            for k, extra in enumerate((z0 + z2, t0, z1 + t2, t1)):
                extra = jnp.where(jnp.logical_and(sub, inside), pltpu.roll(extra, 1, 1), 0.0)
                image_ref[e, f, k // 2, k % 2] = acc[e, f, k] + extra
        return 0

    lax.fori_loop(0, 9, fold, 0)
    return energy


def element_energy(store, pieces, dall_ref):
    def body(e, energy):
        columns, products = element_product(store, pieces, e)
        rho = density_rows(dall_ref, e)
        factor = floor_stiff + (1.0 - floor_stiff) * rho * rho * rho
        for f in range(4):
            energy = energy + chunk_sum(columns[f], products[f] * factor[f : f + 1, :])
        return energy

    return lax.fori_loop(0, 8, body, jnp.zeros((8, LANES), F32))


def square_sum(field):
    def body(e, total):
        for f in range(4):
            for k in range(4):
                held = field[e, f, k // 2, k % 2]
                total = total + held * held
        return total

    return lax.fori_loop(0, 8, body, jnp.zeros((8, LANES), F32))


def sums_tile(gamma, delta):
    rows = lax.broadcasted_iota(jnp.int32, (8, LANES), 0)
    gamma = jnp.sum(gamma, axis=0, keepdims=True)
    delta = jnp.sum(delta, axis=0, keepdims=True)
    return jnp.where(rows == 0, gamma, jnp.where(rows == 1, delta, 0.0))


def read_sums(sum_ref):
    return (
        jnp.sum(sum_ref[0:1, :], axis=1, keepdims=True),
        jnp.sum(sum_ref[1:2, :], axis=1, keepdims=True),
    )


def first_kernel(vf_ref, xhi, yhi, corner, dall_ref, table_ref, r_ref, free_ref, image_ref, tile_ref, store, acc):
    role, gx, gy, row = place_of()
    has_x, has_y = gx < GXN - 1, row < YN - 1
    has_both = jnp.logical_and(has_x, has_y)
    empty = jnp.zeros((8, LANES), F32)
    for kind, ref in ((0, r_ref), (1, free_ref)):
        ref[8] = jnp.zeros((5, 2, 2, 8, LANES), F32)
        for e in range(8):
            ref[e, 0:4] = vf_ref[kind, e]
            for px in range(2):
                ref[e, 4, px, 0] = jnp.where(has_y, yhi[kind, e, px], 0.0)
                ref[e, 4, px, 1] = empty
        for f in range(4):
            for py in range(2):
                ref[8, f, 0, py] = jnp.where(has_x, xhi[kind, f, py], 0.0)
        ref[8, 4, 0, 0] = jnp.where(has_both, corner[kind], 0.0)
    build_store(r_ref, store)
    delta = apply_operator(store, acc, matrix_pieces(table_ref), dall_ref, image_ref)
    tile_ref[...] = sums_tile(square_sum(r_ref), delta)


def field_struct():
    return jax.ShapeDtypeStruct((9, 5, 2, 2, 8, LANES), F32)


def tile_struct():
    return jax.ShapeDtypeStruct((8, LANES), F32)


STORES = [pltpu.VMEM((9, 5, 7, 8, LANES), F32), pltpu.VMEM((9, 5, 7, 8, LANES), F32)]


def first_step(vf, xhi, yhi, corner, dall, table):
    return pl.pallas_call(
        first_kernel,
        out_shape=(field_struct(), field_struct(), field_struct(), tile_struct()),
        in_specs=[VMEM] * 6,
        out_specs=(VMEM,) * 4,
        scratch_shapes=STORES,
        compiler_params=params(),
        name="first_step",
    )(vf, xhi, yhi, corner, dall, table)


def add_faces(image_ref, work, free_ref, xlo, xhi, ylo, yhi, corners):
    role, gx, gy, row = place_of()
    low_x, low_y = gx > 0, row > 0
    work[...] = image_ref[...]
    for f in range(5):
        for p in range(2):
            work[0, f, 0, p] += jnp.where(low_x, xlo[f, p], 0.0)
            work[8, f, 0, p] += xhi[f, p]
    for e in range(9):
        for p in range(2):
            work[e, 0, p, 0] += jnp.where(low_y, ylo[e, p], 0.0)
            work[e, 4, p, 0] += yhi[e, p]
    work[0, 0, 0, 0] += jnp.where(jnp.logical_and(low_x, low_y), corners[0], 0.0)
    work[0, 4, 0, 0] += jnp.where(low_x, corners[1], 0.0)
    work[8, 0, 0, 0] += jnp.where(low_y, corners[2], 0.0)
    work[8, 4, 0, 0] += corners[3]
    work[...] = work[...] * free_ref[...]


def second_kernel(
    r_in, free_ref, image_in, xlo, xhi, ylo, yhi, corners, sum_ref, dall_ref, table_ref,
    s_ref, r_ref, image_ref, tile_ref, store, acc,
):
    add_faces(image_in, s_ref, free_ref, xlo, xhi, ylo, yhi, corners)
    gamma, delta = read_sums(sum_ref)
    alpha = gamma / delta
    r_ref[...] = r_in[...] - alpha.reshape(1, 1, 1, 1, 1, 1) * s_ref[...]
    build_store(r_ref, store)
    out = apply_operator(store, acc, matrix_pieces(table_ref), dall_ref, image_ref)
    tile_ref[...] = sums_tile(square_sum(r_ref), out)


def second_step(r, free, image, faces, total, dall, table):
    return pl.pallas_call(
        second_kernel,
        out_shape=(field_struct(), field_struct(), field_struct(), tile_struct()),
        in_specs=[VMEM] * 11,
        out_specs=(VMEM,) * 4,
        scratch_shapes=STORES,
        compiler_params=params(),
        name="second_step",
    )(r, free, image, *faces, total, dall, table)


def third_kernel(
    r0, r1, s0, free_ref, image_in, xlo, xhi, ylo, yhi, corners, sum0, sum1, dall_ref, table_ref,
    p_ref, u_ref, r_ref, tile_ref, work, store,
):
    add_faces(image_in, work, free_ref, xlo, xhi, ylo, yhi, corners)
    gamma0, delta0 = read_sums(sum0)
    gamma1, delta1 = read_sums(sum1)
    alpha0 = gamma0 / delta0
    beta1 = gamma1 / gamma0
    alpha1 = gamma1 / (delta1 - beta1 * gamma1 / alpha0)
    alpha0, alpha1, beta1 = (v.reshape(1, 1, 1, 1, 1, 1) for v in (alpha0, alpha1, beta1))
    p_ref[...] = r1[...] + beta1 * r0[...]
    u_ref[...] = alpha0 * r0[...] + alpha1 * p_ref[...]
    r_ref[...] = r1[...] - alpha1 * (work[...] + beta1 * s0[...])
    build_store(r_ref, store)
    delta = element_energy(store, matrix_pieces(table_ref), dall_ref)
    tile_ref[...] = sums_tile(square_sum(r_ref), delta)


def third_step(r0, r1, s0, free, image, faces, total0, total1, dall, table):
    return pl.pallas_call(
        third_kernel,
        out_shape=(field_struct(), field_struct(), field_struct(), tile_struct()),
        in_specs=[VMEM] * 14,
        out_specs=(VMEM,) * 4,
        scratch_shapes=[pltpu.VMEM((9, 5, 2, 2, 8, LANES), F32), STORES[0]],
        compiler_params=params(),
        name="third_step",
    )(r0, r1, s0, free, image, *faces, total0, total1, dall, table)


def last_kernel(p1, u1, r2, sum0, sum1, sum2, dall_ref, table_ref, grad_ref, nodes_ref, work, store):
    gamma0, delta0 = read_sums(sum0)
    gamma1, delta1 = read_sums(sum1)
    gamma2, delta2 = read_sums(sum2)
    alpha0 = gamma0 / delta0
    beta1 = gamma1 / gamma0
    alpha1 = gamma1 / (delta1 - beta1 * gamma1 / alpha0)
    beta2 = gamma2 / gamma1
    alpha2 = gamma2 / (delta2 - beta2 * gamma2 / alpha1)
    alpha2, beta2 = (v.reshape(1, 1, 1, 1, 1, 1) for v in (alpha2, beta2))
    work[...] = u1[...] + alpha2 * (r2[...] + beta2 * p1[...])
    build_store(work, store)
    pieces = matrix_pieces(table_ref)
    rows = lax.broadcasted_iota(jnp.int32, (8, LANES), 0)

    def body(e, _):
        columns, products = element_product(store, pieces, e)
        rho = density_rows(dall_ref, e)
        energy = jnp.zeros((8, LANES), F32)
        for f in range(4):
            one = jnp.sum(chunk_sum(columns[f], products[f]), axis=0, keepdims=True)
            energy = jnp.where(rows == f, one, energy)
        grad_ref[e] = -3.0 * rho * rho * (1.0 - floor_stiff) * energy / 32.0
        return 0

    lax.fori_loop(0, 8, body, 0)
    role = lax.axis_index("role")
    matrix = parity_matrix(role, True)

    def unpack(e, _):
        for px in range(2):
            held = jnp.concatenate(
                [work[e, f, px, py] for f in range(4) for py in range(2)], axis=0
            )
            even = lax.dot_general(
                held, matrix[:, :LANES], (((1,), (1,)), ((), ())),
                precision=lax.Precision.HIGHEST, preferred_element_type=F32,
            )
            odd = lax.dot_general(
                held, matrix[:, LANES:], (((1,), (1,)), ((), ())),
                precision=lax.Precision.HIGHEST, preferred_element_type=F32,
            )
            for y in range(8):
                nodes_ref[2 * e + px, y] = (
                    even[8 * y : 8 * y + 8] + pltpu.roll(odd[8 * y : 8 * y + 8], 4, 0)
                )
        return 0

    lax.fori_loop(0, 8, unpack, 0)


def last_step(p1, u1, r2, total0, total1, total2, dall, table):
    return pl.pallas_call(
        last_kernel,
        out_shape=(
            jax.ShapeDtypeStruct((8, 8, LANES), F32),
            jax.ShapeDtypeStruct((16, 8, 8, 256), F32),
        ),
        in_specs=[VMEM] * 8,
        out_specs=(VMEM,) * 2,
        scratch_shapes=[pltpu.VMEM((9, 5, 2, 2, 8, LANES), F32), STORES[0]],
        compiler_params=params(),
        name="last_step",
    )(p1, u1, r2, total0, total1, total2, dall, table)


def role_swap(values):
    return lax.ppermute(values, "role", [(0, 1), (1, 0)])


def nodal_rows(own, other):
    both = jnp.concatenate([own, other], axis=3)
    both = jnp.pad(jnp.transpose(both, (1, 2, 0, 3)), ((0, 0), (0, 0), (0, 1), (0, 0)))
    return jnp.concatenate([both, both], axis=2)


def halves(block, role):
    first, second = block[:, :, :8], block[:, :, 8:]
    keep = jnp.where(role == 0, first, second)
    give = jnp.where(role == 0, second, first)
    return keep, give


def on_device(design, force, clamped_dof_mask, stiffness):
    role = lax.axis_index("role")
    free = (1 - clamped_dof_mask).astype(F32)
    force_keep, force_give = halves(force, role)
    free_keep, free_give = halves(free, role)
    force_other, free_other = role_swap(force_give), role_swap(free_give)

    filter_weight_grid = slab_weight(design.shape)
    filtered = slab_smooth(design) / filter_weight_grid
    density_slab = element_mean(heaviside_projection(filtered)).reshape(16, 4, 64)
    empty = jnp.zeros_like(density_slab)
    density_slab = jnp.where(
        role == 0,
        jnp.concatenate([density_slab, empty], axis=2),
        jnp.concatenate([empty, density_slab], axis=2),
    )
    density_slab = jnp.pad(density_slab, ((0, 0), (0, 4), (0, 0)))

    chosen = jnp.asarray(row_table())
    table = jnp.dot(
        jnp.dot(chosen, stiffness, precision=lax.Precision.HIGHEST), chosen.T, precision=lax.Precision.HIGHEST
    )
    nodal = pl.pallas_call(
        pack_kernel,
        out_shape=jax.ShapeDtypeStruct((2, 8, 4, 2, 2, 8, LANES), F32),
        in_specs=[VMEM] * 2,
        out_specs=VMEM,
        compiler_params=params(),
        name="pack",
    )(nodal_rows(force_keep, force_other), nodal_rows(free_keep, free_other))
    xhi, yhi, corner, dall = start_exchange(nodal, density_slab)
    r0, free, image, tile = first_step(nodal, xhi, yhi, corner, dall, table)
    *faces, total0 = face_exchange(image, tile, 2)
    s0, r1, image, tile = second_step(r0, free, image, faces, total0, dall, table)
    *faces, total1 = face_exchange(image, tile, 3)
    p1, u1, r2, tile = third_step(r0, r1, s0, free, image, faces, total0, total1, dall, table)
    total2 = reduce_all(tile, 4)
    grad, nodes = last_step(p1, u1, r2, total0, total1, total2, dall, table)
    nodes = jnp.transpose(nodes[:, :, :3], (2, 0, 1, 3))
    mine, theirs = nodes[..., :LANES], role_swap(nodes[..., LANES:])
    displacement = jnp.where(
        role == 0,
        jnp.concatenate([mine, theirs], axis=2),
        jnp.concatenate([theirs, mine], axis=2),
    )
    slab_grad = gradient_exchange(grad)[:, :4]
    slab_grad = jnp.where(role == 0, slab_grad[..., :64], slab_grad[..., 64:]).reshape(1, 64, 64)
    voxel_grad = spread(slab_grad) * slope(filtered)
    sensitivity = slab_smooth(voxel_grad / filter_weight_grid)
    return (sensitivity, displacement)


def solution(mesh):
    return jax.shard_map(
        on_device,
        mesh=mesh,
        in_specs=(P(GX_GY, None, "role"), P(None, "gx", "gy", "role"), P(None, "gx", "gy", "role"), P()),
        out_specs=(P(GX_GY, None, "role"), P(None, "gx", "gy", "role")),
        check_vma=False,
    )
```

```python
import functools
import math

import jax
import jax.numpy as jnp
import numpy as np
from jax import lax
from jax.experimental import pallas as pl
from jax.experimental.pallas import tpu as pltpu
from jax.sharding import PartitionSpec as P

sharpness = 4.0
threshold = 0.5
floor_stiff = 0.001
BEND = math.tanh(sharpness * threshold)
FULL = math.tanh(sharpness * threshold) + math.tanh(sharpness * (1.0 - threshold))
HAT = (1.0, 2.0, 3.0, 2.0, 1.0)

MESH = pl.DeviceIdType.MESH
F32 = jnp.float32
BF16 = jnp.bfloat16
I32 = jnp.int32
ROWS = 112
LANES = 128
GXN = 8
YN = 16
CHUNKS = (
    (0, 0, 0), (0, 0, 1), (0, 0, 2), (0, 0, 3), (0, 0, 4), (0, 0, 5),
    (1, 0, 0), (1, 0, 1), (1, 0, 4),
    (0, 1, 0), (0, 1, 2), (0, 1, 6),
    (1, 1, 0), (1, 1, 4),
)
PAIRS = {4: ((0, 0), (0, 1)), 5: ((1, 0), (1, 1)), 6: ((0, 0), (1, 0))}


def row_table():
    table = np.zeros((ROWS, 81), np.float32)
    seen = set()
    for place, (dx, dy, kind) in enumerate(CHUNKS):
        for half in range(2):
            if kind < 4:
                px, py, c = kind // 2, kind % 2, half
            else:
                (px, py), c = PAIRS[kind][half], 2
            if (dx and px) or (dy and py):
                continue
            a, b = px + 2 * dx, py + 2 * dy
            for q in range(3):
                index = ((c * 3 + b) * 3 + a) * 3 + q
                assert index not in seen
                seen.add(index)
                table[place * 8 + half * 4 + q, index] = 1.0
    assert len(seen) == 81
    return table


def place_of():
    role, gx, gy = lax.axis_index("role"), lax.axis_index("gx"), lax.axis_index("gy")
    return role, gx, gy, 2 * gy + role


def device_at(gx, row):
    gx = lax.rem(gx + GXN, GXN)
    row = lax.rem(row + YN, YN)
    return {"role": lax.rem(row, 2), "gx": gx, "gy": lax.div(row, 2)}


def remote(src, dst, send, recv, device):
    return pltpu.make_async_remote_copy(
        src_ref=src, dst_ref=dst, send_sem=send, recv_sem=recv, device_id=device, device_id_type=MESH
    )


def iota(shape, dim):
    return lax.broadcasted_iota(I32, shape, dim)


def pieces_of(values, count):
    parts = []
    for _ in range(count):
        part = values.astype(BF16)
        parts.append(part)
        values = values - part.astype(F32)
    return parts


def slab_of(shift):
    role, gx, gy, row = place_of()
    slab = lax.rem(gx * 8 + gy + shift + 64, 64)
    return lax.div(slab, 8), lax.rem(slab, 8)


def slab_device(shift, other):
    role = lax.axis_index("role")
    gx, gy = slab_of(shift)
    return {"role": (1 - role) if other else role, "gx": gx, "gy": gy}


def partner():
    return slab_device(0, True)


def reach(places, extent):
    total = jnp.zeros(places.shape, F32)
    for k, weight in enumerate(HAT):
        target = places + (k - 2)
        total = total + jnp.where(jnp.logical_and(target >= 0, target < extent), weight, 0.0)
    return jnp.maximum(total, 1.0)


def column_z(role, shape, dim):
    lane = iota(shape, dim)
    beyond = lane - LANES + jnp.where(role == 0, LANES, -2)
    return jnp.where(lane < LANES, lane, jnp.where(lane < LANES + 2, beyond, -4096))


def hat_of(distance):
    return jnp.maximum(3 - jnp.abs(distance), 0).astype(F32)


def at(field, e, f, kind):
    return field[e, kind // 2, 16 * f + 8 * (kind % 2) : 16 * f + 8 * (kind % 2) + 8]


def parity_matrix(role):
    rows, cols = iota((256, 256), 0), iota((256, 256), 1)
    half = jnp.where(rows < LANES, role, 1 - role)
    spot = half * LANES + lax.rem(rows, LANES)
    return (spot == 2 * lax.rem(cols, LANES) + lax.div(cols, LANES)).astype(F32).astype(BF16)


def parity_back(role):
    rows, cols = iota((256, 256), 0), iota((256, 256), 1)
    half = jnp.where(cols < LANES, role, 1 - role)
    spot = half * LANES + lax.rem(cols, LANES)
    return (spot == 2 * lax.rem(rows, LANES) + lax.div(rows, LANES)).astype(F32).astype(BF16)


def mul(left, right):
    return jnp.dot(left, right, preferred_element_type=F32)


def edge_stage(r):
    role = lax.axis_index("role")
    rows, cols = iota((16, LANES), 0), iota((16, LANES), 1)
    chosen = jnp.where(role == 0, 124 + rows, rows)
    chosen = jnp.logical_and(cols == chosen, rows < 4).astype(F32).astype(BF16)
    for x in range(4):
        total = None
        for part in pieces_of(r.design[x], 2):
            one = lax.dot_general(chosen, part, (((1,), (1,)), ((), ())), preferred_element_type=F32)
            total = one if total is None else total + one
        r.edge[:, 256 * x : 256 * x + 256] = total[:8]


def design_copies(r):
    return [
        remote(r.design, r.lo, r.dsend.at[0], r.drecv.at[0], slab_device(1, False)),
        remote(r.design, r.hi, r.dsend.at[1], r.drecv.at[1], slab_device(-1, False)),
        remote(r.edge, r.edges.at[1], r.dsend.at[2], r.drecv.at[2], slab_device(0, True)),
        remote(r.edge, r.edges.at[0], r.dsend.at[3], r.drecv.at[3], slab_device(1, True)),
        remote(r.edge, r.edges.at[2], r.dsend.at[4], r.drecv.at[4], slab_device(-1, True)),
    ]


def nodal_copies(r):
    role = lax.axis_index("role")
    spot = pl.ds(pl.multiple_of(8 * (1 - role), 8), 8)
    return [
        remote(r.force.at[:, :, spot], r.force_other, r.dsend.at[5], r.drecv.at[5], partner()),
        remote(r.mask.at[:, :, spot], r.mask_other, r.dsend.at[6], r.drecv.at[6], partner()),
    ]


def swap_stage(r):
    copies = design_copies(r)
    for copy in copies + nodal_copies(r):
        copy.start()
    for copy in copies:
        copy.wait()


def filter_stage(r):
    role, gx, gy, row = place_of()
    slab = gx * 8 + gy
    has_lo, has_hi = slab > 0, slab < 63

    @pl.when(jnp.logical_not(has_lo))
    def _():
        r.lo[...] = jnp.zeros_like(r.lo)
        r.edges[0] = jnp.zeros((8, 1024), F32)

    @pl.when(jnp.logical_not(has_hi))
    def _():
        r.hi[...] = jnp.zeros_like(r.hi)
        r.edges[2] = jnp.zeros((8, 1024), F32)

    band = hat_of(column_z(role, (LANES, 256), 1) - iota((LANES, 256), 0)).astype(BF16)
    bands = jnp.concatenate([band, band], axis=0)
    step = iota((16, 256), 0)
    far = lax.rem(step, 8)
    spot = jnp.where(role == 0, LANES + far, far - 4)
    rim = hat_of(column_z(role, (16, 256), 1) - spot)
    rim = jnp.where(far < 4, rim, 0.0).astype(BF16)

    def plane(p, rows):
        ref = (r.lo, r.design, r.hi)[p // 4]
        return ref[p % 4, rows]

    def mix(get):
        return 3.0 * get(2) + 2.0 * (get(1) + get(3)) + (get(0) + get(4))

    for i in range(8):
        beyond = mix(lambda k: r.edges[(i + k) // 4, :, 256 * ((i + k) % 4) : 256 * ((i + k) % 4) + 256])
        beyond = jnp.concatenate(pieces_of(beyond, 2), axis=0)
        beyond = lax.dot_general(beyond, rim, (((0,), (0,)), ((), ())), preferred_element_type=F32)
        for b in range(4):
            rows = slice(64 * b, 64 * b + 64)
            wide = mix(lambda k: plane(i + k, rows))
            out = mul(jnp.concatenate(pieces_of(wide, 2), axis=1), bands)
            r.zc[i, 8 + 64 * b : 72 + 64 * b] = out + beyond[rows]
        r.zc[i, 0:8] = jnp.zeros((8, 256), F32)
        r.zc[i, 264:272] = jnp.zeros((8, 256), F32)

    z_places = column_z(role, (1, 256), 1) + role * LANES
    by_z = 1.0 / reach(z_places, 256)
    r.psum[...] = jnp.zeros_like(r.psum)

    def body(i, _):
        x = 4 * slab + i - 2
        inside = jnp.logical_and(x >= 0, x < 256)
        own = jnp.logical_and(i >= 2, i < 6)
        by_x = 1.0 / reach(jnp.full((1, 256), x, I32), 256)
        by_xz = by_z * by_x
        for b in range(8):
            first = 32 * b
            by = by_xz / reach(iota((32, 256), 0) + first, 256)
            total = (
                3.0 * r.zc[i, 8 + first : 40 + first]
                + 2.0 * (r.zc[i, 7 + first : 39 + first] + r.zc[i, 9 + first : 41 + first])
                + (r.zc[i, 6 + first : 38 + first] + r.zc[i, 10 + first : 42 + first])
            )
            bent = jnp.tanh(sharpness * (total * by - threshold))
            r.m[i, first : first + 32] = jnp.where(inside, (1.0 - bent * bent) * (by * (sharpness / FULL)), 0.0)
            shown = (BEND + bent[:, :LANES]) * (1.0 / FULL)
            r.psum[first : first + 32] += jnp.where(own, shown, 0.0)
        return 0

    lax.fori_loop(0, 8, body, 0)
    rows, cols = iota((LANES, 256), 0), iota((LANES, 256), 1)
    gather = jnp.logical_and(
        lax.div(cols, 16) == lax.div(rows, 8), lax.div(lax.rem(cols, 16), 4) == lax.rem(rows, 8)
    ).astype(F32).astype(BF16)
    parts = pieces_of(r.psum[...], 3)
    by_rows = mul(gather, parts[0]) + mul(gather, parts[1]) + mul(gather, parts[2])
    rows, cols = iota((LANES, LANES), 0), iota((LANES, LANES), 1)
    merge = (cols == 64 * role + lax.div(rows, 2)).astype(F32).astype(BF16)
    parts = pieces_of(by_rows, 3)
    density = (mul(parts[0], merge) + mul(parts[1], merge) + mul(parts[2], merge)) * (1.0 / 32.0)
    for k in range(YN):
        r.dens[k] = density[8 * k : 8 * k + 8]


def pack_stage(r):
    for copy in nodal_copies(r):
        copy.wait()
    role = lax.axis_index("role")
    matrix = parity_matrix(role)
    spot = pl.ds(pl.multiple_of(8 * role, 8), 8)
    r.vf[...] = jnp.zeros_like(r.vf)
    for q in range(3):
        own = r.force[q, :, spot].reshape(LANES, LANES)
        wide = jnp.concatenate([own, r.force_other[q].reshape(LANES, LANES)], axis=1)
        force = None
        for part in pieces_of(wide, 3):
            one = mul(part, matrix)
            force = one if force is None else force + one
        own = r.mask[q, :, spot].reshape(LANES, LANES)
        wide = jnp.concatenate([own, r.mask_other[q].reshape(LANES, LANES)], axis=1)
        free = mul((1 - wide).astype(F32).astype(BF16), matrix)
        force = force * free
        for x in range(16):
            for half in range(2):
                for kind, values in ((0, force), (1, free)):
                    r.vf[kind, x // 2, x % 2, pl.ds(4 * half + q, 8, stride=8)] = values[
                        8 * x : 8 * x + 8, LANES * half : LANES * half + LANES
                    ]


def spread_stage(r):
    role, gx, gy, row = place_of()
    copies = []
    for k in range(1, YN):
        target = lax.rem(row + k, YN)
        copies.append(
            remote(r.dens.at[target], r.dall.at[row], r.nsend.at[k], r.nrecv.at[k], device_at(gx, row + k))
        )
    copies.append(remote(r.vf.at[:, 0, 0], r.nxhi, r.nsend.at[16], r.nrecv.at[16], device_at(gx - 1, row)))
    copies.append(
        remote(r.vf.at[:, :, :, 0:8], r.nyhi, r.nsend.at[17], r.nrecv.at[17], device_at(gx, row - 1))
    )
    copies.append(
        remote(r.vf.at[:, 0, 0, 0:8], r.ncorner, r.nsend.at[18], r.nrecv.at[18], device_at(gx - 1, row - 1))
    )
    for copy in copies:
        copy.start()
    r.dall[row] = r.dens[row]
    for copy in copies:
        copy.wait()


def frame_stage(r):
    role, gx, gy, row = place_of()
    has_x, has_y = gx < GXN - 1, row < YN - 1
    has_both = jnp.logical_and(has_x, has_y)
    for kind, ref in ((0, r.r0), (1, r.free)):
        for e in range(8):
            for px in range(2):
                ref[e, px, 0:64] = r.vf[kind, e, px]
                ref[e, px, 64:72] = jnp.where(has_y, r.nyhi[kind, e, px], 0.0)
                ref[e, px, 72:80] = jnp.zeros((8, LANES), F32)
        ref[8, 0, 0:64] = jnp.where(has_x, r.nxhi[kind], 0.0)
        ref[8, 0, 64:72] = jnp.where(has_both, r.ncorner[kind], 0.0)
        ref[8, 0, 72:80] = jnp.zeros((8, LANES), F32)
        ref[8, 1] = jnp.zeros((80, LANES), F32)
    for e in range(8):
        r.rho[e] = r.dall[2 * e] + r.dall[2 * e + 1]
    whole = r.table[...]
    high, low = pieces_of(whole, 2)
    r.stiff[...] = jnp.concatenate(
        [
            jnp.concatenate([high, high], axis=1),
            jnp.concatenate([low, jnp.zeros_like(low)], axis=1),
        ],
        axis=0,
    )


def build_store(field, store):
    sub = iota((8, LANES), 0) < 4
    inside = iota((8, LANES), 1) < LANES - 1

    def body(e, _):
        for f in range(5):
            held = [at(field, e, f, k) for k in range(4)]
            shifted = [jnp.where(inside, pltpu.roll(v, LANES - 1, 1), 0.0) for v in held]
            turned = [None] + [pltpu.roll(v, 4, 0) for v in shifted[1:]]
            for k in range(4):
                store[e, f, k] = held[k]
            store[e, f, 4] = jnp.where(sub, shifted[0], turned[1])
            store[e, f, 5] = jnp.where(sub, shifted[2], turned[3])
            store[e, f, 6] = jnp.where(sub, shifted[0], turned[2])
        return 0

    lax.fori_loop(0, 9, body, 0)


def element_product(store, stiff, e):
    columns = []
    for f in range(4):
        columns.append(jnp.concatenate([store[e + dx, f + dy, kind] for dx, dy, kind in CHUNKS], axis=0))
    wide = jnp.concatenate(columns, axis=1)
    out = mul(stiff, jnp.concatenate(pieces_of(wide, 2), axis=0))
    product = out[:ROWS] + out[ROWS:]
    return columns, [product[:, f * LANES : (f + 1) * LANES] for f in range(4)]


def chunk_sum(left, right):
    both = left * right
    total = both[:8]
    for k in range(1, len(CHUNKS)):
        total = total + both[8 * k : 8 * k + 8]
    return total


def factor_of(rho):
    return floor_stiff + (1.0 - floor_stiff) * (rho * rho * rho)


def apply_operator(r, image):
    store, acc = r.store, r.acc
    acc[...] = jnp.zeros_like(acc)
    stiff = r.stiff[...]

    def body(e, energy):
        columns, products = element_product(store, stiff, e)
        factor = factor_of(r.rho[e])
        for f in range(4):
            scaled = products[f] * factor[f : f + 1, :]
            energy = energy + chunk_sum(columns[f], scaled)
            for place, (dx, dy, kind) in enumerate(CHUNKS):
                acc[e + dx, f + dy, kind] += scaled[8 * place : 8 * place + 8]
        return energy

    energy = lax.fori_loop(0, 8, body, jnp.zeros((8, LANES), F32))
    keep = jnp.logical_and(iota((8, LANES), 0) < 4, iota((8, LANES), 1) > 0)

    def fold(e, _):
        for f in range(5):
            z0, z1, z2 = acc[e, f, 4], acc[e, f, 5], acc[e, f, 6]
            t0, t1, t2 = (pltpu.roll(v, 4, 0) for v in (z0, z1, z2))
            for k, extra in enumerate((z0 + z2, t0, z1 + t2, t1)):
                extra = jnp.where(keep, pltpu.roll(extra, 1, 1), 0.0)
                first = 16 * f + 8 * (k % 2)
                image[e, k // 2, first : first + 8] = acc[e, f, k] + extra
        return 0

    lax.fori_loop(0, 9, fold, 0)
    return energy


def element_energy(r):
    stiff = r.stiff[...]

    def body(e, energy):
        columns, products = element_product(r.store, stiff, e)
        factor = factor_of(r.rho[e])
        for f in range(4):
            energy = energy + chunk_sum(columns[f], products[f] * factor[f : f + 1, :])
        return energy

    return lax.fori_loop(0, 8, body, jnp.zeros((8, LANES), F32))


def square_sum(field):
    def body(e, total):
        for f in range(4):
            for k in range(4):
                held = at(field, e, f, k)
                total = total + held * held
        return total

    return lax.fori_loop(0, 8, body, jnp.zeros((8, LANES), F32))


def sums_tile(gamma, delta):
    rows = iota((8, LANES), 0)
    gamma = jnp.sum(gamma, axis=0, keepdims=True)
    delta = jnp.sum(delta, axis=0, keepdims=True)
    return jnp.where(rows == 0, gamma, jnp.where(rows == 1, delta, 0.0))


def read_sums(sum_ref):
    return (
        jnp.sum(sum_ref[0:1, :], axis=1, keepdims=True),
        jnp.sum(sum_ref[1:2, :], axis=1, keepdims=True),
    )


def over_nodes(body):
    def step(e, _):
        body(e)
        return 0

    lax.fori_loop(0, 9, step, 0)


def reduce_parts(r, n):
    role, gx, gy, row = place_of()
    tile, slots, second, half = r["tile", n], r["slots", n], r["second", n], r["half", n]
    send, recv = r["rsend", n], r["rrecv", n]
    slots[row] = tile[...]
    copies = []
    for k in range(1, YN):
        copies.append(remote(tile, slots.at[row], send.at[k], recv.at[k], device_at(gx, row + k)))
    for copy in copies:
        copy.start()
    for copy in copies:
        copy.wait()
    part = slots[0]
    for k in range(1, YN):
        part = part + slots[k]
    half[...] = part
    second[gx] = part
    copies = []
    for k in range(1, GXN):
        copies.append(remote(half, second.at[gx], send.at[YN + k], recv.at[YN + k], device_at(gx + k, row)))
    for copy in copies:
        copy.start()
    for copy in copies:
        copy.wait()
    part = second[0]
    for k in range(1, GXN):
        part = part + second[k]
    r["sum", n][...] = part


FACE_MOVES = ((1, 0), (-1, 0), (0, 1), (0, -1), (1, 1), (1, -1), (-1, 1), (-1, -1))


def face_stage(r, n):
    role, gx, gy, row = place_of()
    image, corners = r["image", n], r["corners", n]
    ends = (
        (image.at[8, 0], r["xlo", n]),
        (image.at[0, 0], r["xhi", n]),
        (image.at[:, :, 64:72], r["ylo", n]),
        (image.at[:, :, 0:8], r["yhi", n]),
        (image.at[8, 0, 64:72], corners.at[0]),
        (image.at[8, 0, 0:8], corners.at[1]),
        (image.at[0, 0, 64:72], corners.at[2]),
        (image.at[0, 0, 0:8], corners.at[3]),
    )
    send, recv = r["fsend", n], r["frecv", n]
    copies = []
    for k, ((dx, dy), (src, dst)) in enumerate(zip(FACE_MOVES, ends)):
        copies.append(remote(src, dst, send.at[k], recv.at[k], device_at(gx + dx, row + dy)))
    for copy in copies:
        copy.start()
    reduce_parts(r, n)
    for copy in copies:
        copy.wait()


def add_faces(r, n, work):
    role, gx, gy, row = place_of()
    low_x, low_y = gx > 0, row > 0
    image, corners = r["image", n], r["corners", n]
    xlo, xhi, ylo, yhi = (r[name, n] for name in ("xlo", "xhi", "ylo", "yhi"))
    work[...] = image[...]
    work[0, 0] += jnp.where(low_x, xlo[...], 0.0)
    work[8, 0] += xhi[...]
    for e in range(9):
        for p in range(2):
            work[e, p, 0:8] += jnp.where(low_y, ylo[e, p], 0.0)
            work[e, p, 64:72] += yhi[e, p]
    work[0, 0, 0:8] += jnp.where(jnp.logical_and(low_x, low_y), corners[0], 0.0)
    work[0, 0, 64:72] += jnp.where(low_x, corners[1], 0.0)
    work[8, 0, 0:8] += jnp.where(low_y, corners[2], 0.0)
    work[8, 0, 64:72] += corners[3]
    work[...] = work[...] * r.free[...]


def spare(value):
    return value.reshape(1, 1, 1)


def first_stage(r):
    build_store(r.r0, r.store)
    delta = apply_operator(r, r["image", 0])
    r["tile", 0][...] = sums_tile(square_sum(r.r0), delta)


def second_stage(r):
    add_faces(r, 0, r.s0)
    gamma, delta = read_sums(r["sum", 0])
    alpha = spare(gamma / delta)

    def update(e):
        r.r1[e] = r.r0[e] - alpha * r.s0[e]

    over_nodes(update)
    build_store(r.r1, r.store)
    delta = apply_operator(r, r["image", 1])
    r["tile", 1][...] = sums_tile(square_sum(r.r1), delta)


def third_stage(r):
    add_faces(r, 1, r.work)
    gamma0, delta0 = read_sums(r["sum", 0])
    gamma1, delta1 = read_sums(r["sum", 1])
    alpha0 = gamma0 / delta0
    beta1 = gamma1 / gamma0
    alpha1 = gamma1 / (delta1 - beta1 * gamma1 / alpha0)
    alpha0, alpha1, beta1 = spare(alpha0), spare(alpha1), spare(beta1)

    def update(e):
        p = r.r1[e] + beta1 * r.r0[e]
        r.p1[e] = p
        r.u1[e] = alpha0 * r.r0[e] + alpha1 * p
        r.r2[e] = r.r1[e] - alpha1 * (r.work[e] + beta1 * r.s0[e])

    over_nodes(update)
    build_store(r.r2, r.store)
    delta = element_energy(r)
    r["tile", 2][...] = sums_tile(square_sum(r.r2), delta)


def reduce_stage(r):
    reduce_parts(r, 2)


def last_stage(r):
    gamma0, delta0 = read_sums(r["sum", 0])
    gamma1, delta1 = read_sums(r["sum", 1])
    gamma2, delta2 = read_sums(r["sum", 2])
    alpha0 = gamma0 / delta0
    beta1 = gamma1 / gamma0
    alpha1 = gamma1 / (delta1 - beta1 * gamma1 / alpha0)
    beta2 = gamma2 / gamma1
    alpha2 = spare(gamma2 / (delta2 - beta2 * gamma2 / alpha1))
    beta2 = spare(beta2)

    def update(e):
        r.u[e] = r.u1[e] + alpha2 * (r.r2[e] + beta2 * r.p1[e])

    over_nodes(update)
    build_store(r.u, r.store)
    stiff = r.stiff[...]
    rows = iota((8, LANES), 0)
    r.grad[0] = jnp.zeros((8, LANES), F32)
    r.grad[9] = jnp.zeros((8, LANES), F32)

    def body(e, _):
        columns, products = element_product(r.store, stiff, e)
        rho = r.rho[e]
        energy = jnp.zeros((8, LANES), F32)
        for f in range(4):
            one = jnp.sum(chunk_sum(columns[f], products[f]), axis=0, keepdims=True)
            energy = jnp.where(rows == f, one, energy)
        r.grad[e + 1] = (-3.0 * (1.0 - floor_stiff) / 32.0) * (rho * rho) * energy
        return 0

    lax.fori_loop(0, 8, body, 0)


def edge_targets():
    role, gx, gy, row = place_of()
    up, down = lax.rem(gx + 1, GXN), lax.rem(gx + GXN - 1, GXN)
    return [
        {"role": 0, "gx": up, "gy": 0},
        {"role": 1, "gx": up, "gy": 0},
        {"role": 0, "gx": down, "gy": 7},
        {"role": 1, "gx": down, "gy": 7},
    ]


def gradient_copies(r):
    role, gx, gy, row = place_of()
    copies = []
    for k in range(1, YN):
        target = lax.div(lax.rem(row + k, YN), 2)
        copies.append(
            remote(r.grad.at[pl.ds(target, 3)], r.gall.at[row], r.gsend.at[k], r.grecv.at[k], device_at(gx, row + k))
        )
    return copies


def rim_copies(r):
    role, gx, gy, row = place_of()
    copies = []
    for k, device in enumerate(edge_targets()):
        layer = 8 if k < 2 else 1
        copies.append(remote(r.grad.at[layer], r.grim.at[row], r.esend.at[k], r.erecv.at[row], device))
    return copies


def gradient_stage(r):
    role, gx, gy, row = place_of()
    copies, rims = gradient_copies(r), rim_copies(r)
    for copy in copies + rims:
        copy.start()
    r.gall[row] = r.grad[pl.ds(gy, 3)]
    for copy in copies:
        copy.wait()
    for copy in rims:
        copy.wait_send()

    @pl.when(jnp.logical_or(gy == 0, gy == 7))
    def _():
        for k in range(YN):
            remote(r.grad.at[1], r.grim.at[k], r.esend.at[0], r.erecv.at[k], partner()).wait_recv()


def unpack_stage(r):
    role = lax.axis_index("role")
    back = parity_back(role)
    spot = pl.ds(pl.multiple_of(8 * role, 8), 8)
    for q in range(3):
        even = [r.u[x // 2, x % 2, pl.ds(q, 8, stride=8)] for x in range(16)]
        odd = [r.u[x // 2, x % 2, pl.ds(4 + q, 8, stride=8)] for x in range(16)]
        wide = jnp.concatenate([jnp.concatenate(even, axis=0), jnp.concatenate(odd, axis=0)], axis=1)
        total = None
        for part in pieces_of(wide, 3):
            one = mul(part, back)
            total = one if total is None else total + one
        r.disp[q, :, spot] = total[:, :LANES].reshape(16, 8, LANES)
        r.give[q] = total[:, LANES:].reshape(16, 8, LANES)


def give_copy(r):
    role = lax.axis_index("role")
    spot = pl.ds(pl.multiple_of(8 * role, 8), 8)
    return remote(r.give, r.disp.at[:, :, spot], r.osend.at[0], r.orecv.at[0], partner())


def give_stage(r):
    give_copy(r).start()


def given_stage(r):
    give_copy(r).wait()


def final_stage(r):
    role, gx, gy, row = place_of()
    for k in range(YN):
        r.layers[0, 8 * k : 8 * k + 8] = r.gall[k, 0]
        r.layers[1, 8 * k : 8 * k + 8] = r.gall[k, 1]
        r.layers[2, 8 * k : 8 * k + 8] = r.gall[k, 2]

    @pl.when(gy == 0)
    def _():
        for k in range(YN):
            r.layers[0, 8 * k : 8 * k + 8] = r.grim[k]

    @pl.when(gy == 7)
    def _():
        for k in range(YN):
            r.layers[2, 8 * k : 8 * k + 8] = r.grim[k]

    rows = iota((LANES, 256), 0)
    z = column_z(role, (LANES, 256), 1) + role * LANES
    widen = jnp.logical_and(z >= 0, rows == lax.div(jnp.maximum(z, 0), 2)).astype(F32).astype(BF16)
    widen = jnp.concatenate([widen, widen], axis=0)
    rows, cols = iota((256, LANES), 0), iota((256, LANES), 1)
    repeat = (cols == 8 * lax.div(rows, 16) + lax.div(lax.rem(rows, 16), 4)).astype(F32).astype(BF16)
    repeat = jnp.concatenate([repeat, repeat], axis=1)
    for k in range(3):
        wide = mul(jnp.concatenate(pieces_of(r.layers[k], 2), axis=1), widen)
        r.wide[k] = mul(repeat, jnp.concatenate(pieces_of(wide, 2), axis=0))
    band = hat_of(iota((256, LANES), 1) - column_z(role, (256, LANES), 0)).astype(BF16)
    bands = jnp.concatenate([band, band], axis=0)
    for o in range(4):
        r.zc[o, 0:8] = jnp.zeros((8, 256), F32)
        r.zc[o, 264:272] = jnp.zeros((8, 256), F32)
        for b in range(8):
            spot = slice(32 * b, 32 * b + 32)
            total = None
            for layer, planes in ((0, (0, 1)), (1, (2, 3, 4, 5)), (2, (6, 7))):
                part = None
                for i in planes:
                    if o <= i <= o + 4:
                        one = HAT[i - o] * r.m[i, spot]
                        part = one if part is None else part + one
                if part is not None:
                    part = part * r.wide[layer, spot]
                    total = part if total is None else total + part
            r.zc[o, 8 + 32 * b : 40 + 32 * b] = total
        for b in range(8):
            first = 32 * b
            total = (
                3.0 * r.zc[o, 8 + first : 40 + first]
                + 2.0 * (r.zc[o, 7 + first : 39 + first] + r.zc[o, 9 + first : 41 + first])
                + (r.zc[o, 6 + first : 38 + first] + r.zc[o, 10 + first : 42 + first])
            )
            r.sens[o, first : first + 32] = mul(jnp.concatenate(pieces_of(total, 2), axis=1), bands)


FIELD = (9, 2, 80, LANES)
TILE = (8, LANES)


class Refs(dict):
    def __getattr__(self, name):
        return self[name]


def buffers():
    shapes = {
        "edge": (8, 1024), "lo": (4, 256, LANES), "hi": (4, 256, LANES), "edges": (3, 8, 1024),
        "force_other": (3, 16, 8, LANES), "m": (8, 256, 256), "zc": (8, 272, 256), "psum": (256, LANES),
        "dens": (YN, 8, LANES), "vf": (2, 8, 2, 64, LANES), "nxhi": (2, 64, LANES), "nyhi": (2, 8, 2, 8, LANES),
        "ncorner": (2, 8, LANES), "dall": (YN, 8, LANES), "rho": (8, 8, LANES), "store": (9, 5, 7, 8, LANES),
        "acc": (9, 5, 7, 8, LANES), "grad": (10, 8, LANES), "gall": (YN, 3, 8, LANES), "grim": (YN, 8, LANES),
        "give": (3, 16, 8, LANES), "layers": (3, LANES, LANES), "wide": (3, 256, 256),
    }
    for name in ("r0", "free", "s0", "r1", "p1", "u1", "r2", "u", "work"):
        shapes[name] = FIELD
    for n in range(3):
        shapes["tile", n] = shapes["sum", n] = shapes["half", n] = TILE
        shapes["slots", n] = (YN, 8, LANES)
        shapes["second", n] = (GXN, 8, LANES)
    for n in range(2):
        shapes["image", n] = FIELD
        shapes["xlo", n] = shapes["xhi", n] = (80, LANES)
        shapes["ylo", n] = shapes["yhi", n] = (9, 2, 8, LANES)
        shapes["corners", n] = (4, 8, LANES)
    scratch = {name: pltpu.VMEM(shape, F32) for name, shape in shapes.items()}
    scratch["mask_other"] = pltpu.VMEM((3, 16, 8, LANES), I32)
    scratch["stiff"] = pltpu.VMEM((2 * ROWS, 2 * ROWS), BF16)
    counts = {"dsend": 7, "drecv": 7, "nsend": 19, "nrecv": 19, "gsend": 16, "grecv": 16, "esend": 4, "erecv": 16,
              "osend": 1, "orecv": 1}
    for n in range(3):
        counts["rsend", n] = counts["rrecv", n] = 24
        counts["fsend", n] = counts["frecv", n] = 8
    for name, count in counts.items():
        scratch[name] = pltpu.SemaphoreType.DMA((count,))
    return scratch


def greet_all():
    role, gx, gy, row = place_of()
    barrier = pltpu.get_barrier_semaphore()
    devices = [device_at(gx, row + k) for k in range(1, YN)]
    devices += [device_at(gx + k, row) for k in range(1, GXN)]
    devices += [device_at(gx + dx, row + dy) for dx, dy in FACE_MOVES[4:]]
    devices += [slab_device(shift, other) for shift, other in ((1, 0), (-1, 0), (1, 1), (-1, 1))]
    for device in devices:
        pl.semaphore_signal(barrier, inc=1, device_id=device, device_id_type=MESH)

    @pl.when(gy == 0)
    def _():
        for k in range(YN):
            pl.semaphore_signal(barrier, inc=1, device_id=device_at(gx - 1, row * 0 + k), device_id_type=MESH)

    @pl.when(gy == 7)
    def _():
        for k in range(YN):
            pl.semaphore_signal(barrier, inc=1, device_id=device_at(gx + 1, row * 0 + k), device_id_type=MESH)

    return len(devices) + 4


def whole_kernel(names, *refs):
    r = Refs(zip(names, refs))
    count = greet_all()
    edge_stage(r)
    pl.semaphore_wait(pltpu.get_barrier_semaphore(), count)
    swap_stage(r)
    filter_stage(r)
    pack_stage(r)
    spread_stage(r)
    frame_stage(r)
    first_stage(r)
    face_stage(r, 0)
    second_stage(r)
    face_stage(r, 1)
    third_stage(r)
    reduce_stage(r)
    last_stage(r)
    gradient_stage(r)
    unpack_stage(r)
    give_stage(r)
    final_stage(r)
    given_stage(r)


def on_device(design, force, clamped_dof_mask, stiffness):
    chosen = jnp.asarray(row_table())
    table = jnp.dot(
        jnp.dot(chosen, stiffness, precision=lax.Precision.HIGHEST), chosen.T, precision=lax.Precision.HIGHEST
    )
    scratch = buffers()
    names = ["design", "force", "mask", "table", "sens", "disp"] + list(scratch)
    vmem = pl.BlockSpec(memory_space=pltpu.VMEM)
    return pl.pallas_call(
        functools.partial(whole_kernel, names),
        out_shape=(
            jax.ShapeDtypeStruct((4, 256, LANES), F32),
            jax.ShapeDtypeStruct((3, 16, 16, LANES), F32),
        ),
        in_specs=[vmem] * 4,
        out_specs=(vmem, vmem),
        scratch_shapes=list(scratch.values()),
        compiler_params=pltpu.CompilerParams(
            collective_id=0, has_side_effects=True, vmem_limit_bytes=56 * 1024 * 1024
        ),
        name="compliance",
    )(design, force, clamped_dof_mask, table)


def solution(mesh):
    fine = P(("gx", "gy"), None, "role")
    nodes = P(None, "gx", "gy", "role")
    return jax.shard_map(
        on_device, mesh=mesh, in_specs=(fine, nodes, nodes, P()), out_specs=(fine, nodes), check_vma=False
    )
```

```python
import functools
import math

import jax
import jax.numpy as jnp
import numpy as np
from jax import lax
from jax.experimental import pallas as pl
from jax.experimental.pallas import tpu as pltpu
from jax.sharding import PartitionSpec as P

sharpness = 4.0
threshold = 0.5
floor_stiff = 0.001
BEND = math.tanh(sharpness * threshold)
FULL = math.tanh(sharpness * threshold) + math.tanh(sharpness * (1.0 - threshold))
HAT = (1.0, 2.0, 3.0, 2.0, 1.0)

MESH = pl.DeviceIdType.MESH
F32 = jnp.float32
BF16 = jnp.bfloat16
I32 = jnp.int32
ROWS = 112
LANES = 128
GXN = 8
UPWARD = False
YN = 16
CHUNKS = (
    (0, 0, 0), (0, 0, 1), (0, 0, 2), (0, 0, 3), (0, 0, 4), (0, 0, 5),
    (1, 0, 0), (1, 0, 1), (1, 0, 4),
    (0, 1, 0), (0, 1, 2), (0, 1, 6),
    (1, 1, 0), (1, 1, 4),
)
PAIRS = {4: ((0, 0), (0, 1)), 5: ((1, 0), (1, 1)), 6: ((0, 0), (1, 0))}


def row_table():
    table = np.zeros((ROWS, 81), np.float32)
    seen = set()
    for place, (dx, dy, kind) in enumerate(CHUNKS):
        for half in range(2):
            if kind < 4:
                px, py, c = kind // 2, kind % 2, half
            else:
                (px, py), c = PAIRS[kind][half], 2
            if (dx and px) or (dy and py):
                continue
            a, b = px + 2 * dx, py + 2 * dy
            for q in range(3):
                index = ((c * 3 + b) * 3 + a) * 3 + q
                assert index not in seen
                seen.add(index)
                table[place * 8 + half * 4 + q, index] = 1.0
    assert len(seen) == 81
    return table


def place_of():
    role, gx, gy = lax.axis_index("role"), lax.axis_index("gx"), lax.axis_index("gy")
    return role, gx, gy, 2 * gy + role


def device_at(gx, row):
    gx = lax.rem(gx + GXN, GXN)
    row = lax.rem(row + YN, YN)
    return {"role": lax.rem(row, 2), "gx": gx, "gy": lax.div(row, 2)}


def remote(src, dst, send, recv, device):
    return pltpu.make_async_remote_copy(
        src_ref=src, dst_ref=dst, send_sem=send, recv_sem=recv, device_id=device, device_id_type=MESH
    )


def iota(shape, dim):
    return lax.broadcasted_iota(I32, shape, dim)


def pieces_of(values, count):
    parts = []
    for _ in range(count):
        part = values.astype(BF16)
        parts.append(part)
        values = values - part.astype(F32)
    return parts


def slab_of(shift):
    role, gx, gy, row = place_of()
    slab = lax.rem(gx * 8 + gy + shift + 64, 64)
    return lax.div(slab, 8), lax.rem(slab, 8)


def slab_device(shift, other):
    role = lax.axis_index("role")
    gx, gy = slab_of(shift)
    return {"role": (1 - role) if other else role, "gx": gx, "gy": gy}


def partner():
    return slab_device(0, True)


def reach(places, extent):
    total = jnp.zeros(places.shape, F32)
    for k, weight in enumerate(HAT):
        target = places + (k - 2)
        total = total + jnp.where(jnp.logical_and(target >= 0, target < extent), weight, 0.0)
    return jnp.maximum(total, 1.0)


def column_z(role, shape, dim):
    lane = iota(shape, dim)
    beyond = lane - LANES + jnp.where(role == 0, LANES, -2)
    return jnp.where(lane < LANES, lane, jnp.where(lane < LANES + 2, beyond, -4096))


def hat_of(distance):
    return jnp.maximum(3 - jnp.abs(distance), 0).astype(F32)


def at(field, e, f, kind):
    return field[e, kind // 2, 16 * f + 8 * (kind % 2) : 16 * f + 8 * (kind % 2) + 8]


def parity_matrix(role):
    rows, cols = iota((256, 256), 0), iota((256, 256), 1)
    half = jnp.where(rows < LANES, role, 1 - role)
    spot = half * LANES + lax.rem(rows, LANES)
    return (spot == 2 * lax.rem(cols, LANES) + lax.div(cols, LANES)).astype(F32).astype(BF16)


def parity_back(role):
    rows, cols = iota((256, 256), 0), iota((256, 256), 1)
    half = jnp.where(cols < LANES, role, 1 - role)
    spot = half * LANES + lax.rem(cols, LANES)
    return (spot == 2 * lax.rem(rows, LANES) + lax.div(rows, LANES)).astype(F32).astype(BF16)


def mul(left, right):
    return jnp.dot(left, right, preferred_element_type=F32)


def edge_stage(r):
    role = lax.axis_index("role")
    rows, cols = iota((16, LANES), 0), iota((16, LANES), 1)
    chosen = jnp.where(role == 0, 124 + rows, rows)
    chosen = jnp.logical_and(cols == chosen, rows < 4).astype(F32).astype(BF16)
    for x in range(4):
        total = None
        for part in pieces_of(r.design[x], 2):
            one = lax.dot_general(chosen, part, (((1,), (1,)), ((), ())), preferred_element_type=F32)
            total = one if total is None else total + one
        r.edge[:, 256 * x : 256 * x + 256] = total[:8]


def near_copies(r):
    return [
        remote(r.design.at[2:4], r.lo.at[2:4], r.dsend.at[0], r.drecv.at[0], slab_device(1, False)),
        remote(r.design.at[0:2], r.hi.at[0:2], r.dsend.at[1], r.drecv.at[1], slab_device(-1, False)),
        remote(r.edge, r.edges.at[1], r.dsend.at[2], r.drecv.at[2], slab_device(0, True)),
        remote(r.edge, r.edges.at[0], r.dsend.at[3], r.drecv.at[3], slab_device(1, True)),
        remote(r.edge, r.edges.at[2], r.dsend.at[4], r.drecv.at[4], slab_device(-1, True)),
    ]


def far_copies(r):
    return [
        remote(r.design.at[0:2], r.lo.at[0:2], r.dsend.at[5], r.drecv.at[5], slab_device(1, False)),
        remote(r.design.at[2:4], r.hi.at[2:4], r.dsend.at[6], r.drecv.at[6], slab_device(-1, False)),
    ]


def z_neighbour(upward):
    role, gx, gy, row = place_of()
    low = lax.rem(gx, 2)
    same = (low == 0) if upward else (low == 1)
    return {
        "role": jnp.where(same, role, 1 - role), "gx": gx + 1 - 2 * low, "gy": gy,
    }


def force_copy(r):
    spot = pl.ds(pl.multiple_of(8 * (1 - lax.axis_index("role")), 8), 8)
    return remote(r.force.at[:, :, spot], r.force_other, r.dsend.at[7], r.drecv.at[7], partner())


def mask_hop(r, q):
    spot = pl.ds(pl.multiple_of(8 * (1 - lax.axis_index("role")), 8), 8)
    return remote(
        r.mask.at[q, :, spot], r.relay.at[q], r.dsend.at[8 + q], r.drecv.at[8 + q], z_neighbour(UPWARD)
    )


def mask_copy(r, q):
    return remote(
        r.relay.at[q], r.mask_other.at[q], r.dsend.at[11 + q], r.drecv.at[11 + q], z_neighbour(UPWARD)
    )


def swap_stage(r):
    near = near_copies(r)
    for copy in near:
        copy.start()
    for q in range(3):
        mask_hop(r, q).start()
    force_copy(r).start()
    for copy in far_copies(r):
        copy.start()
    table_stage(r)
    for q in range(3):
        mask_hop(r, q).wait()
        mask_copy(r, q).start()
    for copy in near:
        copy.wait()


def table_stage(r):
    chosen = r.chosen[...].astype(BF16)
    table = None
    for part in pieces_of(r.stiffness[...], 3):
        one = mul(chosen, part)
        table = one if table is None else table + one
    whole = None
    for part in pieces_of(table, 3):
        one = lax.dot_general(part, chosen, (((1,), (1,)), ((), ())), preferred_element_type=F32)
        whole = one if whole is None else whole + one
    high, low = pieces_of(whole, 2)
    r.stiff[...] = jnp.concatenate(
        [
            jnp.concatenate([high, high], axis=1),
            jnp.concatenate([low, jnp.zeros_like(low)], axis=1),
        ],
        axis=0,
    )


def mix(get):
    return 3.0 * get(2) + 2.0 * (get(1) + get(3)) + (get(0) + get(4))


def taps_stage(r, planes):
    role = lax.axis_index("role")
    band = hat_of(column_z(role, (LANES, 256), 1) - iota((LANES, 256), 0)).astype(BF16)
    bands = jnp.concatenate([band, band], axis=0)
    far = lax.rem(iota((16, 256), 0), 8)
    spot = jnp.where(role == 0, LANES + far, far - 4)
    rim = hat_of(column_z(role, (16, 256), 1) - spot)
    rim = jnp.where(far < 4, rim, 0.0).astype(BF16)

    def plane(p, rows):
        ref = (r.lo, r.design, r.hi)[p // 4]
        return ref[p % 4, rows]

    for i in planes:
        beyond = mix(lambda k: r.edges[(i + k) // 4, :, 256 * ((i + k) % 4) : 256 * ((i + k) % 4) + 256])
        beyond = jnp.concatenate(pieces_of(beyond, 2), axis=0)
        beyond = lax.dot_general(beyond, rim, (((0,), (0,)), ((), ())), preferred_element_type=F32)
        for b in range(4):
            rows = slice(64 * b, 64 * b + 64)
            wide = mix(lambda k: plane(i + k, rows))
            out = mul(jnp.concatenate(pieces_of(wide, 2), axis=1), bands)
            r.zc[i, 8 + 64 * b : 72 + 64 * b] = out + beyond[rows]
        r.zc[i, 0:8] = jnp.zeros((8, 256), F32)
        r.zc[i, 264:272] = jnp.zeros((8, 256), F32)


def bend_stage(r, count, plane_of, shown):
    role, gx, gy, row = place_of()
    slab = gx * 8 + gy
    z_places = column_z(role, (1, 256), 1) + role * LANES
    by_z = 1.0 / reach(z_places, 256)

    def body(step, _):
        i = plane_of(step)
        x = 4 * slab + i - 2
        inside = jnp.logical_and(x >= 0, x < 256)
        by_x = 1.0 / reach(jnp.full((1, 256), x, I32), 256)
        by_xz = by_z * by_x
        for b in range(8):
            first = 32 * b
            by = by_xz / reach(iota((32, 256), 0) + first, 256)
            total = mix(lambda k: r.zc[i, 6 + k + first : 38 + k + first])
            bent = jnp.tanh(sharpness * (total * by - threshold))
            r.m[i, first : first + 32] = jnp.where(inside, (1.0 - bent * bent) * (by * (sharpness / FULL)), 0.0)
            if shown:
                r.psum[first : first + 32] += (BEND + bent[:, :LANES]) * (1.0 / FULL)
        return 0

    lax.fori_loop(0, count, body, 0)


def inner_stage(r):
    role, gx, gy, row = place_of()
    slab = gx * 8 + gy

    @pl.when(slab == 0)
    def _():
        r.lo[2:4] = jnp.zeros((2, 256, LANES), F32)
        r.edges[0] = jnp.zeros((8, 1024), F32)

    @pl.when(slab == 63)
    def _():
        r.hi[0:2] = jnp.zeros((2, 256, LANES), F32)
        r.edges[2] = jnp.zeros((8, 1024), F32)

    taps_stage(r, (2, 3, 4, 5))
    r.psum[...] = jnp.zeros_like(r.psum)
    bend_stage(r, 4, lambda step: step + 2, True)
    density_stage(r)


def outer_stage(r):
    role, gx, gy, row = place_of()
    slab = gx * 8 + gy
    for copy in far_copies(r):
        copy.wait()

    @pl.when(slab == 0)
    def _():
        r.lo[0:2] = jnp.zeros((2, 256, LANES), F32)

    @pl.when(slab == 63)
    def _():
        r.hi[2:4] = jnp.zeros((2, 256, LANES), F32)

    taps_stage(r, (0, 1, 6, 7))
    bend_stage(r, 4, lambda step: jnp.where(step < 2, step, step + 4), False)


def density_stage(r):
    role = lax.axis_index("role")
    rows, cols = iota((LANES, 256), 0), iota((LANES, 256), 1)
    gather = jnp.logical_and(
        lax.div(cols, 16) == lax.div(rows, 8), lax.div(lax.rem(cols, 16), 4) == lax.rem(rows, 8)
    ).astype(F32).astype(BF16)
    parts = pieces_of(r.psum[...], 3)
    by_rows = mul(gather, parts[0]) + mul(gather, parts[1]) + mul(gather, parts[2])
    rows, cols = iota((LANES, LANES), 0), iota((LANES, LANES), 1)
    merge = (cols == 64 * role + lax.div(rows, 2)).astype(F32).astype(BF16)
    parts = pieces_of(by_rows, 3)
    density = (mul(parts[0], merge) + mul(parts[1], merge) + mul(parts[2], merge)) * (1.0 / 32.0)
    for k in range(YN):
        r.dens[k] = density[8 * k : 8 * k + 8]


def pack_stage(r):
    force_copy(r).wait()
    for q in range(3):
        mask_copy(r, q).wait()
    role = lax.axis_index("role")
    matrix = parity_matrix(role)
    spot = pl.ds(pl.multiple_of(8 * role, 8), 8)
    r.vf[...] = jnp.zeros_like(r.vf)
    for q in range(3):
        own = r.force[q, :, spot].reshape(LANES, LANES)
        wide = jnp.concatenate([own, r.force_other[q].reshape(LANES, LANES)], axis=1)
        force = None
        for part in pieces_of(wide, 3):
            one = mul(part, matrix)
            force = one if force is None else force + one
        own = r.mask[q, :, spot].reshape(LANES, LANES)
        wide = jnp.concatenate([own, r.mask_other[q].reshape(LANES, LANES)], axis=1)
        free = mul((1 - wide).astype(F32).astype(BF16), matrix)
        force = force * free
        for x in range(16):
            for half in range(2):
                for kind, values in ((0, force), (1, free)):
                    r.vf[kind, x // 2, x % 2, pl.ds(4 * half + q, 8, stride=8)] = values[
                        8 * x : 8 * x + 8, LANES * half : LANES * half + LANES
                    ]


def density_copies(r):
    role, gx, gy, row = place_of()
    copies = []
    for k in range(1, YN):
        target = lax.rem(row + k, YN)
        copies.append(
            remote(r.dens.at[target], r.dall.at[row], r.nsend.at[k], r.nrecv.at[k], device_at(gx, row + k))
        )
    return copies


def upper_copies(r):
    role, gx, gy, row = place_of()
    return [
        remote(r.vf.at[:, 0, 0], r.nxhi, r.nsend.at[16], r.nrecv.at[16], device_at(gx - 1, row)),
        remote(r.vf.at[:, :, :, 0:8], r.nyhi, r.nsend.at[17], r.nrecv.at[17], device_at(gx, row - 1)),
        remote(r.vf.at[:, 0, 0, 0:8], r.ncorner, r.nsend.at[18], r.nrecv.at[18], device_at(gx - 1, row - 1)),
    ]


def spread_stage(r):
    role, gx, gy, row = place_of()
    for copy in density_copies(r):
        copy.start()
    r.dall[row] = r.dens[row]


def upper_stage(r):
    for copy in upper_copies(r):
        copy.start()


def frame_stage(r):
    for copy in density_copies(r) + upper_copies(r):
        copy.wait()
    role, gx, gy, row = place_of()
    has_x, has_y = gx < GXN - 1, row < YN - 1
    has_both = jnp.logical_and(has_x, has_y)
    for kind, ref in ((0, r.r0), (1, r.free)):
        for e in range(8):
            for px in range(2):
                ref[e, px, 0:64] = r.vf[kind, e, px]
                ref[e, px, 64:72] = jnp.where(has_y, r.nyhi[kind, e, px], 0.0)
                ref[e, px, 72:80] = jnp.zeros((8, LANES), F32)
        ref[8, 0, 0:64] = jnp.where(has_x, r.nxhi[kind], 0.0)
        ref[8, 0, 64:72] = jnp.where(has_both, r.ncorner[kind], 0.0)
        ref[8, 0, 72:80] = jnp.zeros((8, LANES), F32)
        ref[8, 1] = jnp.zeros((80, LANES), F32)
    for e in range(8):
        r.rho[e] = r.dall[2 * e] + r.dall[2 * e + 1]


def build_store(field, store):
    sub = iota((8, LANES), 0) < 4
    inside = iota((8, LANES), 1) < LANES - 1

    def body(e, _):
        for f in range(5):
            held = [at(field, e, f, k) for k in range(4)]
            shifted = [jnp.where(inside, pltpu.roll(v, LANES - 1, 1), 0.0) for v in held]
            turned = [None] + [pltpu.roll(v, 4, 0) for v in shifted[1:]]
            for k in range(4):
                store[e, f, k] = held[k]
            store[e, f, 4] = jnp.where(sub, shifted[0], turned[1])
            store[e, f, 5] = jnp.where(sub, shifted[2], turned[3])
            store[e, f, 6] = jnp.where(sub, shifted[0], turned[2])
        return 0

    lax.fori_loop(0, 9, body, 0)


def element_product(store, stiff, e):
    columns = []
    for f in range(4):
        columns.append(jnp.concatenate([store[e + dx, f + dy, kind] for dx, dy, kind in CHUNKS], axis=0))
    wide = jnp.concatenate(columns, axis=1)
    out = mul(stiff, jnp.concatenate(pieces_of(wide, 2), axis=0))
    product = out[:ROWS] + out[ROWS:]
    return columns, [product[:, f * LANES : (f + 1) * LANES] for f in range(4)]


def chunk_sum(left, right):
    both = left * right
    total = both[:8]
    for k in range(1, len(CHUNKS)):
        total = total + both[8 * k : 8 * k + 8]
    return total


def factor_of(rho):
    return floor_stiff + (1.0 - floor_stiff) * (rho * rho * rho)


def apply_operator(r, image):
    store, acc = r.store, r.acc
    acc[...] = jnp.zeros_like(acc)
    stiff = r.stiff[...]

    def body(e, energy):
        columns, products = element_product(store, stiff, e)
        factor = factor_of(r.rho[e])
        for f in range(4):
            scaled = products[f] * factor[f : f + 1, :]
            energy = energy + chunk_sum(columns[f], scaled)
            for place, (dx, dy, kind) in enumerate(CHUNKS):
                acc[e + dx, f + dy, kind] += scaled[8 * place : 8 * place + 8]
        return energy

    energy = lax.fori_loop(0, 8, body, jnp.zeros((8, LANES), F32))
    keep = jnp.logical_and(iota((8, LANES), 0) < 4, iota((8, LANES), 1) > 0)

    def fold(e, _):
        for f in range(5):
            z0, z1, z2 = acc[e, f, 4], acc[e, f, 5], acc[e, f, 6]
            t0, t1, t2 = (pltpu.roll(v, 4, 0) for v in (z0, z1, z2))
            for k, extra in enumerate((z0 + z2, t0, z1 + t2, t1)):
                extra = jnp.where(keep, pltpu.roll(extra, 1, 1), 0.0)
                first = 16 * f + 8 * (k % 2)
                image[e, k // 2, first : first + 8] = acc[e, f, k] + extra
        return 0

    lax.fori_loop(0, 9, fold, 0)
    return energy


def element_energy(r):
    stiff = r.stiff[...]

    def body(e, energy):
        columns, products = element_product(r.store, stiff, e)
        factor = factor_of(r.rho[e])
        for f in range(4):
            energy = energy + chunk_sum(columns[f], products[f] * factor[f : f + 1, :])
        return energy

    return lax.fori_loop(0, 8, body, jnp.zeros((8, LANES), F32))


def square_sum(field):
    def body(e, total):
        for f in range(4):
            for k in range(4):
                held = at(field, e, f, k)
                total = total + held * held
        return total

    return lax.fori_loop(0, 8, body, jnp.zeros((8, LANES), F32))


def sums_tile(gamma, delta):
    gamma = jnp.sum(gamma, axis=0, keepdims=True)
    delta = jnp.sum(delta, axis=0, keepdims=True)
    gamma, delta = gamma + pltpu.roll(gamma, 64, 1), delta + pltpu.roll(delta, 64, 1)
    return jnp.where(iota((1, LANES), 1) < 64, gamma, delta)


def read_sums(sum_ref):
    held, low = sum_ref[...], iota((1, LANES), 1) < 64
    return (
        jnp.sum(jnp.where(low, held, 0.0), axis=1, keepdims=True),
        jnp.sum(jnp.where(low, 0.0, held), axis=1, keepdims=True),
    )


def over_nodes(body):
    def step(e, _):
        body(e)
        return 0

    lax.fori_loop(0, 9, step, 0)


def gy_device(shift):
    role, gx, gy, row = place_of()
    return {"role": role, "gx": gx, "gy": lax.rem(gy + shift, 8)}


def cross_device(shift):
    role, gx, gy, row = place_of()
    target = lax.rem(2 * gx + role + shift, 16)
    return {"role": lax.rem(target, 2), "gx": lax.div(target, 2), "gy": gy}


def reduce_parts(r, n):
    role, gx, gy, row = place_of()
    mine, slots, half, send, recv = r["tile", n], r["slots", n], r["half", n], r["rsend", n], r["rrecv", n]
    slots[gy] = mine[...]
    for k in range(1, 8):
        remote(mine, slots.at[gy], send.at[0], recv.at[0], gy_device(k)).start()
    remote(slots.at[0:7], slots.at[0:7], send.at[0], recv.at[0], partner()).wait()
    part = jnp.sum(slots[0:8], axis=0)
    half[...] = part
    place = 8 + 2 * gx + role
    slots[place] = part
    for k in range(1, 16):
        remote(half, slots.at[place], send.at[1], recv.at[1], cross_device(k)).start()
    remote(slots.at[8:23], slots.at[8:23], send.at[1], recv.at[1], partner()).wait()
    r["sum", n][...] = jnp.sum(slots[8:24], axis=0)


FACE_MOVES = ((1, 0), (-1, 0), (0, 1), (0, -1), (1, 1), (1, -1), (-1, 1), (-1, -1))


def face_stage(r, n):
    role, gx, gy, row = place_of()
    image, corners = r["image", n], r["corners", n]
    ends = (
        (image.at[8, 0], r["xlo", n]),
        (image.at[0, 0], r["xhi", n]),
        (image.at[:, :, 64:72], r["ylo", n]),
        (image.at[:, :, 0:8], r["yhi", n]),
        (image.at[8, 0, 64:72], corners.at[0]),
        (image.at[8, 0, 0:8], corners.at[1]),
        (image.at[0, 0, 64:72], corners.at[2]),
        (image.at[0, 0, 0:8], corners.at[3]),
    )
    send, recv = r["fsend", n], r["frecv", n]
    copies = []
    for k, ((dx, dy), (src, dst)) in enumerate(zip(FACE_MOVES, ends)):
        copies.append(remote(src, dst, send.at[k], recv.at[k], device_at(gx + dx, row + dy)))
    for copy in copies:
        copy.start()
    reduce_parts(r, n)
    for copy in copies:
        copy.wait()


def add_faces(r, n, work):
    role, gx, gy, row = place_of()
    low_x, low_y = gx > 0, row > 0
    image, corners = r["image", n], r["corners", n]
    xlo, xhi, ylo, yhi = (r[name, n] for name in ("xlo", "xhi", "ylo", "yhi"))
    work[...] = image[...]
    work[0, 0] += jnp.where(low_x, xlo[...], 0.0)
    work[8, 0] += xhi[...]
    for e in range(9):
        for p in range(2):
            work[e, p, 0:8] += jnp.where(low_y, ylo[e, p], 0.0)
            work[e, p, 64:72] += yhi[e, p]
    work[0, 0, 0:8] += jnp.where(jnp.logical_and(low_x, low_y), corners[0], 0.0)
    work[0, 0, 64:72] += jnp.where(low_x, corners[1], 0.0)
    work[8, 0, 0:8] += jnp.where(low_y, corners[2], 0.0)
    work[8, 0, 64:72] += corners[3]
    work[...] = work[...] * r.free[...]


def spare(value):
    return value.reshape(1, 1, 1)


def first_stage(r):
    build_store(r.r0, r.store)
    delta = apply_operator(r, r["image", 0])
    r["tile", 0][...] = sums_tile(square_sum(r.r0), delta)


def second_stage(r):
    add_faces(r, 0, r.s0)
    gamma, delta = read_sums(r["sum", 0])
    alpha = spare(gamma / delta)

    def update(e):
        r.r1[e] = r.r0[e] - alpha * r.s0[e]

    over_nodes(update)
    build_store(r.r1, r.store)
    delta = apply_operator(r, r["image", 1])
    r["tile", 1][...] = sums_tile(square_sum(r.r1), delta)


def third_stage(r):
    add_faces(r, 1, r.work)
    gamma0, delta0 = read_sums(r["sum", 0])
    gamma1, delta1 = read_sums(r["sum", 1])
    alpha0 = gamma0 / delta0
    beta1 = gamma1 / gamma0
    alpha1 = gamma1 / (delta1 - beta1 * gamma1 / alpha0)
    alpha0, alpha1, beta1 = spare(alpha0), spare(alpha1), spare(beta1)

    def update(e):
        p = r.r1[e] + beta1 * r.r0[e]
        r.p1[e] = p
        r.u1[e] = alpha0 * r.r0[e] + alpha1 * p
        r.r2[e] = r.r1[e] - alpha1 * (r.work[e] + beta1 * r.s0[e])

    over_nodes(update)
    build_store(r.r2, r.store)
    delta = element_energy(r)
    r["tile", 2][...] = sums_tile(square_sum(r.r2), delta)


def reduce_stage(r):
    reduce_parts(r, 2)


def last_stage(r):
    gamma0, delta0 = read_sums(r["sum", 0])
    gamma1, delta1 = read_sums(r["sum", 1])
    gamma2, delta2 = read_sums(r["sum", 2])
    alpha0 = gamma0 / delta0
    beta1 = gamma1 / gamma0
    alpha1 = gamma1 / (delta1 - beta1 * gamma1 / alpha0)
    beta2 = gamma2 / gamma1
    alpha2 = spare(gamma2 / (delta2 - beta2 * gamma2 / alpha1))
    beta2 = spare(beta2)

    def update(e):
        r.u[e] = r.u1[e] + alpha2 * (r.r2[e] + beta2 * r.p1[e])

    over_nodes(update)
    build_store(r.u, r.store)
    stiff = r.stiff[...]
    rows = iota((8, LANES), 0)

    def body(e, before):
        columns, products = element_product(r.store, stiff, e)
        rho = r.rho[e]
        energy = jnp.zeros((8, LANES), F32)
        for f in range(4):
            one = jnp.sum(chunk_sum(columns[f], products[f]), axis=0, keepdims=True)
            energy = jnp.where(rows == f, one, energy)
        layer = (-3.0 * (1.0 - floor_stiff) / 32.0) * (rho * rho) * energy
        r.grad[e] = before + pltpu.roll(layer, 4, 0)
        return layer

    r.grad[8] = lax.fori_loop(0, 8, body, jnp.zeros((8, LANES), F32))


def edge_targets():
    role, gx, gy, row = place_of()
    up, down = lax.rem(gx + 1, GXN), lax.rem(gx + GXN - 1, GXN)
    return [
        {"role": 0, "gx": up, "gy": 0},
        {"role": 1, "gx": up, "gy": 0},
        {"role": 0, "gx": down, "gy": 7},
        {"role": 1, "gx": down, "gy": 7},
    ]


def gradient_copies(r):
    role, gx, gy, row = place_of()
    copies = []
    for k in range(1, YN):
        target = lax.div(lax.rem(row + k, YN), 2)
        copies.append(
            remote(r.grad.at[pl.ds(target, 2)], r.gall.at[row], r.gsend.at[k], r.grecv.at[k], device_at(gx, row + k))
        )
    return copies


def rim_copies(r):
    role, gx, gy, row = place_of()
    copies = []
    for k, device in enumerate(edge_targets()):
        layer = 8 if k < 2 else 0
        copies.append(remote(r.grad.at[layer], r.grim.at[row], r.esend.at[k], r.erecv.at[row], device))
    return copies


def gradient_stage(r):
    role, gx, gy, row = place_of()
    copies, rims = gradient_copies(r), rim_copies(r)
    for copy in copies + rims:
        copy.start()
    r.gall[row] = r.grad[pl.ds(gy, 2)]
    for copy in copies:
        copy.wait()
    for copy in rims:
        copy.wait_send()

    @pl.when(jnp.logical_or(gy == 0, gy == 7))
    def _():
        for k in range(YN):
            remote(r.grad.at[1], r.grim.at[k], r.esend.at[0], r.erecv.at[k], partner()).wait_recv()


def unpack_stage(r):
    role = lax.axis_index("role")
    back = parity_back(role)
    spot = pl.ds(pl.multiple_of(8 * role, 8), 8)
    for q in range(3):
        even = [r.u[x // 2, x % 2, pl.ds(q, 8, stride=8)] for x in range(16)]
        odd = [r.u[x // 2, x % 2, pl.ds(4 + q, 8, stride=8)] for x in range(16)]
        wide = jnp.concatenate([jnp.concatenate(even, axis=0), jnp.concatenate(odd, axis=0)], axis=1)
        total = None
        for part in pieces_of(wide, 3):
            one = mul(part, back)
            total = one if total is None else total + one
        r.disp[q, :, spot] = total[:, :LANES].reshape(16, 8, LANES)
        r.give[q] = total[:, LANES:].reshape(16, 8, LANES)


def give_copy(r):
    role = lax.axis_index("role")
    spot = pl.ds(pl.multiple_of(8 * role, 8), 8)
    return remote(r.give, r.disp.at[:, :, spot], r.osend.at[0], r.orecv.at[0], partner())


def give_stage(r):
    give_copy(r).start()


def given_stage(r):
    give_copy(r).wait()


def final_stage(r):
    role, gx, gy, row = place_of()
    for k in range(YN):
        r.layers[0, 8 * k : 8 * k + 8] = r.gall[k, 0]
        r.layers[1, 8 * k : 8 * k + 8] = r.gall[k, 0]
        r.layers[2, 8 * k : 8 * k + 8] = r.gall[k, 1]

    @pl.when(gy == 0)
    def _():
        for k in range(YN):
            r.layers[0, 8 * k : 8 * k + 8] = r.grim[k]

    @pl.when(gy == 7)
    def _():
        for k in range(YN):
            r.layers[2, 8 * k : 8 * k + 8] = r.grim[k]

    rows = iota((LANES, 256), 0)
    z = column_z(role, (LANES, 256), 1) + role * LANES
    widen = jnp.logical_and(z >= 0, rows == lax.div(jnp.maximum(z, 0), 2)).astype(F32).astype(BF16)
    widen = jnp.concatenate([widen, widen], axis=0)
    rows, cols = iota((256, LANES), 0), iota((256, LANES), 1)
    cols = cols - 8 * lax.div(rows, 16) - lax.div(lax.rem(rows, 16), 4)
    for k in range(3):
        repeat = (cols == (4 if k else 0)).astype(F32).astype(BF16)
        repeat = jnp.concatenate([repeat, repeat], axis=1)
        wide = mul(jnp.concatenate(pieces_of(r.layers[k], 2), axis=1), widen)
        r.wide[k] = mul(repeat, jnp.concatenate(pieces_of(wide, 2), axis=0))
    band = hat_of(iota((256, LANES), 1) - column_z(role, (256, LANES), 0)).astype(BF16)
    bands = jnp.concatenate([band, band], axis=0)
    for o in range(4):
        r.zc[o, 0:8] = jnp.zeros((8, 256), F32)
        r.zc[o, 264:272] = jnp.zeros((8, 256), F32)
        for b in range(8):
            spot = slice(32 * b, 32 * b + 32)
            total = None
            for layer, planes in ((0, (0, 1)), (1, (2, 3, 4, 5)), (2, (6, 7))):
                part = None
                for i in planes:
                    if o <= i <= o + 4:
                        one = HAT[i - o] * r.m[i, spot]
                        part = one if part is None else part + one
                if part is not None:
                    part = part * r.wide[layer, spot]
                    total = part if total is None else total + part
            r.zc[o, 8 + 32 * b : 40 + 32 * b] = total
        for b in range(8):
            first = 32 * b
            total = (
                3.0 * r.zc[o, 8 + first : 40 + first]
                + 2.0 * (r.zc[o, 7 + first : 39 + first] + r.zc[o, 9 + first : 41 + first])
                + (r.zc[o, 6 + first : 38 + first] + r.zc[o, 10 + first : 42 + first])
            )
            r.sens[o, first : first + 32] = mul(jnp.concatenate(pieces_of(total, 2), axis=1), bands)


FIELD = (9, 2, 80, LANES)
TILE = (1, LANES)


class Refs(dict):
    def __getattr__(self, name):
        return self[name]


def buffers():
    shapes = {
        "edge": (8, 1024), "lo": (4, 256, LANES), "hi": (4, 256, LANES), "edges": (3, 8, 1024),
        "force_other": (3, 16, 8, LANES), "m": (8, 256, 256), "zc": (8, 272, 256), "psum": (256, LANES),
        "dens": (YN, 8, LANES), "vf": (2, 8, 2, 64, LANES), "nxhi": (2, 64, LANES), "nyhi": (2, 8, 2, 8, LANES),
        "ncorner": (2, 8, LANES), "dall": (YN, 8, LANES), "rho": (8, 8, LANES), "store": (9, 5, 7, 8, LANES),
        "acc": (9, 5, 7, 8, LANES), "grad": (9, 8, LANES), "gall": (YN, 2, 8, LANES), "grim": (YN, 8, LANES),
        "give": (3, 16, 8, LANES), "layers": (3, LANES, LANES), "wide": (3, 256, 256),
    }
    for name in ("r0", "free", "s0", "r1", "p1", "u1", "r2", "u", "work"):
        shapes[name] = FIELD
    for n in range(3):
        shapes["tile", n] = shapes["sum", n] = shapes["half", n] = TILE
        shapes["slots", n] = (24, 1, LANES)
    for n in range(2):
        shapes["image", n] = FIELD
        shapes["xlo", n] = shapes["xhi", n] = (80, LANES)
        shapes["ylo", n] = shapes["yhi", n] = (9, 2, 8, LANES)
        shapes["corners", n] = (4, 8, LANES)
    scratch = {name: pltpu.VMEM(shape, F32) for name, shape in shapes.items()}
    scratch["relay"] = pltpu.VMEM((3, 16, 8, LANES), I32)
    scratch["mask_other"] = pltpu.VMEM((3, 16, 8, LANES), I32)
    scratch["stiff"] = pltpu.VMEM((2 * ROWS, 2 * ROWS), BF16)
    counts = {"dsend": 14, "drecv": 14, "nsend": 19, "nrecv": 19, "gsend": 16, "grecv": 16, "esend": 4, "erecv": 16,
              "osend": 1, "orecv": 1}
    for n in range(3):
        counts["rsend", n] = counts["rrecv", n] = 2
        counts["fsend", n] = counts["frecv", n] = 8
    for name, count in counts.items():
        scratch[name] = pltpu.SemaphoreType.DMA((count,))
    return scratch


def greet_all():
    role, gx, gy, row = place_of()
    barrier = pltpu.get_barrier_semaphore()
    devices = [device_at(gx, row + k) for k in range(1, YN)]
    devices += [cross_device(k) for k in range(1, 16)]
    devices += [device_at(gx + dx, row + dy) for dx, dy in FACE_MOVES[4:]]
    devices += [slab_device(shift, other) for shift, other in ((1, False), (-1, False), (1, True), (-1, True))]
    devices += [z_neighbour(True), z_neighbour(False), device_at(gx + 1, row), device_at(gx - 1, row)]
    for device in devices:
        pl.semaphore_signal(barrier, inc=1, device_id=device, device_id_type=MESH)

    @pl.when(gy == 0)
    def _():
        for k in range(YN):
            pl.semaphore_signal(barrier, inc=1, device_id=device_at(gx - 1, row * 0 + k), device_id_type=MESH)

    @pl.when(gy == 7)
    def _():
        for k in range(YN):
            pl.semaphore_signal(barrier, inc=1, device_id=device_at(gx + 1, row * 0 + k), device_id_type=MESH)

    return len(devices) + 4


def whole_kernel(names, *refs):
    r = Refs(zip(names, refs))
    count = greet_all()
    edge_stage(r)
    pl.semaphore_wait(pltpu.get_barrier_semaphore(), count)
    swap_stage(r)
    inner_stage(r)
    spread_stage(r)
    pack_stage(r)
    upper_stage(r)
    outer_stage(r)
    frame_stage(r)
    first_stage(r)
    face_stage(r, 0)
    second_stage(r)
    face_stage(r, 1)
    third_stage(r)
    reduce_stage(r)
    last_stage(r)
    gradient_stage(r)
    unpack_stage(r)
    give_stage(r)
    final_stage(r)
    given_stage(r)


def on_device(design, force, clamped_dof_mask, stiffness):
    chosen = jnp.asarray(row_table())
    scratch = buffers()
    names = ["design", "force", "mask", "stiffness", "chosen", "sens", "disp"] + list(scratch)
    vmem = pl.BlockSpec(memory_space=pltpu.VMEM)
    return pl.pallas_call(
        functools.partial(whole_kernel, names),
        out_shape=(
            jax.ShapeDtypeStruct((4, 256, LANES), F32),
            jax.ShapeDtypeStruct((3, 16, 16, LANES), F32),
        ),
        in_specs=[vmem] * 5,
        out_specs=(vmem, vmem),
        scratch_shapes=list(scratch.values()),
        compiler_params=pltpu.CompilerParams(
            collective_id=0, has_side_effects=True, vmem_limit_bytes=36 * 1024 * 1024
        ),
        name="compliance",
    )(design, force, clamped_dof_mask, stiffness, chosen)


def solution(mesh):
    fine = P(("gx", "gy"), None, "role")
    nodes = P(None, "gx", "gy", "role")
    return jax.shard_map(
        on_device, mesh=mesh, in_specs=(fine, nodes, nodes, P()), out_specs=(fine, nodes), check_vma=False
    )
```

```python
import functools
import math

import jax
import jax.numpy as jnp
import numpy as np
from jax import lax
from jax.experimental import pallas as pl
from jax.experimental.pallas import tpu as pltpu
from jax.sharding import PartitionSpec as P

sharpness = 4.0
threshold = 0.5
floor_stiff = 0.001
BEND = math.tanh(sharpness * threshold)
FULL = math.tanh(sharpness * threshold) + math.tanh(sharpness * (1.0 - threshold))
HAT = (1.0, 2.0, 3.0, 2.0, 1.0)

MESH = pl.DeviceIdType.MESH
F32 = jnp.float32
BF16 = jnp.bfloat16
I32 = jnp.int32
ROWS = 112
LANES = 128
GXN = 8
GYN = 8
LAST = 9
CHUNKS = (
    (0, 0, 0), (0, 0, 1), (0, 0, 2), (0, 0, 3), (0, 0, 4), (0, 0, 5),
    (1, 0, 0), (1, 0, 1), (1, 0, 4),
    (0, 1, 0), (0, 1, 2), (0, 1, 6),
    (1, 1, 0), (1, 1, 4),
)
PAIRS = {4: ((0, 0), (0, 1)), 5: ((1, 0), (1, 1)), 6: ((0, 0), (1, 0))}


def row_table():
    table = np.zeros((ROWS, 81), np.float32)
    seen = set()
    for place, (dx, dy, kind) in enumerate(CHUNKS):
        for half in range(2):
            if kind < 4:
                px, py, c = kind // 2, kind % 2, half
            else:
                (px, py), c = PAIRS[kind][half], 2
            if (dx and px) or (dy and py):
                continue
            a, b = px + 2 * dx, py + 2 * dy
            for q in range(3):
                index = ((c * 3 + b) * 3 + a) * 3 + q
                assert index not in seen
                seen.add(index)
                table[place * 8 + half * 4 + q, index] = 1.0
    assert len(seen) == 81
    return table


def place_of():
    return lax.axis_index("role"), lax.axis_index("gx"), lax.axis_index("gy")


def device_at(dx, dy, other=False):
    role, gx, gy = place_of()
    return {
        "role": (1 - role) if other else role,
        "gx": lax.rem(gx + dx + GXN, GXN),
        "gy": lax.rem(gy + dy + GYN, GYN),
    }


def remote(src, dst, send, recv, device):
    return pltpu.make_async_remote_copy(
        src_ref=src, dst_ref=dst, send_sem=send, recv_sem=recv, device_id=device, device_id_type=MESH
    )


def iota(shape, dim):
    return lax.broadcasted_iota(I32, shape, dim)


def pieces_of(values, count):
    parts = []
    for _ in range(count):
        part = values.astype(BF16)
        parts.append(part)
        values = values - part.astype(F32)
    return parts


def slab_of(shift):
    role, gx, gy = place_of()
    slab = lax.rem(gx * 8 + gy + shift + 64, 64)
    return lax.div(slab, 8), lax.rem(slab, 8)


def slab_device(shift, other):
    role = lax.axis_index("role")
    gx, gy = slab_of(shift)
    return {"role": (1 - role) if other else role, "gx": gx, "gy": gy}


def reach(places, extent):
    total = jnp.zeros(places.shape, F32)
    for k, weight in enumerate(HAT):
        target = places + (k - 2)
        total = total + jnp.where(jnp.logical_and(target >= 0, target < extent), weight, 0.0)
    return jnp.maximum(total, 1.0)


def column_z(role, shape, dim):
    lane = iota(shape, dim)
    beyond = lane - LANES + jnp.where(role == 0, LANES, -2)
    return jnp.where(lane < LANES, lane, jnp.where(lane < LANES + 2, beyond, -4096))


def hat_of(distance):
    return jnp.maximum(3 - jnp.abs(distance), 0).astype(F32)


def at(field, e, f, kind):
    return field[e, kind // 2, 16 * f + 8 * (kind % 2) : 16 * f + 8 * (kind % 2) + 8]


def parity_matrix():
    rows, cols = iota((256, 256), 0), iota((256, 256), 1)
    return (rows == 2 * lax.rem(cols, LANES) + lax.div(cols, LANES)).astype(F32).astype(BF16)


def parity_back():
    rows, cols = iota((256, 256), 0), iota((256, 256), 1)
    return (cols == 2 * lax.rem(rows, LANES) + lax.div(rows, LANES)).astype(F32).astype(BF16)


def mul(left, right):
    return jnp.dot(left, right, preferred_element_type=F32)


def edge_stage(r):
    role = lax.axis_index("role")
    rows, cols = iota((16, LANES), 0), iota((16, LANES), 1)
    chosen = jnp.where(role == 0, 124 + rows, rows)
    chosen = jnp.logical_and(cols == chosen, rows < 4).astype(F32).astype(BF16)
    for x in range(4):
        total = None
        for part in pieces_of(r.design[x], 2):
            one = lax.dot_general(chosen, part, (((1,), (1,)), ((), ())), preferred_element_type=F32)
            total = one if total is None else total + one
        r.edge[:, 256 * x : 256 * x + 256] = total[:8]


def near_copies(r):
    return [
        remote(r.design.at[2:4], r.lo.at[2:4], r.dsend.at[0], r.drecv.at[0], slab_device(1, False)),
        remote(r.design.at[0:2], r.hi.at[0:2], r.dsend.at[1], r.drecv.at[1], slab_device(-1, False)),
        remote(r.edge, r.edges.at[1], r.dsend.at[2], r.drecv.at[2], slab_device(0, True)),
        remote(r.edge, r.edges.at[0], r.dsend.at[3], r.drecv.at[3], slab_device(1, True)),
        remote(r.edge, r.edges.at[2], r.dsend.at[4], r.drecv.at[4], slab_device(-1, True)),
    ]


def far_copies(r):
    return [
        remote(r.design.at[0:2], r.lo.at[0:2], r.dsend.at[5], r.drecv.at[5], slab_device(1, False)),
        remote(r.design.at[2:4], r.hi.at[2:4], r.dsend.at[6], r.drecv.at[6], slab_device(-1, False)),
    ]


def swap_stage(r):
    for copy in near_copies(r) + upper_copies(r) + far_copies(r):
        copy.start()
    table_stage(r)
    for copy in upper_copies(r):
        copy.wait()
    frame_stage(r)
    bottom_copy(r).start()
    for copy in near_copies(r):
        copy.wait()


def table_stage(r):
    chosen = r.chosen[...].astype(BF16)
    table = None
    for part in pieces_of(r.stiffness[...], 3):
        one = mul(chosen, part)
        table = one if table is None else table + one
    whole = None
    for part in pieces_of(table, 3):
        one = lax.dot_general(part, chosen, (((1,), (1,)), ((), ())), preferred_element_type=F32)
        whole = one if whole is None else whole + one
    high, low = pieces_of(whole, 2)
    r.stiff[...] = jnp.concatenate(
        [
            jnp.concatenate([high, high], axis=1),
            jnp.concatenate([low, jnp.zeros_like(low)], axis=1),
        ],
        axis=0,
    )


def mix(get):
    return 3.0 * get(2) + 2.0 * (get(1) + get(3)) + (get(0) + get(4))


def taps_stage(r, planes):
    role = lax.axis_index("role")
    band = hat_of(column_z(role, (LANES, 256), 1) - iota((LANES, 256), 0)).astype(BF16)
    bands = jnp.concatenate([band, band], axis=0)
    far = lax.rem(iota((16, 256), 0), 8)
    spot = jnp.where(role == 0, LANES + far, far - 4)
    rim = hat_of(column_z(role, (16, 256), 1) - spot)
    rim = jnp.where(far < 4, rim, 0.0).astype(BF16)

    def plane(p, rows):
        ref = (r.lo, r.design, r.hi)[p // 4]
        return ref[p % 4, rows]

    for i in planes:
        beyond = mix(lambda k: r.edges[(i + k) // 4, :, 256 * ((i + k) % 4) : 256 * ((i + k) % 4) + 256])
        beyond = jnp.concatenate(pieces_of(beyond, 2), axis=0)
        beyond = lax.dot_general(beyond, rim, (((0,), (0,)), ((), ())), preferred_element_type=F32)
        for b in range(4):
            rows = slice(64 * b, 64 * b + 64)
            wide = mix(lambda k: plane(i + k, rows))
            out = mul(jnp.concatenate(pieces_of(wide, 2), axis=1), bands)
            r.zc[i, 8 + 64 * b : 72 + 64 * b] = out + beyond[rows]
        r.zc[i, 0:8] = jnp.zeros((8, 256), F32)
        r.zc[i, 264:272] = jnp.zeros((8, 256), F32)


def bend_stage(r, count, plane_of, shown):
    role, gx, gy = place_of()
    slab = gx * 8 + gy
    z_places = column_z(role, (1, 256), 1) + role * LANES
    by_z = 1.0 / reach(z_places, 256)

    def body(step, _):
        i = plane_of(step)
        x = 4 * slab + i - 2
        inside = jnp.logical_and(x >= 0, x < 256)
        by_x = 1.0 / reach(jnp.full((1, 256), x, I32), 256)
        by_xz = by_z * by_x
        for b in range(8):
            first = 32 * b
            by = by_xz / reach(iota((32, 256), 0) + first, 256)
            total = mix(lambda k: r.zc[i, 6 + k + first : 38 + k + first])
            bent = jnp.tanh(sharpness * (total * by - threshold))
            r.m[i, first : first + 32] = jnp.where(inside, (1.0 - bent * bent) * (by * (sharpness / FULL)), 0.0)
            if shown:
                r.psum[first : first + 32] += (BEND + bent[:, :LANES]) * (1.0 / FULL)
        return 0

    lax.fori_loop(0, count, body, 0)


def inner_stage(r):
    role, gx, gy = place_of()
    slab = gx * 8 + gy

    @pl.when(slab == 0)
    def _():
        r.lo[2:4] = jnp.zeros((2, 256, LANES), F32)
        r.edges[0] = jnp.zeros((8, 1024), F32)

    @pl.when(slab == 63)
    def _():
        r.hi[0:2] = jnp.zeros((2, 256, LANES), F32)
        r.edges[2] = jnp.zeros((8, 1024), F32)

    taps_stage(r, (2, 3, 4, 5))
    r.psum[...] = jnp.zeros_like(r.psum)
    bend_stage(r, 4, lambda step: step + 2, True)
    density_stage(r)


def outer_stage(r):
    role, gx, gy = place_of()
    slab = gx * 8 + gy
    for copy in far_copies(r):
        copy.wait()

    @pl.when(slab == 0)
    def _():
        r.lo[0:2] = jnp.zeros((2, 256, LANES), F32)

    @pl.when(slab == 63)
    def _():
        r.hi[2:4] = jnp.zeros((2, 256, LANES), F32)

    taps_stage(r, (0, 1, 6, 7))
    bend_stage(r, 4, lambda step: jnp.where(step < 2, step, step + 4), False)


def density_stage(r):
    rows, cols = iota((LANES, 256), 0), iota((LANES, 256), 1)
    sub = lax.rem(rows, 8)
    wanted = 8 * lax.div(lax.rem(rows, 64), 8) + 4 * lax.div(rows, 64) + sub
    gather = jnp.logical_and(sub < 4, lax.div(cols, 4) == wanted).astype(F32).astype(BF16)
    parts = pieces_of(r.psum[...], 3)
    by_rows = mul(gather, parts[0]) + mul(gather, parts[1]) + mul(gather, parts[2])
    by_rows = jnp.concatenate([by_rows[:64], by_rows[64:]], axis=1)
    rows, cols = iota((256, LANES), 0), iota((256, LANES), 1)
    merge = (cols == 64 * lax.div(rows, LANES) + lax.div(lax.rem(rows, LANES), 2)).astype(F32).astype(BF16)
    parts = pieces_of(by_rows, 3)
    density = (mul(parts[0], merge) + mul(parts[1], merge) + mul(parts[2], merge)) * (1.0 / 32.0)
    for k in range(GYN):
        r.dens[k] = density[8 * k : 8 * k + 8]


def pack_stage(r):
    matrix = parity_matrix()
    r.vf[...] = jnp.zeros_like(r.vf)
    for q in range(3):
        wide = jnp.concatenate(
            [r.force[q, :, 8 * h : 8 * h + 8].reshape(LANES, LANES) for h in range(2)], axis=1
        )
        force = None
        for part in pieces_of(wide, 3):
            one = mul(part, matrix)
            force = one if force is None else force + one
        wide = jnp.concatenate(
            [r.mask[q, :, 8 * h : 8 * h + 8].reshape(LANES, LANES) for h in range(2)], axis=1
        )
        free = mul((1 - wide).astype(F32).astype(BF16), matrix)
        force = force * free
        for x in range(16):
            for half in range(2):
                for kind, values in ((0, force), (1, free)):
                    r.vf[kind, x // 2, x % 2, pl.ds(4 * half + q, 8, stride=8)] = values[
                        8 * x : 8 * x + 8, LANES * half : LANES * half + LANES
                    ]


def density_copies(r):
    role, gx, gy = place_of()
    copies = []
    for k in range(1, GYN):
        target = lax.rem(gy + k, GYN)
        copies.append(remote(r.dens.at[target], r.dall.at[gy], r.nsend.at[k], r.nrecv.at[k], device_at(0, k)))
    return copies


def upper_copies(r):
    return [
        remote(r.vf.at[:, 0, 0], r.nxhi, r.nsend.at[8], r.nrecv.at[8], device_at(-1, 0)),
        remote(r.vf.at[:, :, :, 0:8], r.nyhi, r.nsend.at[9], r.nrecv.at[9], device_at(0, -1)),
        remote(r.vf.at[:, 0, 0, 0:8], r.ncorner, r.nsend.at[10], r.nrecv.at[10], device_at(-1, -1)),
    ]


def bottom_copy(r):
    return remote(r.bottom, r.nbottom, r.nsend.at[11], r.nrecv.at[11], device_at(0, 0, True))


def spread_stage(r):
    gy = lax.axis_index("gy")
    for copy in density_copies(r):
        copy.start()
    r.dall[gy] = r.dens[gy]


def low_lanes():
    return iota((8, LANES), 1) < 64


def frame_stage(r):
    role, gx, gy = place_of()
    has_x, has_y = gx < GXN - 1, gy < GYN - 1
    has_both = jnp.logical_and(has_x, has_y)
    low = low_lanes()

    def upper(beyond, own):
        return pltpu.roll(jnp.where(low, beyond, own), 64, 1)

    for kind, ref in ((0, r.r0), (1, r.free)):
        for e in range(8):
            for px in range(2):
                ref[e, px, 0:64] = r.vf[kind, e, px]
                ref[e, px, 64:72] = upper(jnp.where(has_y, r.nyhi[kind, e, px], 0.0), r.vf[kind, e, px, 0:8])
                ref[e, px, 72:80] = jnp.zeros((8, LANES), F32)
        beside = jnp.where(has_x, r.nxhi[kind], 0.0)
        ref[8, 0, 0:64] = beside
        ref[8, 0, 64:72] = upper(jnp.where(has_both, r.ncorner[kind], 0.0), beside[0:8])
        ref[8, 0, 72:80] = jnp.zeros((8, LANES), F32)
        ref[8, 1] = jnp.zeros((80, LANES), F32)
        pack_bottom(ref, r.bottom.at[kind])


def pack_bottom(field, out):
    sub, lane = iota((8, LANES), 0) < 4, lax.rem(iota((8, LANES), 1), 64)

    def body(e, _):
        for px in range(2):
            tile = jnp.zeros((8, LANES), F32)
            for j in range(LAST):
                held = field[e, px, 8 * j : 8 * j + 8]
                held = pltpu.roll(held, j, 1) if j else held
                tile = jnp.where(lane == j, held, tile)
            out[2 * e + px] = jnp.where(sub, tile, 0.0)
        return 0

    lax.fori_loop(0, 9, body, 0)


def add_bottom(field, tiles):
    keep = jnp.logical_and(iota((8, LANES), 0) < 4, lax.rem(iota((8, LANES), 1), 64) == 0)

    def body(e, _):
        for px in range(2):
            tile = tiles[2 * e + px]
            for j in range(LAST):
                moved = pltpu.roll(tile, LANES - j, 1) if j else tile
                field[e, px, 8 * j : 8 * j + 8] += jnp.where(keep, moved, 0.0)
        return 0

    lax.fori_loop(0, 9, body, 0)


def top_stage(r):
    role = lax.axis_index("role")
    bottom_copy(r).wait()
    for kind, ref in ((0, r.r0t), (1, r.freet)):
        ref[...] = jnp.where(role == 0, r.nbottom[kind], 0.0)
    for copy in density_copies(r):
        copy.wait()


def build_store(field, top, store):
    sub = iota((8, LANES), 0) < 4
    inside = lax.rem(iota((8, LANES), 1), 64) < 63

    def body(e, _):
        tops = [top[2 * e], top[2 * e + 1]]
        for f in range(5):
            held = [at(field, e, f, k) for k in range(4)]
            shifted = []
            for k in range(4):
                above = pltpu.roll(tops[k // 2], 63 - 2 * f - k % 2, 1)
                shifted.append(jnp.where(inside, pltpu.roll(held[k], LANES - 1, 1), above))
            turned = [None] + [pltpu.roll(v, 4, 0) for v in shifted[1:]]
            for k in range(4):
                store[e, f, k] = held[k]
            store[e, f, 4] = jnp.where(sub, shifted[0], turned[1])
            store[e, f, 5] = jnp.where(sub, shifted[2], turned[3])
            store[e, f, 6] = jnp.where(sub, shifted[0], turned[2])
        return 0

    lax.fori_loop(0, 9, body, 0)


def element_product(store, stiff, e):
    columns = []
    for f in range(4):
        columns.append(jnp.concatenate([store[e + dx, f + dy, kind] for dx, dy, kind in CHUNKS], axis=0))
    wide = jnp.concatenate(columns, axis=1)
    out = mul(stiff, jnp.concatenate(pieces_of(wide, 2), axis=0))
    product = out[:ROWS] + out[ROWS:]
    return columns, [product[:, f * LANES : (f + 1) * LANES] for f in range(4)]


def chunk_sum(left, right):
    both = left * right
    total = both[:8]
    for k in range(1, len(CHUNKS)):
        total = total + both[8 * k : 8 * k + 8]
    return total


def factor_of(rho):
    return floor_stiff + (1.0 - floor_stiff) * (rho * rho * rho)


def apply_operator(r, image, top):
    store, acc = r.store, r.acc
    acc[...] = jnp.zeros_like(acc)
    stiff = r.stiff[...]

    def body(e, energy):
        columns, products = element_product(store, stiff, e)
        factor = factor_of(r.rho[e])
        for f in range(4):
            scaled = products[f] * factor[f : f + 1, :]
            energy = energy + chunk_sum(columns[f], scaled)
            for place, (dx, dy, kind) in enumerate(CHUNKS):
                acc[e + dx, f + dy, kind] += scaled[8 * place : 8 * place + 8]
        return energy

    energy = lax.fori_loop(0, 8, body, jnp.zeros((8, LANES), F32))
    sub, lane = iota((8, LANES), 0) < 4, lax.rem(iota((8, LANES), 1), 64)
    keep = jnp.logical_and(sub, lane > 0)

    def fold(e, _):
        tops = [jnp.zeros((8, LANES), F32), jnp.zeros((8, LANES), F32)]
        for f in range(5):
            z0, z1, z2 = acc[e, f, 4], acc[e, f, 5], acc[e, f, 6]
            t0, t1, t2 = (pltpu.roll(v, 4, 0) for v in (z0, z1, z2))
            for k, extra in enumerate((z0 + z2, t0, z1 + t2, t1)):
                first = 16 * f + 8 * (k % 2)
                image[e, k // 2, first : first + 8] = acc[e, f, k] + jnp.where(keep, pltpu.roll(extra, 1, 1), 0.0)
                j = 2 * f + k % 2
                if j < LAST:
                    tops[k // 2] = jnp.where(lane == j, pltpu.roll(extra, 65 + j, 1), tops[k // 2])
        for px in range(2):
            top[2 * e + px] = jnp.where(sub, tops[px], 0.0)
        return 0

    lax.fori_loop(0, 9, fold, 0)
    return energy


def element_energy(r):
    stiff = r.stiff[...]

    def body(e, energy):
        columns, products = element_product(r.store, stiff, e)
        factor = factor_of(r.rho[e])
        for f in range(4):
            energy = energy + chunk_sum(columns[f], products[f] * factor[f : f + 1, :])
        return energy

    return lax.fori_loop(0, 8, body, jnp.zeros((8, LANES), F32))


def square_sum(field):
    def body(e, total):
        for f in range(4):
            for k in range(4):
                held = at(field, e, f, k)
                total = total + held * held
        return total

    return lax.fori_loop(0, 8, body, jnp.zeros((8, LANES), F32))


def sums_tile(gamma, delta):
    gamma = jnp.sum(gamma, axis=0, keepdims=True)
    delta = jnp.sum(delta, axis=0, keepdims=True)
    gamma, delta = gamma + pltpu.roll(gamma, 64, 1), delta + pltpu.roll(delta, 64, 1)
    return jnp.where(iota((1, LANES), 1) < 64, gamma, delta)


def read_sums(sum_ref):
    held, low = sum_ref[...], iota((1, LANES), 1) < 64
    return (
        jnp.sum(jnp.where(low, held, 0.0), axis=1, keepdims=True),
        jnp.sum(jnp.where(low, 0.0, held), axis=1, keepdims=True),
    )


def over_nodes(body):
    def step(e, _):
        body(e)
        return 0

    lax.fori_loop(0, 9, step, 0)


def cross_device(shift):
    role, gx, gy = place_of()
    target = lax.rem(2 * gx + role + shift, 16)
    return {"role": lax.rem(target, 2), "gx": lax.div(target, 2), "gy": gy}


def reduce_start(r, n):
    gy = lax.axis_index("gy")
    mine, slots, send, recv = r["tile", n], r["slots", n], r["rsend", n], r["rrecv", n]
    slots[gy] = mine[...]
    for k in range(1, GYN):
        remote(mine, slots.at[gy], send.at[0], recv.at[0], device_at(0, k)).start()


def reduce_middle(r, n):
    role, gx, gy = place_of()
    slots, half, send, recv = r["slots", n], r["half", n], r["rsend", n], r["rrecv", n]
    remote(slots.at[0:7], slots.at[0:7], send.at[0], recv.at[0], device_at(0, 0, True)).wait()
    part = jnp.sum(slots[0:8], axis=0)
    half[...] = part
    place = 8 + 2 * gx + role
    slots[place] = part
    for k in range(1, 16):
        remote(half, slots.at[place], send.at[1], recv.at[1], cross_device(k)).start()


def reduce_end(r, n):
    slots, send, recv = r["slots", n], r["rsend", n], r["rrecv", n]
    remote(slots.at[8:23], slots.at[8:23], send.at[1], recv.at[1], device_at(0, 0, True)).wait()
    r["sum", n][...] = jnp.sum(slots[8:24], axis=0)


FACE_MOVES = ((1, 0), (-1, 0), (0, 1), (0, -1), (1, 1), (1, -1), (-1, 1), (-1, -1))


def face_copies(r, n):
    image, corners, top, rows = r["image", n], r["corners", n], r["imaget", n], r["trow", n]
    ends = (
        (image.at[8, 0], r["xlo", n]),
        (image.at[0, 0], r["xhi", n]),
        (image.at[:, :, 64:72], r["ylo", n]),
        (image.at[:, :, 0:8], r["yhi", n]),
        (image.at[8, 0, 64:72], corners.at[0]),
        (image.at[8, 0, 0:8], corners.at[1]),
        (image.at[0, 0, 64:72], corners.at[2]),
        (image.at[0, 0, 0:8], corners.at[3]),
    )
    tops = (top.at[16], top.at[0], rows.at[1], rows.at[0], rows.at[1], rows.at[0], rows.at[1], rows.at[0])
    send, recv = r["fsend", n], r["frecv", n]
    copies = []
    for k, ((dx, dy), (src, dst)) in enumerate(zip(FACE_MOVES, ends)):
        copies.append(remote(src, dst, send.at[k], recv.at[k], device_at(dx, dy)))
        copies.append(remote(tops[k], r["tface", n].at[k], send.at[8 + k], recv.at[8 + k], device_at(dx, dy)))
    return copies


def face_stage(r, n):
    role = lax.axis_index("role")
    image, top, lift = r["image", n], r["imaget", n], r["lift", n]
    reduce_start(r, n)

    @pl.when(role == 0)
    def _():
        lift[...] = top[...]

    @pl.when(role == 1)
    def _():
        pack_bottom(image, lift)

    across = remote(lift, r["lifted", n], r["zsend", n].at[0], r["zrecv", n].at[0], device_at(0, 0, True))
    across.start()
    reduce_middle(r, n)
    across.wait()

    @pl.when(role == 0)
    def _():
        top[...] += r["lifted", n][...]

    @pl.when(role == 1)
    def _():
        add_bottom(image, r["lifted", n])

    lane = iota((8, LANES), 1)
    below, above = jnp.zeros((8, LANES), F32), jnp.zeros((8, LANES), F32)
    for x in range(17):
        tile = top[x]
        below = jnp.where(lane == x, pltpu.roll(tile, x, 1) if x else tile, below)
        above = jnp.where(lane == x, pltpu.roll(tile, 56 + x, 1), above)
    r["trow", n][0] = below
    r["trow", n][1] = above
    copies = face_copies(r, n)
    for copy in copies:
        copy.start()
    reduce_end(r, n)
    for copy in copies:
        copy.wait()


def add_faces(r, n, work, workt):
    role, gx, gy = place_of()
    low_x, low_y = gx > 0, gy > 0
    image, corners, top, tface = r["image", n], r["corners", n], r["imaget", n], r["tface", n]
    xlo, xhi, ylo, yhi = (r[name, n] for name in ("xlo", "xhi", "ylo", "yhi"))
    low = low_lanes()

    def join(e, p, below, above):
        f0, f4 = work[e, p, 0:8], work[e, p, 64:72]
        below = jnp.where(low_y, below, 0.0)
        work[e, p, 0:8] = f0 + pltpu.roll(jnp.where(low, f4, below), 64, 1)
        work[e, p, 64:72] = f4 + pltpu.roll(jnp.where(low, above, f0), 64, 1)

    work[...] = image[...]
    work[0, 0] += jnp.where(low_x, xlo[...], 0.0)
    work[8, 0] += xhi[...]
    join(0, 0, ylo[0, 0] + jnp.where(low_x, corners[0], 0.0), yhi[0, 0] + jnp.where(low_x, corners[1], 0.0))
    join(8, 0, ylo[8, 0] + corners[2], yhi[8, 0] + corners[3])
    for e in range(8):
        for p in range(2):
            if e or p:
                join(e, p, ylo[e, p], yhi[e, p])
    work[...] = work[...] * r.free[...]

    lane = iota((8, LANES), 1)

    def row_of(face, first, last):
        first = jnp.where(low_x, first, 0.0)
        face = face + jnp.where(lane == 0, pltpu.roll(first, LANES - 16, 1), 0.0)
        return face + jnp.where(lane == 16, pltpu.roll(last, 16, 1), 0.0)

    below = jnp.where(low_y, row_of(tface[2], tface[4], tface[6]), 0.0)
    above = row_of(tface[3], tface[5], tface[7])
    for x in range(17):
        tile = top[x]
        if x == 0:
            tile = tile + jnp.where(low_x, tface[0], 0.0)
        if x == 16:
            tile = tile + tface[1]
        total = tile + jnp.where(lane == 64, pltpu.roll(tile, 56, 1), 0.0)
        total = total + jnp.where(lane == 8, pltpu.roll(tile, 72, 1), 0.0)
        total = total + jnp.where(lane == 0, pltpu.roll(below, LANES - x, 1) if x else below, 0.0)
        total = total + jnp.where(lane == 72, pltpu.roll(above, 72 - x, 1), 0.0)
        workt[x] = total * r.freet[x]
    workt[17] = jnp.zeros((8, LANES), F32)


def spare(value):
    return value.reshape(1, 1, 1)


def first_stage(r):
    for e in range(8):
        r.rho[e] = r.dall[e]
    build_store(r.r0, r.r0t, r.store)
    delta = apply_operator(r, r["image", 0], r["imaget", 0])
    r["tile", 0][...] = sums_tile(square_sum(r.r0), delta)


def second_stage(r):
    add_faces(r, 0, r.s0, r.s0t)
    gamma, delta = read_sums(r["sum", 0])
    alpha = spare(gamma / delta)

    def update(e):
        r.r1[e] = r.r0[e] - alpha * r.s0[e]

    over_nodes(update)
    r.r1t[...] = r.r0t[...] - alpha * r.s0t[...]
    build_store(r.r1, r.r1t, r.store)
    delta = apply_operator(r, r["image", 1], r["imaget", 1])
    r["tile", 1][...] = sums_tile(square_sum(r.r1), delta)


def third_stage(r):
    add_faces(r, 1, r.work, r.workt)
    gamma0, delta0 = read_sums(r["sum", 0])
    gamma1, delta1 = read_sums(r["sum", 1])
    alpha0 = gamma0 / delta0
    beta1 = gamma1 / gamma0
    alpha1 = gamma1 / (delta1 - beta1 * gamma1 / alpha0)
    alpha0, alpha1, beta1 = spare(alpha0), spare(alpha1), spare(beta1)

    def update(e):
        p = r.r1[e] + beta1 * r.r0[e]
        r.p1[e] = p
        r.u1[e] = alpha0 * r.r0[e] + alpha1 * p
        r.r2[e] = r.r1[e] - alpha1 * (r.work[e] + beta1 * r.s0[e])

    over_nodes(update)
    p = r.r1t[...] + beta1 * r.r0t[...]
    r.p1t[...] = p
    r.u1t[...] = alpha0 * r.r0t[...] + alpha1 * p
    r.r2t[...] = r.r1t[...] - alpha1 * (r.workt[...] + beta1 * r.s0t[...])
    build_store(r.r2, r.r2t, r.store)
    delta = element_energy(r)
    r["tile", 2][...] = sums_tile(square_sum(r.r2), delta)


def reduce_stage(r):
    reduce_start(r, 2)
    reduce_middle(r, 2)
    reduce_end(r, 2)


def last_stage(r):
    gamma0, delta0 = read_sums(r["sum", 0])
    gamma1, delta1 = read_sums(r["sum", 1])
    gamma2, delta2 = read_sums(r["sum", 2])
    alpha0 = gamma0 / delta0
    beta1 = gamma1 / gamma0
    alpha1 = gamma1 / (delta1 - beta1 * gamma1 / alpha0)
    beta2 = gamma2 / gamma1
    alpha2 = spare(gamma2 / (delta2 - beta2 * gamma2 / alpha1))
    beta2 = spare(beta2)

    def update(e):
        r.u[e] = r.u1[e] + alpha2 * (r.r2[e] + beta2 * r.p1[e])

    over_nodes(update)
    r.ut[...] = r.u1t[...] + alpha2 * (r.r2t[...] + beta2 * r.p1t[...])
    build_store(r.u, r.ut, r.store)
    stiff = r.stiff[...]
    rows = iota((8, LANES), 0)

    def body(e, before):
        columns, products = element_product(r.store, stiff, e)
        rho = r.rho[e]
        energy = jnp.zeros((8, LANES), F32)
        for f in range(4):
            one = jnp.sum(chunk_sum(columns[f], products[f]), axis=0, keepdims=True)
            energy = jnp.where(rows == f, one, energy)
        layer = (-3.0 * (1.0 - floor_stiff) / 32.0) * (rho * rho) * energy
        r.grad[e] = before + pltpu.roll(layer, 4, 0)
        return layer

    r.grad[8] = lax.fori_loop(0, 8, body, jnp.zeros((8, LANES), F32))
    role, lane = lax.axis_index("role"), lax.rem(iota((8, LANES), 1), 64)
    rim = jnp.zeros((8, LANES), F32)
    for k in range(9):
        held = r.grad[k]
        held = jnp.where(role == 0, pltpu.roll(held, k + 65, 1), pltpu.roll(held, k, 1) if k else held)
        rim = jnp.where(lane == k, held, rim)
    r.zgrad[...] = rim


def edge_targets():
    role, gx, gy = place_of()
    up, down = lax.rem(gx + 1, GXN), lax.rem(gx + GXN - 1, GXN)
    return [
        {"role": role, "gx": up, "gy": 0},
        {"role": role, "gx": down, "gy": 7},
        {"role": 1 - role, "gx": up, "gy": 0},
        {"role": 1 - role, "gx": down, "gy": 7},
    ]


def gradient_copies(r):
    gy = lax.axis_index("gy")
    copies = []
    for k in range(GYN):
        target = lax.rem(gy + k, GYN)
        if k:
            copies.append(
                remote(r.grad.at[pl.ds(target, 2)], r.gall.at[gy], r.gsend.at[k], r.grecv.at[k], device_at(0, k))
            )
        copies.append(
            remote(r.zgrad, r.zall.at[gy], r.gsend.at[8 + k], r.grecv.at[8 + k], device_at(0, k, True))
        )
    return copies


def rim_copies(r):
    gy = lax.axis_index("gy")
    up, down, up_z, down_z = edge_targets()
    return [
        remote(r.grad.at[8], r.grim.at[gy], r.esend.at[0], r.erecv.at[gy], up),
        remote(r.grad.at[0], r.grim.at[gy], r.esend.at[1], r.erecv.at[gy], down),
        remote(r.zgrad, r.zrim.at[gy], r.esend.at[2], r.erecv.at[8 + gy], up_z),
        remote(r.zgrad, r.zrim.at[gy], r.esend.at[3], r.erecv.at[8 + gy], down_z),
    ]


def gradient_stage(r):
    gy = lax.axis_index("gy")
    for copy in gradient_copies(r) + rim_copies(r):
        copy.start()
    r.gall[gy] = r.grad[pl.ds(gy, 2)]


def gradient_end(r):
    gy = lax.axis_index("gy")
    for copy in gradient_copies(r):
        copy.wait()
    for copy in rim_copies(r):
        copy.wait_send()

    @pl.when(jnp.logical_or(gy == 0, gy == 7))
    def _():
        for k in range(GYN):
            remote(r.zgrad, r.grim.at[k], r.esend.at[0], r.erecv.at[k], device_at(0, 0, True)).wait_recv()
            remote(r.zgrad, r.zrim.at[k], r.esend.at[0], r.erecv.at[8 + k], device_at(0, 0, True)).wait_recv()


def unpack_stage(r):
    back = parity_back()
    for q in range(3):
        even = [r.u[x // 2, x % 2, pl.ds(q, 8, stride=8)] for x in range(16)]
        odd = [r.u[x // 2, x % 2, pl.ds(4 + q, 8, stride=8)] for x in range(16)]
        wide = jnp.concatenate([jnp.concatenate(even, axis=0), jnp.concatenate(odd, axis=0)], axis=1)
        total = None
        for part in pieces_of(wide, 3):
            one = mul(part, back)
            total = one if total is None else total + one
        r.disp[q, :, 0:8] = total[:, :LANES].reshape(16, 8, LANES)
        r.disp[q, :, 8:16] = total[:, LANES:].reshape(16, 8, LANES)


def final_stage(r):
    role, gx, gy = place_of()
    for k in range(GYN):
        rows = slice(8 * k, 8 * k + 8)
        r.layers[0, rows] = r.gall[k, 0]
        r.layers[1, rows] = r.gall[k, 0]
        r.layers[2, rows] = r.gall[k, 1]
        for layer in range(3):
            r.zlayers[layer, rows] = r.zall[k]

    @pl.when(gy == 0)
    def _():
        for k in range(GYN):
            r.layers[0, 8 * k : 8 * k + 8] = r.grim[k]
            r.zlayers[0, 8 * k : 8 * k + 8] = r.zrim[k]

    @pl.when(gy == 7)
    def _():
        for k in range(GYN):
            r.layers[2, 8 * k : 8 * k + 8] = r.grim[k]
            r.zlayers[2, 8 * k : 8 * k + 8] = r.zrim[k]

    pairs = (jnp.where(gy == 0, 8, gy), gy, jnp.where(gy == 7, 0, gy + 1))
    rows, cols = iota((LANES, 256), 0), iota((LANES, 256), 1)
    fine, beyond = cols < LANES, jnp.logical_and(cols >= LANES, cols < LANES + 2)

    def twice(chosen):
        chosen = chosen.astype(F32).astype(BF16)
        return jnp.concatenate([chosen, chosen], axis=0)

    widen = [twice(jnp.logical_and(fine, rows == 64 * h + lax.div(cols, 2))) for h in range(2)]
    rows_y, cols_y = iota((256, LANES), 0), iota((256, LANES), 1)
    wanted = lax.div(rows_y, 4) - 8 * lax.div(lax.rem(cols_y, 64), 8) - 4 * lax.div(cols_y, 64)
    spot = lax.rem(cols_y, 8)
    for k in range(3):
        wide = []
        main = jnp.concatenate(pieces_of(r.layers[k], 2), axis=1)
        side = jnp.concatenate(pieces_of(r.zlayers[k], 2), axis=1)
        for h in range(2):
            reach_out = twice(jnp.logical_and(beyond, rows == 64 * h + pairs[k]))
            wide.append(mul(main, widen[h]) + mul(side, reach_out))
        wide = jnp.concatenate(wide, axis=0)
        first = 4 if k else 0
        inside = jnp.logical_and(spot >= first, spot < first + 4)
        repeat = jnp.logical_and(inside, wanted == spot - first).astype(F32).astype(BF16)
        repeat = jnp.concatenate([repeat, repeat], axis=1)
        r.wide[k] = mul(repeat, jnp.concatenate(pieces_of(wide, 2), axis=0))
    band = hat_of(iota((256, LANES), 1) - column_z(role, (256, LANES), 0)).astype(BF16)
    bands = jnp.concatenate([band, band], axis=0)
    for o in range(4):
        r.zc[o, 0:8] = jnp.zeros((8, 256), F32)
        r.zc[o, 264:272] = jnp.zeros((8, 256), F32)
        for b in range(8):
            spot = slice(32 * b, 32 * b + 32)
            total = None
            for layer, planes in ((0, (0, 1)), (1, (2, 3, 4, 5)), (2, (6, 7))):
                part = None
                for i in planes:
                    if o <= i <= o + 4:
                        one = HAT[i - o] * r.m[i, spot]
                        part = one if part is None else part + one
                if part is not None:
                    part = part * r.wide[layer, spot]
                    total = part if total is None else total + part
            r.zc[o, 8 + 32 * b : 40 + 32 * b] = total
        for b in range(8):
            first = 32 * b
            total = (
                3.0 * r.zc[o, 8 + first : 40 + first]
                + 2.0 * (r.zc[o, 7 + first : 39 + first] + r.zc[o, 9 + first : 41 + first])
                + (r.zc[o, 6 + first : 38 + first] + r.zc[o, 10 + first : 42 + first])
            )
            r.sens[o, first : first + 32] = mul(jnp.concatenate(pieces_of(total, 2), axis=1), bands)


FIELD = (9, 2, 80, LANES)
TILE = (1, LANES)
TOP = (18, 8, LANES)


class Refs(dict):
    def __getattr__(self, name):
        return self[name]


def buffers():
    shapes = {
        "edge": (8, 1024), "lo": (4, 256, LANES), "hi": (4, 256, LANES), "edges": (3, 8, 1024),
        "m": (8, 256, 256), "zc": (8, 272, 256), "psum": (256, LANES),
        "dens": (GYN, 8, LANES), "vf": (2, 8, 2, 64, LANES), "nxhi": (2, 64, LANES), "nyhi": (2, 8, 2, 8, LANES),
        "ncorner": (2, 8, LANES), "bottom": (2,) + TOP, "nbottom": (2,) + TOP, "dall": (GYN, 8, LANES),
        "rho": (8, 8, LANES), "store": (9, 5, 7, 8, LANES), "acc": (9, 5, 7, 8, LANES), "grad": (9, 8, LANES),
        "zgrad": (8, LANES), "gall": (GYN, 2, 8, LANES), "grim": (GYN, 8, LANES), "zall": (GYN, 8, LANES),
        "zrim": (GYN, 8, LANES), "layers": (3, 64, LANES), "zlayers": (3, 64, LANES), "wide": (3, 256, 256),
    }
    for name in ("r0", "free", "s0", "r1", "p1", "u1", "r2", "u", "work"):
        shapes[name] = FIELD
        shapes[name + "t"] = TOP
    for n in range(3):
        shapes["tile", n] = shapes["sum", n] = shapes["half", n] = TILE
        shapes["slots", n] = (24, 1, LANES)
    for n in range(2):
        shapes["image", n] = FIELD
        shapes["imaget", n] = shapes["lift", n] = shapes["lifted", n] = TOP
        shapes["trow", n] = (2, 8, LANES)
        shapes["tface", n] = (8, 8, LANES)
        shapes["xlo", n] = shapes["xhi", n] = (80, LANES)
        shapes["ylo", n] = shapes["yhi", n] = (9, 2, 8, LANES)
        shapes["corners", n] = (4, 8, LANES)
    scratch = {name: pltpu.VMEM(shape, F32) for name, shape in shapes.items()}
    scratch["stiff"] = pltpu.VMEM((2 * ROWS, 2 * ROWS), BF16)
    counts = {"dsend": 7, "drecv": 7, "nsend": 12, "nrecv": 12, "gsend": 16, "grecv": 16, "esend": 4, "erecv": 16}
    for n in range(3):
        counts["rsend", n] = counts["rrecv", n] = 2
        counts["fsend", n] = counts["frecv", n] = 16
        counts["zsend", n] = counts["zrecv", n] = 1
    for name, count in counts.items():
        scratch[name] = pltpu.SemaphoreType.DMA((count,))
    return scratch


def greet_all():
    gx, gy = lax.axis_index("gx"), lax.axis_index("gy")
    barrier = pltpu.get_barrier_semaphore()
    devices = [device_at(0, k) for k in range(1, GYN)]
    devices += [device_at(0, k, True) for k in range(1, GYN)]
    devices += [cross_device(k) for k in range(1, 16)]
    devices += [device_at(dx, dy) for dx, dy in FACE_MOVES[4:]]
    devices += [slab_device(shift, other) for shift, other in ((1, False), (-1, False), (1, True), (-1, True))]
    for device in devices:
        pl.semaphore_signal(barrier, inc=1, device_id=device, device_id_type=MESH)

    for last, dx in ((0, -1), (7, 1)):

        @pl.when(gy == last)
        def _():
            for k in range(GYN):
                for other in (False, True):
                    device = dict(device_at(dx, 0, other), gy=k)
                    pl.semaphore_signal(barrier, inc=1, device_id=device, device_id_type=MESH)

    return len(devices) + 4


def whole_kernel(names, *refs):
    r = Refs(zip(names, refs))
    count = greet_all()
    edge_stage(r)
    pack_stage(r)
    pl.semaphore_wait(pltpu.get_barrier_semaphore(), count)
    swap_stage(r)
    inner_stage(r)
    spread_stage(r)
    outer_stage(r)
    top_stage(r)
    first_stage(r)
    face_stage(r, 0)
    second_stage(r)
    face_stage(r, 1)
    third_stage(r)
    reduce_stage(r)
    last_stage(r)
    gradient_stage(r)
    unpack_stage(r)
    gradient_end(r)
    final_stage(r)


def on_device(design, force, clamped_dof_mask, stiffness):
    chosen = jnp.asarray(row_table())
    scratch = buffers()
    names = ["design", "force", "mask", "stiffness", "chosen", "sens", "disp"] + list(scratch)
    vmem = pl.BlockSpec(memory_space=pltpu.VMEM)
    return pl.pallas_call(
        functools.partial(whole_kernel, names),
        out_shape=(
            jax.ShapeDtypeStruct((4, 256, LANES), F32),
            jax.ShapeDtypeStruct((3, 16, 16, LANES), F32),
        ),
        in_specs=[vmem] * 5,
        out_specs=(vmem, vmem),
        scratch_shapes=list(scratch.values()),
        compiler_params=pltpu.CompilerParams(
            collective_id=0, has_side_effects=True, vmem_limit_bytes=36 * 1024 * 1024
        ),
        name="compliance",
    )(design, force, clamped_dof_mask, stiffness, chosen)


def solution(mesh):
    fine = P(("gx", "gy"), None, "role")
    nodes = P(None, "gx", "gy", "role")
    return jax.shard_map(
        on_device, mesh=mesh, in_specs=(fine, nodes, nodes, P()), out_specs=(fine, nodes), check_vma=False
    )
```

```python
import functools
import math

import jax
import jax.numpy as jnp
import numpy as np
from jax import lax
from jax.experimental import pallas as pl
from jax.experimental.pallas import tpu as pltpu
from jax.sharding import PartitionSpec as P

sharpness = 4.0
threshold = 0.5
floor_stiff = 0.001
BEND = math.tanh(sharpness * threshold)
FULL = math.tanh(sharpness * threshold) + math.tanh(sharpness * (1.0 - threshold))
HAT = (1.0, 2.0, 3.0, 2.0, 1.0)

MESH = pl.DeviceIdType.MESH
F32 = jnp.float32
BF16 = jnp.bfloat16
I32 = jnp.int32
ROWS = 112
LANES = 128
GXN = 8
GYN = 8
LAST = 9
CHUNKS = (
    (0, 0, 0), (0, 0, 1), (0, 0, 2), (0, 0, 3), (0, 0, 4), (0, 0, 5),
    (1, 0, 0), (1, 0, 1), (1, 0, 4),
    (0, 1, 0), (0, 1, 2), (0, 1, 6),
    (1, 1, 0), (1, 1, 4),
)
PAIRS = {4: ((0, 0), (0, 1)), 5: ((1, 0), (1, 1)), 6: ((0, 0), (1, 0))}


def row_table():
    table = np.zeros((ROWS, 81), np.float32)
    seen = set()
    for place, (dx, dy, kind) in enumerate(CHUNKS):
        for half in range(2):
            if kind < 4:
                px, py, c = kind // 2, kind % 2, half
            else:
                (px, py), c = PAIRS[kind][half], 2
            if (dx and px) or (dy and py):
                continue
            a, b = px + 2 * dx, py + 2 * dy
            for q in range(3):
                index = ((c * 3 + b) * 3 + a) * 3 + q
                assert index not in seen
                seen.add(index)
                table[place * 8 + half * 4 + q, index] = 1.0
    assert len(seen) == 81
    return table


def place_of():
    return lax.axis_index("role"), lax.axis_index("gx"), lax.axis_index("gy")


def device_at(dx, dy, other=False):
    role, gx, gy = place_of()
    return {
        "role": (1 - role) if other else role,
        "gx": lax.rem(gx + dx + GXN, GXN),
        "gy": lax.rem(gy + dy + GYN, GYN),
    }


def remote(src, dst, send, recv, device):
    return pltpu.make_async_remote_copy(
        src_ref=src, dst_ref=dst, send_sem=send, recv_sem=recv, device_id=device, device_id_type=MESH
    )


def iota(shape, dim):
    return lax.broadcasted_iota(I32, shape, dim)


def pieces_of(values, count):
    parts = []
    for _ in range(count):
        part = values.astype(BF16)
        parts.append(part)
        values = values - part.astype(F32)
    return parts


def slab_of(shift):
    role, gx, gy = place_of()
    slab = lax.rem(gx * 8 + gy + shift + 64, 64)
    return lax.div(slab, 8), lax.rem(slab, 8)


def slab_device(shift, other):
    role = lax.axis_index("role")
    gx, gy = slab_of(shift)
    return {"role": (1 - role) if other else role, "gx": gx, "gy": gy}


def reach(places, extent):
    total = jnp.zeros(places.shape, F32)
    for k, weight in enumerate(HAT):
        target = places + (k - 2)
        total = total + jnp.where(jnp.logical_and(target >= 0, target < extent), weight, 0.0)
    return jnp.maximum(total, 1.0)


def column_z(role, shape, dim):
    lane = iota(shape, dim)
    beyond = lane - LANES + jnp.where(role == 0, LANES, -2)
    return jnp.where(lane < LANES, lane, jnp.where(lane < LANES + 2, beyond, -4096))


def hat_of(distance):
    return jnp.maximum(3 - jnp.abs(distance), 0).astype(F32)


def at(field, e, f, kind):
    return field[e, kind // 2, 16 * f + 8 * (kind % 2) : 16 * f + 8 * (kind % 2) + 8]


def parity_matrix():
    rows, cols = iota((256, 256), 0), iota((256, 256), 1)
    return (rows == 2 * lax.rem(cols, LANES) + lax.div(cols, LANES)).astype(F32).astype(BF16)


def parity_back():
    rows, cols = iota((256, 256), 0), iota((256, 256), 1)
    return (cols == 2 * lax.rem(rows, LANES) + lax.div(rows, LANES)).astype(F32).astype(BF16)


def mul(left, right):
    return jnp.dot(left, right, preferred_element_type=F32)


def edge_stage(r):
    role = lax.axis_index("role")
    rows, cols = iota((16, LANES), 0), iota((16, LANES), 1)
    first = jnp.where(role == 0, 124, 0)
    for x in range(2):
        total = None
        for k in range(2):
            inside = jnp.logical_and(rows >= 4 * k, rows < 4 * k + 4)
            chosen = jnp.logical_and(cols == first + rows - 4 * k, inside).astype(F32).astype(BF16)
            for part in pieces_of(r.design[x + 2 * k], 2):
                one = lax.dot_general(chosen, part, (((1,), (1,)), ((), ())), preferred_element_type=F32)
                total = one if total is None else total + one
        r.edge[:, 256 * x : 256 * x + 256] = total[:8]


def near_copies(r):
    return [
        remote(r.design.at[2:4], r.lo.at[2:4], r.dsend.at[0], r.drecv.at[0], slab_device(1, False)),
        remote(r.design.at[0:2], r.hi.at[0:2], r.dsend.at[1], r.drecv.at[1], slab_device(-1, False)),
        remote(r.edge, r.edges.at[1], r.dsend.at[2], r.drecv.at[2], slab_device(0, True)),
        remote(r.edge, r.edges.at[0], r.dsend.at[3], r.drecv.at[3], slab_device(1, True)),
        remote(r.edge, r.edges.at[2], r.dsend.at[4], r.drecv.at[4], slab_device(-1, True)),
    ]


def far_copies(r):
    return [
        remote(r.design.at[0:2], r.lo.at[0:2], r.dsend.at[5], r.drecv.at[5], slab_device(1, False)),
        remote(r.design.at[2:4], r.hi.at[2:4], r.dsend.at[6], r.drecv.at[6], slab_device(-1, False)),
    ]


def swap_stage(r):
    for copy in near_copies(r) + upper_copies(r):
        copy.start()
    table_stage(r)
    for copy in upper_copies(r):
        copy.wait()
    frame_stage(r)
    bottom_copy(r).start()
    for copy in near_copies(r):
        copy.wait()


def table_stage(r):
    chosen = r.chosen[...].astype(BF16)
    table = None
    for part in pieces_of(r.stiffness[...], 3):
        one = mul(chosen, part)
        table = one if table is None else table + one
    whole = None
    for part in pieces_of(table, 3):
        one = lax.dot_general(part, chosen, (((1,), (1,)), ((), ())), preferred_element_type=F32)
        whole = one if whole is None else whole + one
    high, low = pieces_of(whole, 2)
    r.stiff[...] = jnp.concatenate(
        [
            jnp.concatenate([high, high], axis=1),
            jnp.concatenate([low, jnp.zeros_like(low)], axis=1),
        ],
        axis=0,
    )


def mix(get):
    return 3.0 * get(2) + 2.0 * (get(1) + get(3)) + (get(0) + get(4))


def taps_stage(r, planes):
    role = lax.axis_index("role")
    band = hat_of(column_z(role, (LANES, 256), 1) - iota((LANES, 256), 0)).astype(BF16)
    bands = jnp.concatenate([band, band], axis=0)
    far = lax.rem(iota((16, 256), 0), 8)
    spot = jnp.where(role == 0, LANES + far, far - 4)
    rim = hat_of(column_z(role, (16, 256), 1) - spot)
    rim = jnp.where(far < 4, rim, 0.0).astype(BF16)

    def plane(p, rows):
        ref = (r.lo, r.design, r.hi)[p // 4]
        return ref[p % 4, rows]

    def edge_plane(p):
        held = r.edges[p // 4, :, 256 * (p % 2) : 256 * (p % 2) + 256]
        return pltpu.roll(held, 4, 0) if p % 4 > 1 else held

    for i in planes:
        beyond = mix(lambda k: edge_plane(i + k))
        beyond = jnp.concatenate(pieces_of(beyond, 2), axis=0)
        beyond = lax.dot_general(beyond, rim, (((0,), (0,)), ((), ())), preferred_element_type=F32)
        for b in range(4):
            rows = slice(64 * b, 64 * b + 64)
            wide = mix(lambda k: plane(i + k, rows))
            out = mul(jnp.concatenate(pieces_of(wide, 2), axis=1), bands)
            r.zc[i, 8 + 64 * b : 72 + 64 * b] = out + beyond[rows]
        r.zc[i, 0:8] = jnp.zeros((8, 256), F32)
        r.zc[i, 264:272] = jnp.zeros((8, 256), F32)


def bend_stage(r, count, plane_of, shown):
    role, gx, gy = place_of()
    slab = gx * 8 + gy
    z_places = column_z(role, (1, 256), 1) + role * LANES
    by_z = 1.0 / reach(z_places, 256)

    def body(step, _):
        i = plane_of(step)
        x = 4 * slab + i - 2
        inside = jnp.logical_and(x >= 0, x < 256)
        by_x = 1.0 / reach(jnp.full((1, 256), x, I32), 256)
        by_xz = by_z * by_x
        for b in range(8):
            first = 32 * b
            by = by_xz / reach(iota((32, 256), 0) + first, 256)
            total = mix(lambda k: r.zc[i, 6 + k + first : 38 + k + first])
            bent = jnp.tanh(sharpness * (total * by - threshold))
            r.m[i, first : first + 32] = jnp.where(inside, (1.0 - bent * bent) * (by * (sharpness / FULL)), 0.0)
            if shown:
                r.psum[first : first + 32] += (BEND + bent[:, :LANES]) * (1.0 / FULL)
        return 0

    lax.fori_loop(0, count, body, 0)


def inner_stage(r):
    role, gx, gy = place_of()
    slab = gx * 8 + gy

    @pl.when(slab == 0)
    def _():
        r.lo[2:4] = jnp.zeros((2, 256, LANES), F32)
        r.edges[0] = jnp.zeros((8, 512), F32)

    @pl.when(slab == 63)
    def _():
        r.hi[0:2] = jnp.zeros((2, 256, LANES), F32)
        r.edges[2] = jnp.zeros((8, 512), F32)

    taps_stage(r, (2, 3, 4, 5))
    r.psum[...] = jnp.zeros_like(r.psum)
    bend_stage(r, 4, lambda step: step + 2, True)
    density_stage(r)


def outer_stage(r):
    role, gx, gy = place_of()
    slab = gx * 8 + gy
    for copy in far_copies(r):
        copy.wait()

    @pl.when(slab == 0)
    def _():
        r.lo[0:2] = jnp.zeros((2, 256, LANES), F32)

    @pl.when(slab == 63)
    def _():
        r.hi[2:4] = jnp.zeros((2, 256, LANES), F32)

    taps_stage(r, (0, 1, 6, 7))
    bend_stage(r, 4, lambda step: jnp.where(step < 2, step, step + 4), False)


def density_stage(r):
    rows, cols = iota((LANES, 256), 0), iota((LANES, 256), 1)
    sub = lax.rem(rows, 8)
    wanted = 8 * lax.div(lax.rem(rows, 64), 8) + 4 * lax.div(rows, 64) + sub
    gather = jnp.logical_and(sub < 4, lax.div(cols, 4) == wanted).astype(F32).astype(BF16)
    parts = pieces_of(r.psum[...], 3)
    by_rows = mul(gather, parts[0]) + mul(gather, parts[1]) + mul(gather, parts[2])
    by_rows = jnp.concatenate([by_rows[:64], by_rows[64:]], axis=1)
    rows, cols = iota((256, LANES), 0), iota((256, LANES), 1)
    merge = (cols == 64 * lax.div(rows, LANES) + lax.div(lax.rem(rows, LANES), 2)).astype(F32).astype(BF16)
    parts = pieces_of(by_rows, 3)
    density = (mul(parts[0], merge) + mul(parts[1], merge) + mul(parts[2], merge)) * (1.0 / 32.0)
    for k in range(GYN):
        r.dens[k] = density[8 * k : 8 * k + 8]


def pack_stage(r):
    matrix = parity_matrix()
    r.vf[...] = jnp.zeros_like(r.vf)
    for q in range(3):
        wide = jnp.concatenate(
            [r.force[q, :, 8 * h : 8 * h + 8].reshape(LANES, LANES) for h in range(2)], axis=1
        )
        force = None
        for part in pieces_of(wide, 3):
            one = mul(part, matrix)
            force = one if force is None else force + one
        wide = jnp.concatenate(
            [r.mask[q, :, 8 * h : 8 * h + 8].reshape(LANES, LANES) for h in range(2)], axis=1
        )
        free = mul((1 - wide).astype(F32).astype(BF16), matrix)
        force = force * free
        for x in range(16):
            for half in range(2):
                for kind, values in ((0, force), (1, free)):
                    r.vf[kind, x // 2, x % 2, pl.ds(4 * half + q, 8, stride=8)] = values[
                        8 * x : 8 * x + 8, LANES * half : LANES * half + LANES
                    ]


def density_copies(r):
    role, gx, gy = place_of()
    copies = []
    for k in range(1, GYN):
        target = lax.rem(gy + k, GYN)
        copies.append(remote(r.dens.at[target], r.dall.at[gy], r.nsend.at[k], r.nrecv.at[k], device_at(0, k)))
    return copies


def upper_copies(r):
    return [
        remote(r.vf.at[:, 0, 0], r.nxhi, r.nsend.at[8], r.nrecv.at[8], device_at(-1, 0)),
        remote(r.vf.at[:, :, :, 0:8], r.nyhi, r.nsend.at[9], r.nrecv.at[9], device_at(0, -1)),
        remote(r.vf.at[:, 0, 0, 0:8], r.ncorner, r.nsend.at[10], r.nrecv.at[10], device_at(-1, -1)),
    ]


def bottom_copy(r):
    return remote(r.packed, r.npacked, r.nsend.at[11], r.nrecv.at[11], device_at(0, 0, True))


def spread_stage(r):
    gy = lax.axis_index("gy")
    for copy in density_copies(r):
        copy.start()
    for copy in far_copies(r):
        copy.start()
    r.dall[gy] = r.dens[gy]


def low_lanes():
    return iota((8, LANES), 1) < 64


def frame_stage(r):
    role, gx, gy = place_of()
    has_x, has_y = gx < GXN - 1, gy < GYN - 1
    has_both = jnp.logical_and(has_x, has_y)
    low = low_lanes()

    def upper(beyond, own):
        return pltpu.roll(jnp.where(low, beyond, own), 64, 1)

    for kind, ref in ((0, r.r0), (1, r.free)):
        for e in range(8):
            for px in range(2):
                ref[e, px, 0:64] = r.vf[kind, e, px]
                ref[e, px, 64:72] = upper(jnp.where(has_y, r.nyhi[kind, e, px], 0.0), r.vf[kind, e, px, 0:8])
                ref[e, px, 72:80] = jnp.zeros((8, LANES), F32)
        beside = jnp.where(has_x, r.nxhi[kind], 0.0)
        ref[8, 0, 0:64] = beside
        ref[8, 0, 64:72] = upper(jnp.where(has_both, r.ncorner[kind], 0.0), beside[0:8])
        ref[8, 0, 72:80] = jnp.zeros((8, LANES), F32)
        ref[8, 1] = jnp.zeros((80, LANES), F32)
        pack_bottom(ref, r.bottom.at[kind])
    compress(lambda x: r.bottom[0, x] + pltpu.roll(r.bottom[1, x], 4, 0), r.packed)


def pack_bottom(field, out):
    sub, lane = iota((8, LANES), 0) < 4, lax.rem(iota((8, LANES), 1), 64)

    def body(e, _):
        for px in range(2):
            tile = jnp.zeros((8, LANES), F32)
            for j in range(LAST):
                held = field[e, px, 8 * j : 8 * j + 8]
                held = pltpu.roll(held, j, 1) if j else held
                tile = jnp.where(lane == j, held, tile)
            out[2 * e + px] = jnp.where(sub, tile, 0.0)
        return 0

    lax.fori_loop(0, 9, body, 0)


def compress(tiles, out):
    lane = lax.div(lax.rem(iota((8, LANES), 1), 64), 9)
    for group in range(3):
        total = jnp.zeros((8, LANES), F32)
        for m in range(7):
            x = 7 * group + m
            if x < 17:
                held = tiles(x)
                total = jnp.where(lane == m, pltpu.roll(held, 9 * m, 1) if m else held, total)
        out[group] = total


def expand(packed, x):
    held, m = packed[x // 7], x % 7
    held = pltpu.roll(held, LANES - 9 * m, 1) if m else held
    return jnp.where(lax.rem(iota((8, LANES), 1), 64) < 9, held, 0.0)


def add_bottom(field, tiles):
    keep = jnp.logical_and(iota((8, LANES), 0) < 4, lax.rem(iota((8, LANES), 1), 64) == 0)

    def body(e, _):
        for px in range(2):
            tile = tiles[2 * e + px]
            for j in range(LAST):
                moved = pltpu.roll(tile, LANES - j, 1) if j else tile
                field[e, px, 8 * j : 8 * j + 8] += jnp.where(keep, moved, 0.0)
        return 0

    lax.fori_loop(0, 9, body, 0)


def top_stage(r):
    role = lax.axis_index("role")
    bottom_copy(r).wait()
    keep = jnp.logical_and(iota((8, LANES), 0) < 4, role == 0)
    for x in range(17):
        held = expand(r.npacked, x)
        r.r0t[x] = jnp.where(keep, held, 0.0)
        r.freet[x] = jnp.where(keep, pltpu.roll(held, 4, 0), 0.0)
    r.r0t[17] = jnp.zeros((8, LANES), F32)
    r.freet[17] = jnp.zeros((8, LANES), F32)
    for copy in density_copies(r):
        copy.wait()


def build_store(field, top, store):
    sub = iota((8, LANES), 0) < 4
    inside = lax.rem(iota((8, LANES), 1), 64) < 63

    def body(e, _):
        tops = [top[2 * e], top[2 * e + 1]]
        for f in range(5):
            held = [at(field, e, f, k) for k in range(4)]
            shifted = []
            for k in range(4):
                above = pltpu.roll(tops[k // 2], 63 - 2 * f - k % 2, 1)
                shifted.append(jnp.where(inside, pltpu.roll(held[k], LANES - 1, 1), above))
            turned = [None] + [pltpu.roll(v, 4, 0) for v in shifted[1:]]
            for k in range(4):
                store[e, f, k] = held[k]
            store[e, f, 4] = jnp.where(sub, shifted[0], turned[1])
            store[e, f, 5] = jnp.where(sub, shifted[2], turned[3])
            store[e, f, 6] = jnp.where(sub, shifted[0], turned[2])
        return 0

    lax.fori_loop(0, 9, body, 0)


def element_product(store, stiff, e):
    columns = []
    for f in range(4):
        columns.append(jnp.concatenate([store[e + dx, f + dy, kind] for dx, dy, kind in CHUNKS], axis=0))
    wide = jnp.concatenate(columns, axis=1)
    out = mul(stiff, jnp.concatenate(pieces_of(wide, 2), axis=0))
    product = out[:ROWS] + out[ROWS:]
    return columns, [product[:, f * LANES : (f + 1) * LANES] for f in range(4)]


def chunk_sum(left, right):
    both = left * right
    total = both[:8]
    for k in range(1, len(CHUNKS)):
        total = total + both[8 * k : 8 * k + 8]
    return total


def factor_of(rho):
    return floor_stiff + (1.0 - floor_stiff) * (rho * rho * rho)


def apply_operator(r, n, gamma):
    image, top = r["image", n], r["imaget", n]
    store, acc = r.store, r.acc
    acc[...] = jnp.zeros_like(acc)
    stiff = r.stiff[...]

    def body(e, energy):
        columns, products = element_product(store, stiff, e)
        factor = factor_of(r.rho[e])
        for f in range(4):
            scaled = products[f] * factor[f : f + 1, :]
            energy = energy + chunk_sum(columns[f], scaled)
            for place, (dx, dy, kind) in enumerate(CHUNKS):
                acc[e + dx, f + dy, kind] += scaled[8 * place : 8 * place + 8]
        return energy

    energy = lax.fori_loop(0, 8, body, jnp.zeros((8, LANES), F32))
    r["tile", n][...] = sums_tile(gamma, energy)
    reduce_start(r, n)
    sub, lane = iota((8, LANES), 0) < 4, lax.rem(iota((8, LANES), 1), 64)
    keep = jnp.logical_and(sub, lane > 0)

    def fold(e, _):
        tops = [jnp.zeros((8, LANES), F32), jnp.zeros((8, LANES), F32)]
        for f in range(5):
            z0, z1, z2 = acc[e, f, 4], acc[e, f, 5], acc[e, f, 6]
            t0, t1, t2 = (pltpu.roll(v, 4, 0) for v in (z0, z1, z2))
            for k, extra in enumerate((z0 + z2, t0, z1 + t2, t1)):
                first = 16 * f + 8 * (k % 2)
                image[e, k // 2, first : first + 8] = acc[e, f, k] + jnp.where(keep, pltpu.roll(extra, 1, 1), 0.0)
                j = 2 * f + k % 2
                if j < LAST:
                    tops[k // 2] = jnp.where(lane == j, pltpu.roll(extra, 65 + j, 1), tops[k // 2])
        for px in range(2):
            top[2 * e + px] = jnp.where(sub, tops[px], 0.0)
        return 0

    lax.fori_loop(0, 9, fold, 0)


def element_energy(r):
    stiff = r.stiff[...]

    def body(e, energy):
        columns, products = element_product(r.store, stiff, e)
        factor = factor_of(r.rho[e])
        for f in range(4):
            energy = energy + chunk_sum(columns[f], products[f] * factor[f : f + 1, :])
        return energy

    return lax.fori_loop(0, 8, body, jnp.zeros((8, LANES), F32))


def square_sum(field):
    def body(e, total):
        for f in range(4):
            for k in range(4):
                held = at(field, e, f, k)
                total = total + held * held
        return total

    return lax.fori_loop(0, 8, body, jnp.zeros((8, LANES), F32))


def sums_tile(gamma, delta):
    gamma = jnp.sum(gamma, axis=0, keepdims=True)
    delta = jnp.sum(delta, axis=0, keepdims=True)
    gamma, delta = gamma + pltpu.roll(gamma, 64, 1), delta + pltpu.roll(delta, 64, 1)
    return jnp.where(iota((1, LANES), 1) < 64, gamma, delta)


def read_sums(sum_ref):
    held, low = sum_ref[...], iota((1, LANES), 1) < 64
    return (
        jnp.sum(jnp.where(low, held, 0.0), axis=1, keepdims=True),
        jnp.sum(jnp.where(low, 0.0, held), axis=1, keepdims=True),
    )


def over_nodes(body):
    def step(e, _):
        body(e)
        return 0

    lax.fori_loop(0, 9, step, 0)


def cross_device(shift):
    role, gx, gy = place_of()
    target = lax.rem(2 * gx + role + shift, 16)
    return {"role": lax.rem(target, 2), "gx": lax.div(target, 2), "gy": gy}


def reduce_start(r, n):
    gy = lax.axis_index("gy")
    mine, slots, send, recv = r["tile", n], r["slots", n], r["rsend", n], r["rrecv", n]
    slots[gy] = mine[...]
    for k in range(1, GYN):
        remote(mine, slots.at[gy], send.at[0], recv.at[0], device_at(0, k)).start()


def reduce_middle(r, n):
    role, gx, gy = place_of()
    slots, half, send, recv = r["slots", n], r["half", n], r["rsend", n], r["rrecv", n]
    remote(slots.at[0:7], slots.at[0:7], send.at[0], recv.at[0], device_at(0, 0, True)).wait()
    part = jnp.sum(slots[0:8], axis=0)
    half[...] = part
    place = 8 + 2 * gx + role
    slots[place] = part
    for k in range(1, 16):
        remote(half, slots.at[place], send.at[1], recv.at[1], cross_device(k)).start()


def reduce_end(r, n):
    slots, send, recv = r["slots", n], r["rsend", n], r["rrecv", n]
    remote(slots.at[8:23], slots.at[8:23], send.at[1], recv.at[1], device_at(0, 0, True)).wait()
    r["sum", n][...] = jnp.sum(slots[8:24], axis=0)


FACE_MOVES = ((1, 0), (-1, 0), (0, 1), (0, -1), (1, 1), (1, -1), (-1, 1), (-1, -1))


def face_copies(r, n):
    image, corners, top, rows = r["image", n], r["corners", n], r["imaget", n], r["trow", n]
    ends = (
        (image.at[8, 0], r["xlo", n]),
        (image.at[0, 0], r["xhi", n]),
        (image.at[:, :, 64:72], r["ylo", n]),
        (image.at[:, :, 0:8], r["yhi", n]),
        (image.at[8, 0, 64:72], corners.at[0]),
        (image.at[8, 0, 0:8], corners.at[1]),
        (image.at[0, 0, 64:72], corners.at[2]),
        (image.at[0, 0, 0:8], corners.at[3]),
    )
    tops = (top.at[16], top.at[0], rows.at[1], rows.at[0], rows.at[1], rows.at[0], rows.at[1], rows.at[0])
    send, recv = r["fsend", n], r["frecv", n]
    copies = []
    for k, ((dx, dy), (src, dst)) in enumerate(zip(FACE_MOVES, ends)):
        copies.append(remote(src, dst, send.at[k], recv.at[k], device_at(dx, dy)))
        copies.append(remote(tops[k], r["tface", n].at[k], send.at[8 + k], recv.at[8 + k], device_at(dx, dy)))
    return copies


def face_stage(r, n):
    role = lax.axis_index("role")
    image, top, lift = r["image", n], r["imaget", n], r["lift", n]

    @pl.when(role == 0)
    def _():
        lift[...] = top[...]

    @pl.when(role == 1)
    def _():
        pack_bottom(image, lift)

    compress(lambda x: lift[x], r["packed", n])
    across = remote(r["packed", n], r["lifted", n], r["zsend", n].at[0], r["zrecv", n].at[0], device_at(0, 0, True))
    across.start()
    reduce_middle(r, n)
    across.wait()

    for x in range(17):
        lift[x] = expand(r["lifted", n], x)
    lift[17] = jnp.zeros((8, LANES), F32)

    @pl.when(role == 0)
    def _():
        top[...] += lift[...]

    @pl.when(role == 1)
    def _():
        add_bottom(image, lift)

    lane = iota((8, LANES), 1)
    below, above = jnp.zeros((8, LANES), F32), jnp.zeros((8, LANES), F32)
    for x in range(17):
        tile = top[x]
        below = jnp.where(lane == x, pltpu.roll(tile, x, 1) if x else tile, below)
        above = jnp.where(lane == x, pltpu.roll(tile, 56 + x, 1), above)
    r["trow", n][0] = below
    r["trow", n][1] = above
    copies = face_copies(r, n)
    for copy in copies:
        copy.start()
    if n == 0:
        outer_stage(r)
    reduce_end(r, n)
    for copy in copies:
        copy.wait()


def add_faces(r, n, work, workt):
    role, gx, gy = place_of()
    low_x, low_y = gx > 0, gy > 0
    image, corners, top, tface = r["image", n], r["corners", n], r["imaget", n], r["tface", n]
    xlo, xhi, ylo, yhi = (r[name, n] for name in ("xlo", "xhi", "ylo", "yhi"))
    low = low_lanes()

    def join(e, p, below, above):
        f0, f4 = work[e, p, 0:8], work[e, p, 64:72]
        below = jnp.where(low_y, below, 0.0)
        work[e, p, 0:8] = f0 + pltpu.roll(jnp.where(low, f4, below), 64, 1)
        work[e, p, 64:72] = f4 + pltpu.roll(jnp.where(low, above, f0), 64, 1)

    work[...] = image[...]
    work[0, 0] += jnp.where(low_x, xlo[...], 0.0)
    work[8, 0] += xhi[...]
    join(0, 0, ylo[0, 0] + jnp.where(low_x, corners[0], 0.0), yhi[0, 0] + jnp.where(low_x, corners[1], 0.0))
    join(8, 0, ylo[8, 0] + corners[2], yhi[8, 0] + corners[3])
    for e in range(8):
        for p in range(2):
            if e or p:
                join(e, p, ylo[e, p], yhi[e, p])
    work[...] = work[...] * r.free[...]

    lane = iota((8, LANES), 1)

    def row_of(face, first, last):
        first = jnp.where(low_x, first, 0.0)
        face = face + jnp.where(lane == 0, pltpu.roll(first, LANES - 16, 1), 0.0)
        return face + jnp.where(lane == 16, pltpu.roll(last, 16, 1), 0.0)

    below = jnp.where(low_y, row_of(tface[2], tface[4], tface[6]), 0.0)
    above = row_of(tface[3], tface[5], tface[7])
    for x in range(17):
        tile = top[x]
        if x == 0:
            tile = tile + jnp.where(low_x, tface[0], 0.0)
        if x == 16:
            tile = tile + tface[1]
        total = tile + jnp.where(lane == 64, pltpu.roll(tile, 56, 1), 0.0)
        total = total + jnp.where(lane == 8, pltpu.roll(tile, 72, 1), 0.0)
        total = total + jnp.where(lane == 0, pltpu.roll(below, LANES - x, 1) if x else below, 0.0)
        total = total + jnp.where(lane == 72, pltpu.roll(above, 72 - x, 1), 0.0)
        workt[x] = total * r.freet[x]
    workt[17] = jnp.zeros((8, LANES), F32)


def spare(value):
    return value.reshape(1, 1, 1)


def first_stage(r):
    for e in range(8):
        r.rho[e] = r.dall[e]
    build_store(r.r0, r.r0t, r.store)
    apply_operator(r, 0, square_sum(r.r0))


def second_stage(r):
    add_faces(r, 0, r.s0, r.s0t)
    gamma, delta = read_sums(r["sum", 0])
    alpha = spare(gamma / delta)

    def update(e):
        r.r1[e] = r.r0[e] - alpha * r.s0[e]

    over_nodes(update)
    r.r1t[...] = r.r0t[...] - alpha * r.s0t[...]
    build_store(r.r1, r.r1t, r.store)
    apply_operator(r, 1, square_sum(r.r1))


def third_stage(r):
    add_faces(r, 1, r.work, r.workt)
    gamma0, delta0 = read_sums(r["sum", 0])
    gamma1, delta1 = read_sums(r["sum", 1])
    alpha0 = gamma0 / delta0
    beta1 = gamma1 / gamma0
    alpha1 = gamma1 / (delta1 - beta1 * gamma1 / alpha0)
    alpha0, alpha1, beta1 = spare(alpha0), spare(alpha1), spare(beta1)

    def update(e):
        p = r.r1[e] + beta1 * r.r0[e]
        r.p1[e] = p
        r.u1[e] = alpha0 * r.r0[e] + alpha1 * p
        r.r2[e] = r.r1[e] - alpha1 * (r.work[e] + beta1 * r.s0[e])

    over_nodes(update)
    p = r.r1t[...] + beta1 * r.r0t[...]
    r.p1t[...] = p
    r.u1t[...] = alpha0 * r.r0t[...] + alpha1 * p
    r.r2t[...] = r.r1t[...] - alpha1 * (r.workt[...] + beta1 * r.s0t[...])
    build_store(r.r2, r.r2t, r.store)
    delta = element_energy(r)
    r["tile", 2][...] = sums_tile(square_sum(r.r2), delta)


def reduce_stage(r):
    reduce_start(r, 2)
    reduce_middle(r, 2)
    reduce_end(r, 2)


def last_stage(r):
    gamma0, delta0 = read_sums(r["sum", 0])
    gamma1, delta1 = read_sums(r["sum", 1])
    gamma2, delta2 = read_sums(r["sum", 2])
    alpha0 = gamma0 / delta0
    beta1 = gamma1 / gamma0
    alpha1 = gamma1 / (delta1 - beta1 * gamma1 / alpha0)
    beta2 = gamma2 / gamma1
    alpha2 = spare(gamma2 / (delta2 - beta2 * gamma2 / alpha1))
    beta2 = spare(beta2)

    def update(e):
        r.u[e] = r.u1[e] + alpha2 * (r.r2[e] + beta2 * r.p1[e])

    over_nodes(update)
    r.ut[...] = r.u1t[...] + alpha2 * (r.r2t[...] + beta2 * r.p1t[...])
    build_store(r.u, r.ut, r.store)
    stiff = r.stiff[...]
    rows = iota((8, LANES), 0)

    def body(e, before):
        columns, products = element_product(r.store, stiff, e)
        rho = r.rho[e]
        energy = jnp.zeros((8, LANES), F32)
        for f in range(4):
            one = jnp.sum(chunk_sum(columns[f], products[f]), axis=0, keepdims=True)
            energy = jnp.where(rows == f, one, energy)
        layer = (-3.0 * (1.0 - floor_stiff) / 32.0) * (rho * rho) * energy
        r.grad[e] = before + pltpu.roll(layer, 4, 0)
        return layer

    r.grad[8] = lax.fori_loop(0, 8, body, jnp.zeros((8, LANES), F32))
    role, lane = lax.axis_index("role"), lax.rem(iota((8, LANES), 1), 64)
    rim = jnp.zeros((8, LANES), F32)
    for k in range(9):
        held = r.grad[k]
        held = jnp.where(role == 0, pltpu.roll(held, k + 65, 1), pltpu.roll(held, k, 1) if k else held)
        rim = jnp.where(lane == k, held, rim)
    r.zgrad[...] = rim


def edge_targets():
    role, gx, gy = place_of()
    up, down = lax.rem(gx + 1, GXN), lax.rem(gx + GXN - 1, GXN)
    return [
        {"role": role, "gx": up, "gy": 0},
        {"role": role, "gx": down, "gy": 7},
        {"role": 1 - role, "gx": up, "gy": 0},
        {"role": 1 - role, "gx": down, "gy": 7},
    ]


def gradient_copies(r):
    gy = lax.axis_index("gy")
    copies = []
    for k in range(GYN):
        target = lax.rem(gy + k, GYN)
        if k:
            copies.append(
                remote(r.grad.at[pl.ds(target, 2)], r.gall.at[gy], r.gsend.at[k], r.grecv.at[k], device_at(0, k))
            )
        copies.append(
            remote(r.zgrad, r.zall.at[gy], r.gsend.at[8 + k], r.grecv.at[8 + k], device_at(0, k, True))
        )
    return copies


def rim_copies(r):
    gy = lax.axis_index("gy")
    up, down, up_z, down_z = edge_targets()
    return [
        remote(r.grad.at[8], r.grim.at[gy], r.esend.at[0], r.erecv.at[gy], up),
        remote(r.grad.at[0], r.grim.at[gy], r.esend.at[1], r.erecv.at[gy], down),
        remote(r.zgrad, r.zrim.at[gy], r.esend.at[2], r.erecv.at[8 + gy], up_z),
        remote(r.zgrad, r.zrim.at[gy], r.esend.at[3], r.erecv.at[8 + gy], down_z),
    ]


def gradient_stage(r):
    gy = lax.axis_index("gy")
    for copy in gradient_copies(r) + rim_copies(r):
        copy.start()
    r.gall[gy] = r.grad[pl.ds(gy, 2)]


def gradient_end(r):
    gy = lax.axis_index("gy")
    for copy in gradient_copies(r):
        copy.wait()
    for copy in rim_copies(r):
        copy.wait_send()

    @pl.when(jnp.logical_or(gy == 0, gy == 7))
    def _():
        for k in range(GYN):
            remote(r.zgrad, r.grim.at[k], r.esend.at[0], r.erecv.at[k], device_at(0, 0, True)).wait_recv()
            remote(r.zgrad, r.zrim.at[k], r.esend.at[0], r.erecv.at[8 + k], device_at(0, 0, True)).wait_recv()


def unpack_stage(r):
    back = parity_back()
    for q in range(3):
        even = [r.u[x // 2, x % 2, pl.ds(q, 8, stride=8)] for x in range(16)]
        odd = [r.u[x // 2, x % 2, pl.ds(4 + q, 8, stride=8)] for x in range(16)]
        wide = jnp.concatenate([jnp.concatenate(even, axis=0), jnp.concatenate(odd, axis=0)], axis=1)
        total = None
        for part in pieces_of(wide, 3):
            one = mul(part, back)
            total = one if total is None else total + one
        r.disp[q, :, 0:8] = total[:, :LANES].reshape(16, 8, LANES)
        r.disp[q, :, 8:16] = total[:, LANES:].reshape(16, 8, LANES)


def final_stage(r):
    role, gx, gy = place_of()
    for k in range(GYN):
        rows = slice(8 * k, 8 * k + 8)
        r.layers[0, rows] = r.gall[k, 0]
        r.layers[1, rows] = r.gall[k, 0]
        r.layers[2, rows] = r.gall[k, 1]
        for layer in range(3):
            r.zlayers[layer, rows] = r.zall[k]

    @pl.when(gy == 0)
    def _():
        for k in range(GYN):
            r.layers[0, 8 * k : 8 * k + 8] = r.grim[k]
            r.zlayers[0, 8 * k : 8 * k + 8] = r.zrim[k]

    @pl.when(gy == 7)
    def _():
        for k in range(GYN):
            r.layers[2, 8 * k : 8 * k + 8] = r.grim[k]
            r.zlayers[2, 8 * k : 8 * k + 8] = r.zrim[k]

    pairs = (jnp.where(gy == 0, 8, gy), gy, jnp.where(gy == 7, 0, gy + 1))
    rows, cols = iota((LANES, 256), 0), iota((LANES, 256), 1)
    fine, beyond = cols < LANES, jnp.logical_and(cols >= LANES, cols < LANES + 2)

    def twice(chosen):
        chosen = chosen.astype(F32).astype(BF16)
        return jnp.concatenate([chosen, chosen], axis=0)

    widen = [twice(jnp.logical_and(fine, rows == 64 * h + lax.div(cols, 2))) for h in range(2)]
    rows_y, cols_y = iota((256, LANES), 0), iota((256, LANES), 1)
    wanted = lax.div(rows_y, 4) - 8 * lax.div(lax.rem(cols_y, 64), 8) - 4 * lax.div(cols_y, 64)
    spot = lax.rem(cols_y, 8)
    for k in range(3):
        wide = []
        main = jnp.concatenate(pieces_of(r.layers[k], 2), axis=1)
        side = jnp.concatenate(pieces_of(r.zlayers[k], 2), axis=1)
        for h in range(2):
            reach_out = twice(jnp.logical_and(beyond, rows == 64 * h + pairs[k]))
            wide.append(mul(main, widen[h]) + mul(side, reach_out))
        wide = jnp.concatenate(wide, axis=0)
        first = 4 if k else 0
        inside = jnp.logical_and(spot >= first, spot < first + 4)
        repeat = jnp.logical_and(inside, wanted == spot - first).astype(F32).astype(BF16)
        repeat = jnp.concatenate([repeat, repeat], axis=1)
        r.wide[k] = mul(repeat, jnp.concatenate(pieces_of(wide, 2), axis=0))
    band = hat_of(iota((256, LANES), 1) - column_z(role, (256, LANES), 0)).astype(BF16)
    bands = jnp.concatenate([band, band], axis=0)
    for o in range(4):
        r.zc[o, 0:8] = jnp.zeros((8, 256), F32)
        r.zc[o, 264:272] = jnp.zeros((8, 256), F32)
        for b in range(8):
            spot = slice(32 * b, 32 * b + 32)
            total = None
            for layer, planes in ((0, (0, 1)), (1, (2, 3, 4, 5)), (2, (6, 7))):
                part = None
                for i in planes:
                    if o <= i <= o + 4:
                        one = HAT[i - o] * r.m[i, spot]
                        part = one if part is None else part + one
                if part is not None:
                    part = part * r.wide[layer, spot]
                    total = part if total is None else total + part
            r.zc[o, 8 + 32 * b : 40 + 32 * b] = total
        for b in range(8):
            first = 32 * b
            total = (
                3.0 * r.zc[o, 8 + first : 40 + first]
                + 2.0 * (r.zc[o, 7 + first : 39 + first] + r.zc[o, 9 + first : 41 + first])
                + (r.zc[o, 6 + first : 38 + first] + r.zc[o, 10 + first : 42 + first])
            )
            r.sens[o, first : first + 32] = mul(jnp.concatenate(pieces_of(total, 2), axis=1), bands)


FIELD = (9, 2, 80, LANES)
TILE = (1, LANES)
TOP = (18, 8, LANES)


class Refs(dict):
    def __getattr__(self, name):
        return self[name]


def buffers():
    shapes = {
        "edge": (8, 512), "lo": (4, 256, LANES), "hi": (4, 256, LANES), "edges": (3, 8, 512),
        "m": (8, 256, 256), "zc": (8, 272, 256), "psum": (256, LANES),
        "dens": (GYN, 8, LANES), "vf": (2, 8, 2, 64, LANES), "nxhi": (2, 64, LANES), "nyhi": (2, 8, 2, 8, LANES),
        "ncorner": (2, 8, LANES), "bottom": (2,) + TOP, "packed": (3, 8, LANES), "npacked": (3, 8, LANES), "dall": (GYN, 8, LANES),
        "rho": (8, 8, LANES), "store": (9, 5, 7, 8, LANES), "acc": (9, 5, 7, 8, LANES), "grad": (9, 8, LANES),
        "zgrad": (8, LANES), "gall": (GYN, 2, 8, LANES), "grim": (GYN, 8, LANES), "zall": (GYN, 8, LANES),
        "zrim": (GYN, 8, LANES), "layers": (3, 64, LANES), "zlayers": (3, 64, LANES), "wide": (3, 256, 256),
    }
    for name in ("r0", "free", "s0", "r1", "p1", "u1", "r2", "u", "work"):
        shapes[name] = FIELD
        shapes[name + "t"] = TOP
    for n in range(3):
        shapes["tile", n] = shapes["sum", n] = shapes["half", n] = TILE
        shapes["slots", n] = (24, 1, LANES)
    for n in range(2):
        shapes["image", n] = FIELD
        shapes["imaget", n] = shapes["lift", n] = TOP
        shapes["packed", n] = shapes["lifted", n] = (3, 8, LANES)
        shapes["trow", n] = (2, 8, LANES)
        shapes["tface", n] = (8, 8, LANES)
        shapes["xlo", n] = shapes["xhi", n] = (80, LANES)
        shapes["ylo", n] = shapes["yhi", n] = (9, 2, 8, LANES)
        shapes["corners", n] = (4, 8, LANES)
    scratch = {name: pltpu.VMEM(shape, F32) for name, shape in shapes.items()}
    scratch["stiff"] = pltpu.VMEM((2 * ROWS, 2 * ROWS), BF16)
    counts = {"dsend": 7, "drecv": 7, "nsend": 12, "nrecv": 12, "gsend": 16, "grecv": 16, "esend": 4, "erecv": 16}
    for n in range(3):
        counts["rsend", n] = counts["rrecv", n] = 2
        counts["fsend", n] = counts["frecv", n] = 16
        counts["zsend", n] = counts["zrecv", n] = 1
    for name, count in counts.items():
        scratch[name] = pltpu.SemaphoreType.DMA((count,))
    return scratch


def greet_all():
    barrier = pltpu.get_barrier_semaphore()
    devices = [device_at(0, k) for k in range(1, GYN)]
    devices += [cross_device(k) for k in range(1, 16)]
    devices += [device_at(dx, dy) for dx, dy in FACE_MOVES[4:]]
    devices += [slab_device(shift, other) for shift, other in ((1, False), (-1, False), (1, True), (-1, True))]
    for device in devices:
        pl.semaphore_signal(barrier, inc=1, device_id=device, device_id_type=MESH)

    return len(devices)


def whole_kernel(names, *refs):
    r = Refs(zip(names, refs))
    count = greet_all()
    edge_stage(r)
    pack_stage(r)
    pl.semaphore_wait(pltpu.get_barrier_semaphore(), count)
    swap_stage(r)
    inner_stage(r)
    spread_stage(r)
    top_stage(r)
    first_stage(r)
    face_stage(r, 0)
    second_stage(r)
    face_stage(r, 1)
    third_stage(r)
    reduce_stage(r)
    last_stage(r)
    gradient_stage(r)
    unpack_stage(r)
    gradient_end(r)
    final_stage(r)


def on_device(design, force, clamped_dof_mask, stiffness):
    chosen = jnp.asarray(row_table())
    scratch = buffers()
    names = ["design", "force", "mask", "stiffness", "chosen", "sens", "disp"] + list(scratch)
    vmem = pl.BlockSpec(memory_space=pltpu.VMEM)
    return pl.pallas_call(
        functools.partial(whole_kernel, names),
        out_shape=(
            jax.ShapeDtypeStruct((4, 256, LANES), F32),
            jax.ShapeDtypeStruct((3, 16, 16, LANES), F32),
        ),
        in_specs=[vmem] * 5,
        out_specs=(vmem, vmem),
        scratch_shapes=list(scratch.values()),
        compiler_params=pltpu.CompilerParams(
            collective_id=0, has_side_effects=True, vmem_limit_bytes=36 * 1024 * 1024
        ),
        name="compliance",
    )(design, force, clamped_dof_mask, stiffness, chosen)


def solution(mesh):
    fine = P(("gx", "gy"), None, "role")
    nodes = P(None, "gx", "gy", "role")
    return jax.shard_map(
        on_device, mesh=mesh, in_specs=(fine, nodes, nodes, P()), out_specs=(fine, nodes), check_vma=False
    )
```

```python
import functools
import math

import jax
import jax.numpy as jnp
import numpy as np
from jax import lax
from jax.experimental import pallas as pl
from jax.experimental.pallas import tpu as pltpu
from jax.sharding import PartitionSpec as P

sharpness = 4.0
threshold = 0.5
floor_stiff = 0.001
BEND = math.tanh(sharpness * threshold)
FULL = math.tanh(sharpness * threshold) + math.tanh(sharpness * (1.0 - threshold))
HAT = (1.0, 2.0, 3.0, 2.0, 1.0)

MESH = pl.DeviceIdType.MESH
F32 = jnp.float32
BF16 = jnp.bfloat16
I32 = jnp.int32
ROWS = 112
LANES = 128
GXN = 8
GYN = 8
LAST = 9
CHUNKS = (
    (0, 0, 0), (0, 0, 1), (0, 0, 2), (0, 0, 3), (0, 0, 4), (0, 0, 5),
    (1, 0, 0), (1, 0, 1), (1, 0, 4),
    (0, 1, 0), (0, 1, 2), (0, 1, 6),
    (1, 1, 0), (1, 1, 4),
)
PAIRS = {4: ((0, 0), (0, 1)), 5: ((1, 0), (1, 1)), 6: ((0, 0), (1, 0))}


def row_table():
    table = np.zeros((ROWS, 81), np.float32)
    seen = set()
    for place, (dx, dy, kind) in enumerate(CHUNKS):
        for half in range(2):
            if kind < 4:
                px, py, c = kind // 2, kind % 2, half
            else:
                (px, py), c = PAIRS[kind][half], 2
            if (dx and px) or (dy and py):
                continue
            a, b = px + 2 * dx, py + 2 * dy
            for q in range(3):
                index = ((c * 3 + b) * 3 + a) * 3 + q
                assert index not in seen
                seen.add(index)
                table[place * 8 + half * 4 + q, index] = 1.0
    assert len(seen) == 81
    return table


def place_of():
    return lax.axis_index("role"), lax.axis_index("gx"), lax.axis_index("gy")


def device_at(dx, dy, other=False):
    role, gx, gy = place_of()
    return {
        "role": (1 - role) if other else role,
        "gx": lax.rem(gx + dx + GXN, GXN),
        "gy": lax.rem(gy + dy + GYN, GYN),
    }


def remote(src, dst, send, recv, device):
    return pltpu.make_async_remote_copy(
        src_ref=src, dst_ref=dst, send_sem=send, recv_sem=recv, device_id=device, device_id_type=MESH
    )


def iota(shape, dim):
    return lax.broadcasted_iota(I32, shape, dim)


def pieces_of(values, count):
    parts = []
    for _ in range(count):
        part = values.astype(BF16)
        parts.append(part)
        values = values - part.astype(F32)
    return parts


def slab_of(shift):
    role, gx, gy = place_of()
    slab = lax.rem(gx * 8 + gy + shift + 64, 64)
    return lax.div(slab, 8), lax.rem(slab, 8)


def slab_device(shift, other):
    role = lax.axis_index("role")
    gx, gy = slab_of(shift)
    return {"role": (1 - role) if other else role, "gx": gx, "gy": gy}


def reach(places, extent):
    total = jnp.zeros(places.shape, F32)
    for k, weight in enumerate(HAT):
        target = places + (k - 2)
        total = total + jnp.where(jnp.logical_and(target >= 0, target < extent), weight, 0.0)
    return jnp.maximum(total, 1.0)


def column_z(role, shape, dim):
    lane = iota(shape, dim)
    beyond = lane - LANES + jnp.where(role == 0, LANES, -2)
    return jnp.where(lane < LANES, lane, jnp.where(lane < LANES + 2, beyond, -4096))


def hat_of(distance):
    return jnp.maximum(3 - jnp.abs(distance), 0).astype(F32)


def at(field, e, f, kind):
    return field[e, kind // 2, 16 * f + 8 * (kind % 2) : 16 * f + 8 * (kind % 2) + 8]


def parity_matrix():
    rows, cols = iota((256, 256), 0), iota((256, 256), 1)
    return (rows == 2 * lax.rem(cols, LANES) + lax.div(cols, LANES)).astype(F32).astype(BF16)


def parity_back():
    rows, cols = iota((256, 256), 0), iota((256, 256), 1)
    return (cols == 2 * lax.rem(rows, LANES) + lax.div(rows, LANES)).astype(F32).astype(BF16)


def mul(left, right):
    return jnp.dot(left, right, preferred_element_type=F32)


def edge_stage(r):
    role = lax.axis_index("role")
    rows, cols = iota((16, LANES), 0), iota((16, LANES), 1)
    first = jnp.where(role == 0, 124, 0)
    for x in range(2):
        total = None
        for k in range(2):
            inside = jnp.logical_and(rows >= 4 * k, rows < 4 * k + 4)
            chosen = jnp.logical_and(cols == first + rows - 4 * k, inside).astype(F32).astype(BF16)
            for part in pieces_of(r.design[x + 2 * k], 2):
                one = lax.dot_general(chosen, part, (((1,), (1,)), ((), ())), preferred_element_type=F32)
                total = one if total is None else total + one
        r.edge[:, 256 * x : 256 * x + 256] = total[:8]


def near_copies(r):
    return [
        remote(r.design.at[2:4], r.lo.at[2:4], r.dsend.at[0], r.drecv.at[0], slab_device(1, False)),
        remote(r.design.at[0:2], r.hi.at[0:2], r.dsend.at[1], r.drecv.at[1], slab_device(-1, False)),
        remote(r.edge, r.edges.at[1], r.dsend.at[2], r.drecv.at[2], slab_device(0, True)),
        remote(r.edge, r.edges.at[0], r.dsend.at[3], r.drecv.at[3], slab_device(1, True)),
        remote(r.edge, r.edges.at[2], r.dsend.at[4], r.drecv.at[4], slab_device(-1, True)),
    ]


def far_copies(r):
    return [
        remote(r.design.at[0:2], r.lo.at[0:2], r.dsend.at[5], r.drecv.at[5], slab_device(1, False)),
        remote(r.design.at[2:4], r.hi.at[2:4], r.dsend.at[6], r.drecv.at[6], slab_device(-1, False)),
    ]


def swap_stage(r):
    for copy in near_copies(r) + upper_copies(r):
        copy.start()
    table_stage(r)
    for copy in upper_copies(r):
        copy.wait()
    frame_stage(r)
    bottom_copy(r).start()
    for copy in near_copies(r):
        copy.wait()


def table_stage(r):
    chosen = r.chosen[...].astype(BF16)
    table = None
    for part in pieces_of(r.stiffness[...], 3):
        one = mul(chosen, part)
        table = one if table is None else table + one
    whole = None
    for part in pieces_of(table, 3):
        one = lax.dot_general(part, chosen, (((1,), (1,)), ((), ())), preferred_element_type=F32)
        whole = one if whole is None else whole + one
    high, low = pieces_of(whole, 2)
    r.stiff[...] = jnp.concatenate(
        [
            jnp.concatenate([high, high], axis=1),
            jnp.concatenate([low, jnp.zeros_like(low)], axis=1),
        ],
        axis=0,
    )


def mix(get):
    return 3.0 * get(2) + 2.0 * (get(1) + get(3)) + (get(0) + get(4))


def taps_stage(r, planes):
    role = lax.axis_index("role")
    band = hat_of(column_z(role, (LANES, 256), 1) - iota((LANES, 256), 0)).astype(BF16)
    bands = jnp.concatenate([band, band], axis=0)
    far = lax.rem(iota((16, 256), 0), 8)
    spot = jnp.where(role == 0, LANES + far, far - 4)
    rim = hat_of(column_z(role, (16, 256), 1) - spot)
    rim = jnp.where(far < 4, rim, 0.0).astype(BF16)

    def plane(p, rows):
        ref = (r.lo, r.design, r.hi)[p // 4]
        return ref[p % 4, rows]

    def edge_plane(p):
        held = r.edges[p // 4, :, 256 * (p % 2) : 256 * (p % 2) + 256]
        return pltpu.roll(held, 4, 0) if p % 4 > 1 else held

    for i in planes:
        beyond = mix(lambda k: edge_plane(i + k))
        beyond = jnp.concatenate(pieces_of(beyond, 2), axis=0)
        beyond = lax.dot_general(beyond, rim, (((0,), (0,)), ((), ())), preferred_element_type=F32)
        for b in range(4):
            rows = slice(64 * b, 64 * b + 64)
            wide = mix(lambda k: plane(i + k, rows))
            out = mul(jnp.concatenate(pieces_of(wide, 2), axis=1), bands)
            r.zc[i, 8 + 64 * b : 72 + 64 * b] = out + beyond[rows]
        r.zc[i, 0:8] = jnp.zeros((8, 256), F32)
        r.zc[i, 264:272] = jnp.zeros((8, 256), F32)


def bend_stage(r, count, plane_of, shown):
    role, gx, gy = place_of()
    slab = gx * 8 + gy
    z_places = column_z(role, (1, 256), 1) + role * LANES
    by_z = 1.0 / reach(z_places, 256)

    def body(step, _):
        i = plane_of(step)
        x = 4 * slab + i - 2
        inside = jnp.logical_and(x >= 0, x < 256)
        by_x = 1.0 / reach(jnp.full((1, 256), x, I32), 256)
        by_xz = by_z * by_x
        for b in range(8):
            first = 32 * b
            by = by_xz / reach(iota((32, 256), 0) + first, 256)
            total = mix(lambda k: r.zc[i, 6 + k + first : 38 + k + first])
            bent = jnp.tanh(sharpness * (total * by - threshold))
            r.m[i, first : first + 32] = jnp.where(inside, (1.0 - bent * bent) * (by * (sharpness / FULL)), 0.0)
            if shown:
                r.psum[first : first + 32] += (BEND + bent[:, :LANES]) * (1.0 / FULL)
        return 0

    lax.fori_loop(0, count, body, 0)


def inner_stage(r):
    role, gx, gy = place_of()
    slab = gx * 8 + gy

    @pl.when(slab == 0)
    def _():
        r.lo[2:4] = jnp.zeros((2, 256, LANES), F32)
        r.edges[0] = jnp.zeros((8, 512), F32)

    @pl.when(slab == 63)
    def _():
        r.hi[0:2] = jnp.zeros((2, 256, LANES), F32)
        r.edges[2] = jnp.zeros((8, 512), F32)

    taps_stage(r, (2, 3, 4, 5))
    r.psum[...] = jnp.zeros_like(r.psum)
    bend_stage(r, 4, lambda step: step + 2, True)
    density_stage(r)


def outer_stage(r):
    role, gx, gy = place_of()
    slab = gx * 8 + gy
    for copy in far_copies(r):
        copy.wait()

    @pl.when(slab == 0)
    def _():
        r.lo[0:2] = jnp.zeros((2, 256, LANES), F32)

    @pl.when(slab == 63)
    def _():
        r.hi[2:4] = jnp.zeros((2, 256, LANES), F32)

    taps_stage(r, (0, 1, 6, 7))
    bend_stage(r, 4, lambda step: jnp.where(step < 2, step, step + 4), False)


def density_stage(r):
    rows, cols = iota((LANES, 256), 0), iota((LANES, 256), 1)
    sub = lax.rem(rows, 8)
    wanted = 8 * lax.div(lax.rem(rows, 64), 8) + 4 * lax.div(rows, 64) + sub
    gather = jnp.logical_and(sub < 4, lax.div(cols, 4) == wanted).astype(F32).astype(BF16)
    parts = pieces_of(r.psum[...], 3)
    by_rows = mul(gather, parts[0]) + mul(gather, parts[1]) + mul(gather, parts[2])
    by_rows = jnp.concatenate([by_rows[:64], by_rows[64:]], axis=1)
    rows, cols = iota((256, LANES), 0), iota((256, LANES), 1)
    merge = (cols == 64 * lax.div(rows, LANES) + lax.div(lax.rem(rows, LANES), 2)).astype(F32).astype(BF16)
    parts = pieces_of(by_rows, 3)
    density = (mul(parts[0], merge) + mul(parts[1], merge) + mul(parts[2], merge)) * (1.0 / 32.0)
    for k in range(GYN):
        r.dens[k] = density[8 * k : 8 * k + 8]


def pack_stage(r):
    matrix = parity_matrix()
    r.vf[...] = jnp.zeros_like(r.vf)
    for q in range(3):
        wide = jnp.concatenate(
            [r.force[q, :, 8 * h : 8 * h + 8].reshape(LANES, LANES) for h in range(2)], axis=1
        )
        force = None
        for part in pieces_of(wide, 3):
            one = mul(part, matrix)
            force = one if force is None else force + one
        wide = jnp.concatenate(
            [r.mask[q, :, 8 * h : 8 * h + 8].reshape(LANES, LANES) for h in range(2)], axis=1
        )
        free = mul((1 - wide).astype(F32).astype(BF16), matrix)
        force = force * free
        for x in range(16):
            for half in range(2):
                for kind, values in ((0, force), (1, free)):
                    r.vf[kind, x // 2, x % 2, pl.ds(4 * half + q, 8, stride=8)] = values[
                        8 * x : 8 * x + 8, LANES * half : LANES * half + LANES
                    ]


def density_copies(r):
    role, gx, gy = place_of()
    copies = []
    for k in range(1, GYN):
        target = lax.rem(gy + k, GYN)
        copies.append(remote(r.dens.at[target], r.dall.at[gy], r.nsend.at[k], r.nrecv.at[k], device_at(0, k)))
    return copies


def upper_copies(r):
    return [
        remote(r.vf.at[:, 0, 0], r.nxhi, r.nsend.at[8], r.nrecv.at[8], device_at(-1, 0)),
        remote(r.vf.at[:, :, :, 0:8], r.nyhi, r.nsend.at[9], r.nrecv.at[9], device_at(0, -1)),
        remote(r.vf.at[:, 0, 0, 0:8], r.ncorner, r.nsend.at[10], r.nrecv.at[10], device_at(-1, -1)),
    ]


def bottom_copy(r):
    return remote(r.packed, r.npacked, r.nsend.at[11], r.nrecv.at[11], device_at(0, 0, True))


def spread_stage(r):
    gy = lax.axis_index("gy")
    for copy in density_copies(r):
        copy.start()
    for copy in far_copies(r):
        copy.start()
    r.dall[gy] = r.dens[gy]


def low_lanes():
    return iota((8, LANES), 1) < 64


def frame_stage(r):
    role, gx, gy = place_of()
    has_x, has_y = gx < GXN - 1, gy < GYN - 1
    has_both = jnp.logical_and(has_x, has_y)
    low = low_lanes()

    def upper(beyond, own):
        return pltpu.roll(jnp.where(low, beyond, own), 64, 1)

    for kind, ref in ((0, r.r0), (1, r.free)):
        for e in range(8):
            for px in range(2):
                ref[e, px, 0:64] = r.vf[kind, e, px]
                ref[e, px, 64:72] = upper(jnp.where(has_y, r.nyhi[kind, e, px], 0.0), r.vf[kind, e, px, 0:8])
                ref[e, px, 72:80] = jnp.zeros((8, LANES), F32)
        beside = jnp.where(has_x, r.nxhi[kind], 0.0)
        ref[8, 0, 0:64] = beside
        ref[8, 0, 64:72] = upper(jnp.where(has_both, r.ncorner[kind], 0.0), beside[0:8])
        ref[8, 0, 72:80] = jnp.zeros((8, LANES), F32)
        ref[8, 1] = jnp.zeros((80, LANES), F32)
        pack_bottom(ref, r.bottom.at[kind])
    compress(lambda x: r.bottom[0, x] + pltpu.roll(r.bottom[1, x], 4, 0), r.packed)


def pack_bottom(field, out):
    sub, lane = iota((8, LANES), 0) < 4, lax.rem(iota((8, LANES), 1), 64)

    def body(e, _):
        for px in range(2):
            tile = jnp.zeros((8, LANES), F32)
            for j in range(LAST):
                held = field[e, px, 8 * j : 8 * j + 8]
                held = pltpu.roll(held, j, 1) if j else held
                tile = jnp.where(lane == j, held, tile)
            out[2 * e + px] = jnp.where(sub, tile, 0.0)
        return 0

    lax.fori_loop(0, 9, body, 0)


def compress(tiles, out):
    lane = lax.div(lax.rem(iota((8, LANES), 1), 64), 9)
    for group in range(3):
        total = jnp.zeros((8, LANES), F32)
        for m in range(7):
            x = 7 * group + m
            if x < 17:
                held = tiles(x)
                total = jnp.where(lane == m, pltpu.roll(held, 9 * m, 1) if m else held, total)
        out[group] = total


def expand(packed, x):
    held, m = packed[x // 7], x % 7
    held = pltpu.roll(held, LANES - 9 * m, 1) if m else held
    return jnp.where(lax.rem(iota((8, LANES), 1), 64) < 9, held, 0.0)


def set_bottom(field, tiles):
    keep = jnp.logical_and(iota((8, LANES), 0) < 4, lax.rem(iota((8, LANES), 1), 64) == 0)

    def body(e, _):
        for px in range(2):
            tile = tiles[2 * e + px]
            for j in range(LAST):
                moved = pltpu.roll(tile, LANES - j, 1) if j else tile
                spot = slice(8 * j, 8 * j + 8)
                field[e, px, spot] = jnp.where(keep, moved, field[e, px, spot])
        return 0

    lax.fori_loop(0, 9, body, 0)


def top_stage(r):
    role = lax.axis_index("role")
    bottom_copy(r).wait()
    keep = jnp.logical_and(iota((8, LANES), 0) < 4, role == 0)
    for x in range(17):
        held = expand(r.npacked, x)
        r.r0t[x] = jnp.where(keep, held, 0.0)
        r.freet[x] = jnp.where(keep, pltpu.roll(held, 4, 0), 0.0)
    r.r0t[17] = jnp.zeros((8, LANES), F32)
    r.freet[17] = jnp.zeros((8, LANES), F32)
    for copy in density_copies(r):
        copy.wait()


def build_store(field, top, store):
    sub = iota((8, LANES), 0) < 4
    inside = lax.rem(iota((8, LANES), 1), 64) < 63

    def body(e, _):
        tops = [top[2 * e], top[2 * e + 1]]
        for f in range(5):
            held = [at(field, e, f, k) for k in range(4)]
            shifted = []
            for k in range(4):
                above = pltpu.roll(tops[k // 2], 63 - 2 * f - k % 2, 1)
                shifted.append(jnp.where(inside, pltpu.roll(held[k], LANES - 1, 1), above))
            turned = [None] + [pltpu.roll(v, 4, 0) for v in shifted[1:]]
            for k in range(4):
                store[e, f, k] = held[k]
            store[e, f, 4] = jnp.where(sub, shifted[0], turned[1])
            store[e, f, 5] = jnp.where(sub, shifted[2], turned[3])
            store[e, f, 6] = jnp.where(sub, shifted[0], turned[2])
        return 0

    lax.fori_loop(0, 9, body, 0)


def element_product(store, stiff, e):
    columns = []
    for f in range(4):
        columns.append(jnp.concatenate([store[e + dx, f + dy, kind] for dx, dy, kind in CHUNKS], axis=0))
    wide = jnp.concatenate(columns, axis=1)
    out = mul(stiff, jnp.concatenate(pieces_of(wide, 2), axis=0))
    product = out[:ROWS] + out[ROWS:]
    return columns, [product[:, f * LANES : (f + 1) * LANES] for f in range(4)]


def chunk_sum(left, right):
    both = left * right
    total = both[:8]
    for k in range(1, len(CHUNKS)):
        total = total + both[8 * k : 8 * k + 8]
    return total


def factor_of(rho):
    return floor_stiff + (1.0 - floor_stiff) * (rho * rho * rho)


def apply_operator(r, n, gamma):
    image, top = r["image", n], r["imaget", n]
    store, acc = r.store, r.acc
    acc[...] = jnp.zeros_like(acc)
    stiff = r.stiff[...]

    def body(e, energy):
        columns, products = element_product(store, stiff, e)
        factor = factor_of(r.rho[e])
        for f in range(4):
            scaled = products[f] * factor[f : f + 1, :]
            energy = energy + chunk_sum(columns[f], scaled)
            for place, (dx, dy, kind) in enumerate(CHUNKS):
                acc[e + dx, f + dy, kind] += scaled[8 * place : 8 * place + 8]
        return energy

    energy = lax.fori_loop(0, 8, body, jnp.zeros((8, LANES), F32))
    r["tile", n][...] = sums_tile(gamma, energy)
    reduce_start(r, n)
    sub, lane = iota((8, LANES), 0) < 4, lax.rem(iota((8, LANES), 1), 64)
    keep = jnp.logical_and(sub, lane > 0)

    def fold(e, _):
        tops = [jnp.zeros((8, LANES), F32), jnp.zeros((8, LANES), F32)]
        for f in range(5):
            z0, z1, z2 = acc[e, f, 4], acc[e, f, 5], acc[e, f, 6]
            t0, t1, t2 = (pltpu.roll(v, 4, 0) for v in (z0, z1, z2))
            for k, extra in enumerate((z0 + z2, t0, z1 + t2, t1)):
                first = 16 * f + 8 * (k % 2)
                image[e, k // 2, first : first + 8] = acc[e, f, k] + jnp.where(keep, pltpu.roll(extra, 1, 1), 0.0)
                j = 2 * f + k % 2
                if j < LAST:
                    tops[k // 2] = jnp.where(lane == j, pltpu.roll(extra, 65 + j, 1), tops[k // 2])
        for px in range(2):
            top[2 * e + px] = jnp.where(sub, tops[px], 0.0)
        return 0

    lax.fori_loop(0, 9, fold, 0)


def element_energy(r):
    stiff = r.stiff[...]

    def body(e, energy):
        columns, products = element_product(r.store, stiff, e)
        factor = factor_of(r.rho[e])
        for f in range(4):
            energy = energy + chunk_sum(columns[f], products[f] * factor[f : f + 1, :])
        return energy

    return lax.fori_loop(0, 8, body, jnp.zeros((8, LANES), F32))


def square_sum(field):
    def body(e, total):
        for f in range(4):
            for k in range(4):
                held = at(field, e, f, k)
                total = total + held * held
        return total

    return lax.fori_loop(0, 8, body, jnp.zeros((8, LANES), F32))


def sums_tile(gamma, delta):
    gamma = jnp.sum(gamma, axis=0, keepdims=True)
    delta = jnp.sum(delta, axis=0, keepdims=True)
    gamma, delta = gamma + pltpu.roll(gamma, 64, 1), delta + pltpu.roll(delta, 64, 1)
    return jnp.where(iota((1, LANES), 1) < 64, gamma, delta)


def read_sums(sum_ref):
    held, low = sum_ref[...], iota((1, LANES), 1) < 64
    return (
        jnp.sum(jnp.where(low, held, 0.0), axis=1, keepdims=True),
        jnp.sum(jnp.where(low, 0.0, held), axis=1, keepdims=True),
    )


def over_nodes(body):
    def step(e, _):
        body(e)
        return 0

    lax.fori_loop(0, 9, step, 0)


def cross_device(shift):
    role, gx, gy = place_of()
    target = lax.rem(2 * gx + role + shift, 16)
    return {"role": lax.rem(target, 2), "gx": lax.div(target, 2), "gy": gy}


def reduce_start(r, n):
    gy = lax.axis_index("gy")
    mine, slots, send, recv = r["tile", n], r["slots", n], r["rsend", n], r["rrecv", n]
    slots[gy] = mine[...]
    for k in range(1, GYN):
        remote(mine, slots.at[gy], send.at[0], recv.at[0], device_at(0, k)).start()


def reduce_middle(r, n):
    role, gx, gy = place_of()
    slots, half, send, recv = r["slots", n], r["half", n], r["rsend", n], r["rrecv", n]
    remote(slots.at[0:7], slots.at[0:7], send.at[0], recv.at[0], device_at(0, 0, True)).wait()
    part = jnp.sum(slots[0:8], axis=0)
    half[...] = part
    place = 8 + 2 * gx + role
    slots[place] = part
    for k in range(1, 16):
        remote(half, slots.at[place], send.at[1], recv.at[1], cross_device(k)).start()


def reduce_end(r, n):
    slots, send, recv = r["slots", n], r["rsend", n], r["rrecv", n]
    remote(slots.at[8:23], slots.at[8:23], send.at[1], recv.at[1], device_at(0, 0, True)).wait()
    r["sum", n][...] = jnp.sum(slots[8:24], axis=0)


FACE_MOVES = ((1, 0), (-1, 0), (0, 1), (0, -1), (1, 1), (1, -1), (-1, 1), (-1, -1))


def face_copies(r, n):
    image, corners = r["image", n], r["corners", n]
    ends = (
        (image.at[8, 0], r["xlo", n]),
        (image.at[0, 0], r["xhi", n]),
        (image.at[:, :, 64:72], r["ylo", n]),
        (image.at[:, :, 0:8], r["yhi", n]),
        (image.at[8, 0, 64:72], corners.at[0]),
        (image.at[8, 0, 0:8], corners.at[1]),
        (image.at[0, 0, 64:72], corners.at[2]),
        (image.at[0, 0, 0:8], corners.at[3]),
    )
    send, recv = r["fsend", n], r["frecv", n]
    return [
        remote(src, dst, send.at[k], recv.at[k], device_at(dx, dy))
        for k, ((dx, dy), (src, dst)) in enumerate(zip(FACE_MOVES, ends))
    ]


def plane_copies(r, n):
    lift, rows, send, recv = r["lift", n], r["trow", n], r["zsend", n], r["zrecv", n]
    tiles = (lift.at[16], lift.at[0], rows.at[1], rows.at[0], rows.at[1], rows.at[0], rows.at[1], rows.at[0])
    copies = [remote(r["packed", n], r["lifted", n], send.at[16], recv.at[16], device_at(0, 0, True))]
    for k, (dx, dy) in enumerate(FACE_MOVES):
        for other in range(2):
            m = 2 * k + other
            copies.append(
                remote(tiles[k], r["tface", n].at[m], send.at[m], recv.at[m], device_at(dx, dy, other == 1))
            )
    return copies


def face_stage(r, n):
    role = lax.axis_index("role")
    image, top, lift = r["image", n], r["imaget", n], r["lift", n]
    faces = face_copies(r, n)
    for copy in faces:
        copy.start()

    @pl.when(role == 0)
    def _():
        lift[...] = top[...]

    @pl.when(role == 1)
    def _():
        pack_bottom(image, lift)

    compress(lambda x: lift[x], r["packed", n])
    lane = iota((8, LANES), 1)
    below, above = jnp.zeros((8, LANES), F32), jnp.zeros((8, LANES), F32)
    for x in range(17):
        tile = lift[x]
        below = jnp.where(lane == x, pltpu.roll(tile, x, 1) if x else tile, below)
        above = jnp.where(lane == x, pltpu.roll(tile, 56 + x, 1), above)
    r["trow", n][0] = below
    r["trow", n][1] = above
    planes = plane_copies(r, n)
    for copy in planes:
        copy.start()
    reduce_middle(r, n)
    if n == 0:
        outer_stage(r)
    reduce_end(r, n)
    for copy in faces + planes:
        copy.wait()


def add_faces(r, n, work, workt):
    role, gx, gy = place_of()
    low_x, low_y = gx > 0, gy > 0
    image, corners = r["image", n], r["corners", n]
    lift, lifted, edges = r["lift", n], r["lifted", n], r["tface", n]
    tface = [edges[2 * k] + edges[2 * k + 1] for k in range(8)]
    xlo, xhi, ylo, yhi = (r[name, n] for name in ("xlo", "xhi", "ylo", "yhi"))
    low = low_lanes()

    def join(e, p, below, above):
        f0, f4 = work[e, p, 0:8], work[e, p, 64:72]
        below = jnp.where(low_y, below, 0.0)
        work[e, p, 0:8] = f0 + pltpu.roll(jnp.where(low, f4, below), 64, 1)
        work[e, p, 64:72] = f4 + pltpu.roll(jnp.where(low, above, f0), 64, 1)

    work[...] = image[...]
    work[0, 0] += jnp.where(low_x, xlo[...], 0.0)
    work[8, 0] += xhi[...]
    join(0, 0, ylo[0, 0] + jnp.where(low_x, corners[0], 0.0), yhi[0, 0] + jnp.where(low_x, corners[1], 0.0))
    join(8, 0, ylo[8, 0] + corners[2], yhi[8, 0] + corners[3])
    for e in range(8):
        for p in range(2):
            if e or p:
                join(e, p, ylo[e, p], yhi[e, p])

    lane = iota((8, LANES), 1)

    def row_of(face, first, last):
        first = jnp.where(low_x, first, 0.0)
        face = face + jnp.where(lane == 0, pltpu.roll(first, LANES - 16, 1), 0.0)
        return face + jnp.where(lane == 16, pltpu.roll(last, 16, 1), 0.0)

    below = jnp.where(low_y, row_of(tface[2], tface[4], tface[6]), 0.0)
    above = row_of(tface[3], tface[5], tface[7])
    for x in range(17):
        tile = lift[x] + expand(lifted, x)
        if x == 0:
            tile = tile + jnp.where(low_x, tface[0], 0.0)
        if x == 16:
            tile = tile + tface[1]
        total = tile + jnp.where(lane == 64, pltpu.roll(tile, 56, 1), 0.0)
        total = total + jnp.where(lane == 8, pltpu.roll(tile, 72, 1), 0.0)
        total = total + jnp.where(lane == 0, pltpu.roll(below, LANES - x, 1) if x else below, 0.0)
        total = total + jnp.where(lane == 72, pltpu.roll(above, 72 - x, 1), 0.0)
        workt[x] = total
    workt[17] = jnp.zeros((8, LANES), F32)

    @pl.when(role == 1)
    def _():
        set_bottom(work, workt)

    work[...] = work[...] * r.free[...]
    workt[...] = workt[...] * r.freet[...]


def spare(value):
    return value.reshape(1, 1, 1)


def first_stage(r):
    for e in range(8):
        r.rho[e] = r.dall[e]
    build_store(r.r0, r.r0t, r.store)
    apply_operator(r, 0, square_sum(r.r0))


def second_stage(r):
    add_faces(r, 0, r.s0, r.s0t)
    gamma, delta = read_sums(r["sum", 0])
    alpha = spare(gamma / delta)

    def update(e):
        r.r1[e] = r.r0[e] - alpha * r.s0[e]

    over_nodes(update)
    r.r1t[...] = r.r0t[...] - alpha * r.s0t[...]
    build_store(r.r1, r.r1t, r.store)
    apply_operator(r, 1, square_sum(r.r1))


def third_stage(r):
    add_faces(r, 1, r.work, r.workt)
    gamma0, delta0 = read_sums(r["sum", 0])
    gamma1, delta1 = read_sums(r["sum", 1])
    alpha0 = gamma0 / delta0
    beta1 = gamma1 / gamma0
    alpha1 = gamma1 / (delta1 - beta1 * gamma1 / alpha0)
    alpha0, alpha1, beta1 = spare(alpha0), spare(alpha1), spare(beta1)

    def update(e):
        p = r.r1[e] + beta1 * r.r0[e]
        r.p1[e] = p
        r.u1[e] = alpha0 * r.r0[e] + alpha1 * p
        r.r2[e] = r.r1[e] - alpha1 * (r.work[e] + beta1 * r.s0[e])

    over_nodes(update)
    p = r.r1t[...] + beta1 * r.r0t[...]
    r.p1t[...] = p
    r.u1t[...] = alpha0 * r.r0t[...] + alpha1 * p
    r.r2t[...] = r.r1t[...] - alpha1 * (r.workt[...] + beta1 * r.s0t[...])
    build_store(r.r2, r.r2t, r.store)
    delta = element_energy(r)
    r["tile", 2][...] = sums_tile(square_sum(r.r2), delta)


def reduce_stage(r):
    reduce_start(r, 2)
    reduce_middle(r, 2)
    reduce_end(r, 2)


def last_stage(r):
    gamma0, delta0 = read_sums(r["sum", 0])
    gamma1, delta1 = read_sums(r["sum", 1])
    gamma2, delta2 = read_sums(r["sum", 2])
    alpha0 = gamma0 / delta0
    beta1 = gamma1 / gamma0
    alpha1 = gamma1 / (delta1 - beta1 * gamma1 / alpha0)
    beta2 = gamma2 / gamma1
    alpha2 = spare(gamma2 / (delta2 - beta2 * gamma2 / alpha1))
    beta2 = spare(beta2)

    def update(e):
        r.u[e] = r.u1[e] + alpha2 * (r.r2[e] + beta2 * r.p1[e])

    over_nodes(update)
    r.ut[...] = r.u1t[...] + alpha2 * (r.r2t[...] + beta2 * r.p1t[...])
    build_store(r.u, r.ut, r.store)
    stiff = r.stiff[...]
    rows = iota((8, LANES), 0)

    def body(e, before):
        columns, products = element_product(r.store, stiff, e)
        rho = r.rho[e]
        energy = jnp.zeros((8, LANES), F32)
        for f in range(4):
            one = jnp.sum(chunk_sum(columns[f], products[f]), axis=0, keepdims=True)
            energy = jnp.where(rows == f, one, energy)
        layer = (-3.0 * (1.0 - floor_stiff) / 32.0) * (rho * rho) * energy
        r.grad[e] = before + pltpu.roll(layer, 4, 0)
        return layer

    r.grad[8] = lax.fori_loop(0, 8, body, jnp.zeros((8, LANES), F32))
    role, lane = lax.axis_index("role"), lax.rem(iota((8, LANES), 1), 64)
    rim = jnp.zeros((8, LANES), F32)
    for k in range(9):
        held = r.grad[k]
        held = jnp.where(role == 0, pltpu.roll(held, k + 65, 1), pltpu.roll(held, k, 1) if k else held)
        rim = jnp.where(lane == k, held, rim)
    r.zgrad[...] = rim


def edge_targets():
    role, gx, gy = place_of()
    up, down = lax.rem(gx + 1, GXN), lax.rem(gx + GXN - 1, GXN)
    return [
        {"role": role, "gx": up, "gy": 0},
        {"role": role, "gx": down, "gy": 7},
        {"role": 1 - role, "gx": up, "gy": 0},
        {"role": 1 - role, "gx": down, "gy": 7},
    ]


def gradient_copies(r):
    gy = lax.axis_index("gy")
    copies = []
    for k in range(GYN):
        target = lax.rem(gy + k, GYN)
        if k:
            copies.append(
                remote(r.grad.at[pl.ds(target, 2)], r.gall.at[gy], r.gsend.at[k], r.grecv.at[k], device_at(0, k))
            )
        copies.append(
            remote(r.zgrad, r.zall.at[gy], r.gsend.at[8 + k], r.grecv.at[8 + k], device_at(0, k, True))
        )
    return copies


def rim_copies(r):
    gy = lax.axis_index("gy")
    up, down, up_z, down_z = edge_targets()
    return [
        remote(r.grad.at[8], r.grim.at[gy], r.esend.at[0], r.erecv.at[gy], up),
        remote(r.grad.at[0], r.grim.at[gy], r.esend.at[1], r.erecv.at[gy], down),
        remote(r.zgrad, r.zrim.at[gy], r.esend.at[2], r.erecv.at[8 + gy], up_z),
        remote(r.zgrad, r.zrim.at[gy], r.esend.at[3], r.erecv.at[8 + gy], down_z),
    ]


def gradient_stage(r):
    gy = lax.axis_index("gy")
    for copy in gradient_copies(r) + rim_copies(r):
        copy.start()
    r.gall[gy] = r.grad[pl.ds(gy, 2)]


def gradient_end(r):
    gy = lax.axis_index("gy")
    for copy in gradient_copies(r):
        copy.wait()
    for copy in rim_copies(r):
        copy.wait_send()

    @pl.when(jnp.logical_or(gy == 0, gy == 7))
    def _():
        for k in range(GYN):
            remote(r.zgrad, r.grim.at[k], r.esend.at[0], r.erecv.at[k], device_at(0, 0, True)).wait_recv()
            remote(r.zgrad, r.zrim.at[k], r.esend.at[0], r.erecv.at[8 + k], device_at(0, 0, True)).wait_recv()


def unpack_stage(r):
    back = parity_back()
    for q in range(3):
        even = [r.u[x // 2, x % 2, pl.ds(q, 8, stride=8)] for x in range(16)]
        odd = [r.u[x // 2, x % 2, pl.ds(4 + q, 8, stride=8)] for x in range(16)]
        wide = jnp.concatenate([jnp.concatenate(even, axis=0), jnp.concatenate(odd, axis=0)], axis=1)
        total = None
        for part in pieces_of(wide, 3):
            one = mul(part, back)
            total = one if total is None else total + one
        r.disp[q, :, 0:8] = total[:, :LANES].reshape(16, 8, LANES)
        r.disp[q, :, 8:16] = total[:, LANES:].reshape(16, 8, LANES)


def final_stage(r):
    role, gx, gy = place_of()
    for k in range(GYN):
        rows = slice(8 * k, 8 * k + 8)
        r.layers[0, rows] = r.gall[k, 0]
        r.layers[1, rows] = r.gall[k, 0]
        r.layers[2, rows] = r.gall[k, 1]
        for layer in range(3):
            r.zlayers[layer, rows] = r.zall[k]

    @pl.when(gy == 0)
    def _():
        for k in range(GYN):
            r.layers[0, 8 * k : 8 * k + 8] = r.grim[k]
            r.zlayers[0, 8 * k : 8 * k + 8] = r.zrim[k]

    @pl.when(gy == 7)
    def _():
        for k in range(GYN):
            r.layers[2, 8 * k : 8 * k + 8] = r.grim[k]
            r.zlayers[2, 8 * k : 8 * k + 8] = r.zrim[k]

    pairs = (jnp.where(gy == 0, 8, gy), gy, jnp.where(gy == 7, 0, gy + 1))
    rows, cols = iota((LANES, 256), 0), iota((LANES, 256), 1)
    fine, beyond = cols < LANES, jnp.logical_and(cols >= LANES, cols < LANES + 2)

    def twice(chosen):
        chosen = chosen.astype(F32).astype(BF16)
        return jnp.concatenate([chosen, chosen], axis=0)

    widen = [twice(jnp.logical_and(fine, rows == 64 * h + lax.div(cols, 2))) for h in range(2)]
    rows_y, cols_y = iota((256, LANES), 0), iota((256, LANES), 1)
    wanted = lax.div(rows_y, 4) - 8 * lax.div(lax.rem(cols_y, 64), 8) - 4 * lax.div(cols_y, 64)
    spot = lax.rem(cols_y, 8)
    for k in range(3):
        wide = []
        main = jnp.concatenate(pieces_of(r.layers[k], 2), axis=1)
        side = jnp.concatenate(pieces_of(r.zlayers[k], 2), axis=1)
        for h in range(2):
            reach_out = twice(jnp.logical_and(beyond, rows == 64 * h + pairs[k]))
            wide.append(mul(main, widen[h]) + mul(side, reach_out))
        wide = jnp.concatenate(wide, axis=0)
        first = 4 if k else 0
        inside = jnp.logical_and(spot >= first, spot < first + 4)
        repeat = jnp.logical_and(inside, wanted == spot - first).astype(F32).astype(BF16)
        repeat = jnp.concatenate([repeat, repeat], axis=1)
        r.wide[k] = mul(repeat, jnp.concatenate(pieces_of(wide, 2), axis=0))
    band = hat_of(iota((256, LANES), 1) - column_z(role, (256, LANES), 0)).astype(BF16)
    bands = jnp.concatenate([band, band], axis=0)
    for o in range(4):
        r.zc[o, 0:8] = jnp.zeros((8, 256), F32)
        r.zc[o, 264:272] = jnp.zeros((8, 256), F32)
        for b in range(8):
            spot = slice(32 * b, 32 * b + 32)
            total = None
            for layer, planes in ((0, (0, 1)), (1, (2, 3, 4, 5)), (2, (6, 7))):
                part = None
                for i in planes:
                    if o <= i <= o + 4:
                        one = HAT[i - o] * r.m[i, spot]
                        part = one if part is None else part + one
                if part is not None:
                    part = part * r.wide[layer, spot]
                    total = part if total is None else total + part
            r.zc[o, 8 + 32 * b : 40 + 32 * b] = total
        for b in range(8):
            first = 32 * b
            total = (
                3.0 * r.zc[o, 8 + first : 40 + first]
                + 2.0 * (r.zc[o, 7 + first : 39 + first] + r.zc[o, 9 + first : 41 + first])
                + (r.zc[o, 6 + first : 38 + first] + r.zc[o, 10 + first : 42 + first])
            )
            r.sens[o, first : first + 32] = mul(jnp.concatenate(pieces_of(total, 2), axis=1), bands)


FIELD = (9, 2, 80, LANES)
TILE = (1, LANES)
TOP = (18, 8, LANES)


class Refs(dict):
    def __getattr__(self, name):
        return self[name]


def buffers():
    shapes = {
        "edge": (8, 512), "lo": (4, 256, LANES), "hi": (4, 256, LANES), "edges": (3, 8, 512),
        "m": (8, 256, 256), "zc": (8, 272, 256), "psum": (256, LANES),
        "dens": (GYN, 8, LANES), "vf": (2, 8, 2, 64, LANES), "nxhi": (2, 64, LANES), "nyhi": (2, 8, 2, 8, LANES),
        "ncorner": (2, 8, LANES), "bottom": (2,) + TOP, "packed": (3, 8, LANES), "npacked": (3, 8, LANES), "dall": (GYN, 8, LANES),
        "rho": (8, 8, LANES), "store": (9, 5, 7, 8, LANES), "acc": (9, 5, 7, 8, LANES), "grad": (9, 8, LANES),
        "zgrad": (8, LANES), "gall": (GYN, 2, 8, LANES), "grim": (GYN, 8, LANES), "zall": (GYN, 8, LANES),
        "zrim": (GYN, 8, LANES), "layers": (3, 64, LANES), "zlayers": (3, 64, LANES), "wide": (3, 256, 256),
    }
    for name in ("r0", "free", "s0", "r1", "p1", "u1", "r2", "u", "work"):
        shapes[name] = FIELD
        shapes[name + "t"] = TOP
    for n in range(3):
        shapes["tile", n] = shapes["sum", n] = shapes["half", n] = TILE
        shapes["slots", n] = (24, 1, LANES)
    for n in range(2):
        shapes["image", n] = FIELD
        shapes["imaget", n] = shapes["lift", n] = TOP
        shapes["packed", n] = shapes["lifted", n] = (3, 8, LANES)
        shapes["trow", n] = (2, 8, LANES)
        shapes["tface", n] = (16, 8, LANES)
        shapes["xlo", n] = shapes["xhi", n] = (80, LANES)
        shapes["ylo", n] = shapes["yhi", n] = (9, 2, 8, LANES)
        shapes["corners", n] = (4, 8, LANES)
    scratch = {name: pltpu.VMEM(shape, F32) for name, shape in shapes.items()}
    scratch["stiff"] = pltpu.VMEM((2 * ROWS, 2 * ROWS), BF16)
    counts = {"dsend": 7, "drecv": 7, "nsend": 12, "nrecv": 12, "gsend": 16, "grecv": 16, "esend": 4, "erecv": 16}
    for n in range(3):
        counts["rsend", n] = counts["rrecv", n] = 2
        counts["fsend", n] = counts["frecv", n] = 8
        counts["zsend", n] = counts["zrecv", n] = 17
    for name, count in counts.items():
        scratch[name] = pltpu.SemaphoreType.DMA((count,))
    return scratch


def greet_all():
    barrier = pltpu.get_barrier_semaphore()
    devices = [device_at(0, k) for k in range(1, GYN)]
    devices += [cross_device(k) for k in range(1, 16)]
    devices += [device_at(dx, dy) for dx, dy in FACE_MOVES[4:]]
    devices += [slab_device(shift, other) for shift, other in ((1, False), (-1, False), (1, True), (-1, True))]
    for device in devices:
        pl.semaphore_signal(barrier, inc=1, device_id=device, device_id_type=MESH)

    return len(devices)


def whole_kernel(names, *refs):
    r = Refs(zip(names, refs))
    count = greet_all()
    edge_stage(r)
    pack_stage(r)
    pl.semaphore_wait(pltpu.get_barrier_semaphore(), count)
    swap_stage(r)
    inner_stage(r)
    spread_stage(r)
    top_stage(r)
    first_stage(r)
    face_stage(r, 0)
    second_stage(r)
    face_stage(r, 1)
    third_stage(r)
    reduce_stage(r)
    last_stage(r)
    gradient_stage(r)
    unpack_stage(r)
    gradient_end(r)
    final_stage(r)


def on_device(design, force, clamped_dof_mask, stiffness):
    chosen = jnp.asarray(row_table())
    scratch = buffers()
    names = ["design", "force", "mask", "stiffness", "chosen", "sens", "disp"] + list(scratch)
    vmem = pl.BlockSpec(memory_space=pltpu.VMEM)
    return pl.pallas_call(
        functools.partial(whole_kernel, names),
        out_shape=(
            jax.ShapeDtypeStruct((4, 256, LANES), F32),
            jax.ShapeDtypeStruct((3, 16, 16, LANES), F32),
        ),
        in_specs=[vmem] * 5,
        out_specs=(vmem, vmem),
        scratch_shapes=list(scratch.values()),
        compiler_params=pltpu.CompilerParams(
            collective_id=0, has_side_effects=True, vmem_limit_bytes=36 * 1024 * 1024
        ),
        name="compliance",
    )(design, force, clamped_dof_mask, stiffness, chosen)


def solution(mesh):
    fine = P(("gx", "gy"), None, "role")
    nodes = P(None, "gx", "gy", "role")
    return jax.shard_map(
        on_device, mesh=mesh, in_specs=(fine, nodes, nodes, P()), out_specs=(fine, nodes), check_vma=False
    )
```

```python
import functools
import math

import jax
import jax.numpy as jnp
import numpy as np
from jax import lax
from jax.experimental import pallas as pl
from jax.experimental.pallas import tpu as pltpu
from jax.sharding import PartitionSpec as P

sharpness = 4.0
threshold = 0.5
floor_stiff = 0.001
BEND = math.tanh(sharpness * threshold)
FULL = math.tanh(sharpness * threshold) + math.tanh(sharpness * (1.0 - threshold))
HAT = (1.0, 2.0, 3.0, 2.0, 1.0)

MESH = pl.DeviceIdType.MESH
F32 = jnp.float32
BF16 = jnp.bfloat16
I32 = jnp.int32
ROWS = 112
LANES = 128
GXN = 8
GYN = 8
LAST = 9
CHUNKS = (
    (0, 0, 0), (0, 0, 1), (0, 0, 2), (0, 0, 3), (0, 0, 4), (0, 0, 5),
    (1, 0, 0), (1, 0, 1), (1, 0, 4),
    (0, 1, 0), (0, 1, 2), (0, 1, 6),
    (1, 1, 0), (1, 1, 4),
)
PAIRS = {4: ((0, 0), (0, 1)), 5: ((1, 0), (1, 1)), 6: ((0, 0), (1, 0))}


def row_table():
    table = np.zeros((ROWS, 81), np.float32)
    seen = set()
    for place, (dx, dy, kind) in enumerate(CHUNKS):
        for half in range(2):
            if kind < 4:
                px, py, c = kind // 2, kind % 2, half
            else:
                (px, py), c = PAIRS[kind][half], 2
            if (dx and px) or (dy and py):
                continue
            a, b = px + 2 * dx, py + 2 * dy
            for q in range(3):
                index = ((c * 3 + b) * 3 + a) * 3 + q
                assert index not in seen
                seen.add(index)
                table[place * 8 + half * 4 + q, index] = 1.0
    assert len(seen) == 81
    return table


def place_of():
    return lax.axis_index("role"), lax.axis_index("gx"), lax.axis_index("gy")


def device_at(dx, dy, other=False):
    role, gx, gy = place_of()
    return {
        "role": (1 - role) if other else role,
        "gx": lax.rem(gx + dx + GXN, GXN),
        "gy": lax.rem(gy + dy + GYN, GYN),
    }


def remote(src, dst, send, recv, device):
    return pltpu.make_async_remote_copy(
        src_ref=src, dst_ref=dst, send_sem=send, recv_sem=recv, device_id=device, device_id_type=MESH
    )


def iota(shape, dim):
    return lax.broadcasted_iota(I32, shape, dim)


def pieces_of(values, count):
    parts = []
    for _ in range(count):
        part = values.astype(BF16)
        parts.append(part)
        values = values - part.astype(F32)
    return parts


def slab_of(shift):
    role, gx, gy = place_of()
    slab = lax.rem(gx * 8 + gy + shift + 64, 64)
    return lax.div(slab, 8), lax.rem(slab, 8)


def slab_device(shift, other):
    role = lax.axis_index("role")
    gx, gy = slab_of(shift)
    return {"role": (1 - role) if other else role, "gx": gx, "gy": gy}


def reach(places, extent):
    total = jnp.zeros(places.shape, F32)
    for k, weight in enumerate(HAT):
        target = places + (k - 2)
        total = total + jnp.where(jnp.logical_and(target >= 0, target < extent), weight, 0.0)
    return jnp.maximum(total, 1.0)


def column_z(role, shape, dim):
    lane = iota(shape, dim)
    beyond = lane - LANES + jnp.where(role == 0, LANES, -2)
    return jnp.where(lane < LANES, lane, jnp.where(lane < LANES + 2, beyond, -4096))


def hat_of(distance):
    return jnp.maximum(3 - jnp.abs(distance), 0).astype(F32)


def at(field, e, f, kind):
    return field[e, kind // 2, 16 * f + 8 * (kind % 2) : 16 * f + 8 * (kind % 2) + 8]


def parity_matrix():
    rows, cols = iota((256, 256), 0), iota((256, 256), 1)
    return (rows == 2 * lax.rem(cols, LANES) + lax.div(cols, LANES)).astype(F32).astype(BF16)


def parity_back():
    rows, cols = iota((256, 256), 0), iota((256, 256), 1)
    return (cols == 2 * lax.rem(rows, LANES) + lax.div(rows, LANES)).astype(F32).astype(BF16)


def mul(left, right):
    return jnp.dot(left, right, preferred_element_type=F32)


def edge_stage(r):
    role = lax.axis_index("role")
    rows, cols = iota((16, LANES), 0), iota((16, LANES), 1)
    first = jnp.where(role == 0, 124, 0)
    for x in range(2):
        total = None
        for k in range(2):
            inside = jnp.logical_and(rows >= 4 * k, rows < 4 * k + 4)
            chosen = jnp.logical_and(cols == first + rows - 4 * k, inside).astype(F32).astype(BF16)
            for part in pieces_of(r.design[x + 2 * k], 2):
                one = lax.dot_general(chosen, part, (((1,), (1,)), ((), ())), preferred_element_type=F32)
                total = one if total is None else total + one
        r.edge[:, 256 * x : 256 * x + 256] = total[:8]


def near_copies(r):
    return [
        remote(r.design.at[2:4], r.lo.at[2:4], r.dsend.at[0], r.drecv.at[0], slab_device(1, False)),
        remote(r.design.at[0:2], r.hi.at[0:2], r.dsend.at[1], r.drecv.at[1], slab_device(-1, False)),
        remote(r.edge, r.edges.at[1], r.dsend.at[2], r.drecv.at[2], slab_device(0, True)),
        remote(r.edge, r.edges.at[0], r.dsend.at[3], r.drecv.at[3], slab_device(1, True)),
        remote(r.edge, r.edges.at[2], r.dsend.at[4], r.drecv.at[4], slab_device(-1, True)),
    ]


def far_copies(r):
    return [
        remote(r.design.at[0:2], r.lo.at[0:2], r.dsend.at[5], r.drecv.at[5], slab_device(1, False)),
        remote(r.design.at[2:4], r.hi.at[2:4], r.dsend.at[6], r.drecv.at[6], slab_device(-1, False)),
    ]


def swap_stage(r):
    for copy in near_copies(r) + upper_copies(r):
        copy.start()
    table_stage(r)
    for copy in upper_copies(r):
        copy.wait()
    frame_stage(r)
    bottom_copy(r).start()
    for copy in near_copies(r):
        copy.wait()


def table_stage(r):
    chosen = r.chosen[...].astype(BF16)
    table = None
    for part in pieces_of(r.stiffness[...], 3):
        one = mul(chosen, part)
        table = one if table is None else table + one
    whole = None
    for part in pieces_of(table, 3):
        one = lax.dot_general(part, chosen, (((1,), (1,)), ((), ())), preferred_element_type=F32)
        whole = one if whole is None else whole + one
    high, low = pieces_of(whole, 2)
    r.stiff[...] = jnp.concatenate(
        [
            jnp.concatenate([high, high], axis=1),
            jnp.concatenate([low, jnp.zeros_like(low)], axis=1),
        ],
        axis=0,
    )


def mix(get):
    return 3.0 * get(2) + 2.0 * (get(1) + get(3)) + (get(0) + get(4))


def taps_stage(r, planes):
    role = lax.axis_index("role")
    band = hat_of(column_z(role, (LANES, 256), 1) - iota((LANES, 256), 0)).astype(BF16)
    bands = jnp.concatenate([band, band], axis=0)
    far = lax.rem(iota((16, 256), 0), 8)
    spot = jnp.where(role == 0, LANES + far, far - 4)
    rim = hat_of(column_z(role, (16, 256), 1) - spot)
    rim = jnp.where(far < 4, rim, 0.0).astype(BF16)

    def plane(p, rows):
        ref = (r.lo, r.design, r.hi)[p // 4]
        return ref[p % 4, rows]

    def edge_plane(p):
        held = r.edges[p // 4, :, 256 * (p % 2) : 256 * (p % 2) + 256]
        return pltpu.roll(held, 4, 0) if p % 4 > 1 else held

    for i in planes:
        beyond = mix(lambda k: edge_plane(i + k))
        beyond = jnp.concatenate(pieces_of(beyond, 2), axis=0)
        beyond = lax.dot_general(beyond, rim, (((0,), (0,)), ((), ())), preferred_element_type=F32)
        for b in range(4):
            rows = slice(64 * b, 64 * b + 64)
            wide = mix(lambda k: plane(i + k, rows))
            out = mul(jnp.concatenate(pieces_of(wide, 2), axis=1), bands)
            r.zc[i, 8 + 64 * b : 72 + 64 * b] = out + beyond[rows]
        r.zc[i, 0:8] = jnp.zeros((8, 256), F32)
        r.zc[i, 264:272] = jnp.zeros((8, 256), F32)


def bend_stage(r, count, plane_of, shown):
    role, gx, gy = place_of()
    slab = gx * 8 + gy
    z_places = column_z(role, (1, 256), 1) + role * LANES
    by_z = 1.0 / reach(z_places, 256)

    def body(step, _):
        i = plane_of(step)
        x = 4 * slab + i - 2
        inside = jnp.logical_and(x >= 0, x < 256)
        by_x = 1.0 / reach(jnp.full((1, 256), x, I32), 256)
        by_xz = by_z * by_x
        for b in range(8):
            first = 32 * b
            by = by_xz / reach(iota((32, 256), 0) + first, 256)
            total = mix(lambda k: r.zc[i, 6 + k + first : 38 + k + first])
            bent = jnp.tanh(sharpness * (total * by - threshold))
            r.m[i, first : first + 32] = jnp.where(inside, (1.0 - bent * bent) * (by * (sharpness / FULL)), 0.0)
            if shown:
                r.psum[first : first + 32] += (BEND + bent[:, :LANES]) * (1.0 / FULL)
        return 0

    lax.fori_loop(0, count, body, 0, unroll=2)


def inner_stage(r):
    role, gx, gy = place_of()
    slab = gx * 8 + gy

    @pl.when(slab == 0)
    def _():
        r.lo[2:4] = jnp.zeros((2, 256, LANES), F32)
        r.edges[0] = jnp.zeros((8, 512), F32)

    @pl.when(slab == 63)
    def _():
        r.hi[0:2] = jnp.zeros((2, 256, LANES), F32)
        r.edges[2] = jnp.zeros((8, 512), F32)

    taps_stage(r, (2, 3, 4, 5))
    r.psum[...] = jnp.zeros_like(r.psum)
    bend_stage(r, 4, lambda step: step + 2, True)
    density_stage(r)


def outer_stage(r):
    role, gx, gy = place_of()
    slab = gx * 8 + gy
    for copy in far_copies(r):
        copy.wait()

    @pl.when(slab == 0)
    def _():
        r.lo[0:2] = jnp.zeros((2, 256, LANES), F32)

    @pl.when(slab == 63)
    def _():
        r.hi[2:4] = jnp.zeros((2, 256, LANES), F32)

    taps_stage(r, (0, 1, 6, 7))
    bend_stage(r, 4, lambda step: jnp.where(step < 2, step, step + 4), False)


def density_stage(r):
    rows, cols = iota((LANES, 256), 0), iota((LANES, 256), 1)
    sub = lax.rem(rows, 8)
    wanted = 8 * lax.div(lax.rem(rows, 64), 8) + 4 * lax.div(rows, 64) + sub
    gather = jnp.logical_and(sub < 4, lax.div(cols, 4) == wanted).astype(F32).astype(BF16)
    parts = pieces_of(r.psum[...], 3)
    by_rows = mul(gather, parts[0]) + mul(gather, parts[1]) + mul(gather, parts[2])
    by_rows = jnp.concatenate([by_rows[:64], by_rows[64:]], axis=1)
    rows, cols = iota((256, LANES), 0), iota((256, LANES), 1)
    merge = (cols == 64 * lax.div(rows, LANES) + lax.div(lax.rem(rows, LANES), 2)).astype(F32).astype(BF16)
    parts = pieces_of(by_rows, 3)
    density = (mul(parts[0], merge) + mul(parts[1], merge) + mul(parts[2], merge)) * (1.0 / 32.0)
    for k in range(GYN):
        r.dens[k] = density[8 * k : 8 * k + 8]


def pack_stage(r):
    matrix = parity_matrix()
    r.vf[...] = jnp.zeros_like(r.vf)
    for q in range(3):
        wide = jnp.concatenate(
            [r.force[q, :, 8 * h : 8 * h + 8].reshape(LANES, LANES) for h in range(2)], axis=1
        )
        force = None
        for part in pieces_of(wide, 3):
            one = mul(part, matrix)
            force = one if force is None else force + one
        wide = jnp.concatenate(
            [r.mask[q, :, 8 * h : 8 * h + 8].reshape(LANES, LANES) for h in range(2)], axis=1
        )
        free = mul((1 - wide).astype(F32).astype(BF16), matrix)
        force = force * free
        for x in range(16):
            for half in range(2):
                for kind, values in ((0, force), (1, free)):
                    r.vf[kind, x // 2, x % 2, pl.ds(4 * half + q, 8, stride=8)] = values[
                        8 * x : 8 * x + 8, LANES * half : LANES * half + LANES
                    ]


def density_copies(r):
    role, gx, gy = place_of()
    copies = []
    for k in range(1, GYN):
        target = lax.rem(gy + k, GYN)
        copies.append(remote(r.dens.at[target], r.dall.at[gy], r.nsend.at[k], r.nrecv.at[k], device_at(0, k)))
    return copies


def upper_copies(r):
    return [
        remote(r.vf.at[:, 0, 0], r.nxhi, r.nsend.at[8], r.nrecv.at[8], device_at(-1, 0)),
        remote(r.vf.at[:, :, :, 0:8], r.nyhi, r.nsend.at[9], r.nrecv.at[9], device_at(0, -1)),
        remote(r.vf.at[:, 0, 0, 0:8], r.ncorner, r.nsend.at[10], r.nrecv.at[10], device_at(-1, -1)),
    ]


def bottom_copy(r):
    return remote(r.packed, r.npacked, r.nsend.at[11], r.nrecv.at[11], device_at(0, 0, True))


def spread_stage(r):
    gy = lax.axis_index("gy")
    for copy in density_copies(r):
        copy.start()
    for copy in far_copies(r):
        copy.start()
    r.dall[gy] = r.dens[gy]


def low_lanes():
    return iota((8, LANES), 1) < 64


def frame_stage(r):
    role, gx, gy = place_of()
    has_x, has_y = gx < GXN - 1, gy < GYN - 1
    has_both = jnp.logical_and(has_x, has_y)
    low = low_lanes()

    def upper(beyond, own):
        return pltpu.roll(jnp.where(low, beyond, own), 64, 1)

    for kind, ref in ((0, r.r0), (1, r.free)):
        for e in range(8):
            for px in range(2):
                ref[e, px, 0:64] = r.vf[kind, e, px]
                ref[e, px, 64:72] = upper(jnp.where(has_y, r.nyhi[kind, e, px], 0.0), r.vf[kind, e, px, 0:8])
                ref[e, px, 72:80] = jnp.zeros((8, LANES), F32)
        beside = jnp.where(has_x, r.nxhi[kind], 0.0)
        ref[8, 0, 0:64] = beside
        ref[8, 0, 64:72] = upper(jnp.where(has_both, r.ncorner[kind], 0.0), beside[0:8])
        ref[8, 0, 72:80] = jnp.zeros((8, LANES), F32)
        ref[8, 1] = jnp.zeros((80, LANES), F32)
        pack_bottom(ref, r.bottom.at[kind])
    compress(lambda x: r.bottom[0, x] + pltpu.roll(r.bottom[1, x], 4, 0), r.packed)


def pack_bottom(field, out):
    sub, lane = iota((8, LANES), 0) < 4, lax.rem(iota((8, LANES), 1), 64)

    def body(e, _):
        for px in range(2):
            tile = jnp.zeros((8, LANES), F32)
            for j in range(LAST):
                held = field[e, px, 8 * j : 8 * j + 8]
                held = pltpu.roll(held, j, 1) if j else held
                tile = jnp.where(lane == j, held, tile)
            out[2 * e + px] = jnp.where(sub, tile, 0.0)
        return 0

    lax.fori_loop(0, 9, body, 0, unroll=9)


def compress(tiles, out):
    lane = lax.div(lax.rem(iota((8, LANES), 1), 64), 9)
    for group in range(3):
        total = jnp.zeros((8, LANES), F32)
        for m in range(7):
            x = 7 * group + m
            if x < 17:
                held = tiles(x)
                total = jnp.where(lane == m, pltpu.roll(held, 9 * m, 1) if m else held, total)
        out[group] = total


def expand(packed, x):
    held, m = packed[x // 7], x % 7
    held = pltpu.roll(held, LANES - 9 * m, 1) if m else held
    return jnp.where(lax.rem(iota((8, LANES), 1), 64) < 9, held, 0.0)


def set_bottom(field, tiles):
    keep = jnp.logical_and(iota((8, LANES), 0) < 4, lax.rem(iota((8, LANES), 1), 64) == 0)

    def body(e, _):
        for px in range(2):
            tile = tiles[2 * e + px]
            for j in range(LAST):
                moved = pltpu.roll(tile, LANES - j, 1) if j else tile
                spot = slice(8 * j, 8 * j + 8)
                field[e, px, spot] = jnp.where(keep, moved, field[e, px, spot])
        return 0

    lax.fori_loop(0, 9, body, 0, unroll=9)


def top_stage(r):
    role = lax.axis_index("role")
    bottom_copy(r).wait()
    keep = jnp.logical_and(iota((8, LANES), 0) < 4, role == 0)
    for x in range(17):
        held = expand(r.npacked, x)
        r.r0t[x] = jnp.where(keep, held, 0.0)
        r.freet[x] = jnp.where(keep, pltpu.roll(held, 4, 0), 0.0)
    r.r0t[17] = jnp.zeros((8, LANES), F32)
    r.freet[17] = jnp.zeros((8, LANES), F32)
    for copy in density_copies(r):
        copy.wait()


def build_store(field, top, store):
    sub = iota((8, LANES), 0) < 4
    inside = lax.rem(iota((8, LANES), 1), 64) < 63

    def body(e, _):
        tops = [top[2 * e], top[2 * e + 1]]
        for f in range(5):
            held = [at(field, e, f, k) for k in range(4)]
            shifted = []
            for k in range(4):
                above = pltpu.roll(tops[k // 2], 63 - 2 * f - k % 2, 1)
                shifted.append(jnp.where(inside, pltpu.roll(held[k], LANES - 1, 1), above))
            turned = [None] + [pltpu.roll(v, 4, 0) for v in shifted[1:]]
            for k in range(4):
                store[e, f, k] = held[k]
            store[e, f, 4] = jnp.where(sub, shifted[0], turned[1])
            store[e, f, 5] = jnp.where(sub, shifted[2], turned[3])
            store[e, f, 6] = jnp.where(sub, shifted[0], turned[2])
        return 0

    lax.fori_loop(0, 9, body, 0, unroll=9)


def element_product(store, stiff, e):
    columns = []
    for f in range(4):
        columns.append(jnp.concatenate([store[e + dx, f + dy, kind] for dx, dy, kind in CHUNKS], axis=0))
    wide = jnp.concatenate(columns, axis=1)
    out = mul(stiff, jnp.concatenate(pieces_of(wide, 2), axis=0))
    product = out[:ROWS] + out[ROWS:]
    return columns, [product[:, f * LANES : (f + 1) * LANES] for f in range(4)]


def chunk_sum(left, right):
    both = left * right
    total = both[:8]
    for k in range(1, len(CHUNKS)):
        total = total + both[8 * k : 8 * k + 8]
    return total


def factor_of(rho):
    return floor_stiff + (1.0 - floor_stiff) * (rho * rho * rho)


def apply_operator(r, n, gamma):
    image, top = r["image", n], r["imaget", n]
    store, acc = r.store, r.acc
    acc[...] = jnp.zeros_like(acc)
    stiff = r.stiff[...]

    def body(e, energy):
        columns, products = element_product(store, stiff, e)
        factor = factor_of(r.rho[e])
        for f in range(4):
            scaled = products[f] * factor[f : f + 1, :]
            energy = energy + chunk_sum(columns[f], scaled)
            for place, (dx, dy, kind) in enumerate(CHUNKS):
                acc[e + dx, f + dy, kind] += scaled[8 * place : 8 * place + 8]
        return energy

    energy = lax.fori_loop(0, 8, body, jnp.zeros((8, LANES), F32), unroll=8)
    r["tile", n][...] = sums_tile(gamma, energy)
    reduce_start(r, n)
    sub, lane = iota((8, LANES), 0) < 4, lax.rem(iota((8, LANES), 1), 64)
    keep = jnp.logical_and(sub, lane > 0)

    def fold(e, _):
        tops = [jnp.zeros((8, LANES), F32), jnp.zeros((8, LANES), F32)]
        for f in range(5):
            z0, z1, z2 = acc[e, f, 4], acc[e, f, 5], acc[e, f, 6]
            t0, t1, t2 = (pltpu.roll(v, 4, 0) for v in (z0, z1, z2))
            for k, extra in enumerate((z0 + z2, t0, z1 + t2, t1)):
                first = 16 * f + 8 * (k % 2)
                image[e, k // 2, first : first + 8] = acc[e, f, k] + jnp.where(keep, pltpu.roll(extra, 1, 1), 0.0)
                j = 2 * f + k % 2
                if j < LAST:
                    tops[k // 2] = jnp.where(lane == j, pltpu.roll(extra, 65 + j, 1), tops[k // 2])
        for px in range(2):
            top[2 * e + px] = jnp.where(sub, tops[px], 0.0)
        return 0

    lax.fori_loop(0, 9, fold, 0, unroll=9)


def element_energy(r):
    stiff = r.stiff[...]

    def body(e, energy):
        columns, products = element_product(r.store, stiff, e)
        factor = factor_of(r.rho[e])
        for f in range(4):
            energy = energy + chunk_sum(columns[f], products[f] * factor[f : f + 1, :])
        return energy

    return lax.fori_loop(0, 8, body, jnp.zeros((8, LANES), F32), unroll=8)


def square_sum(field):
    def body(e, total):
        for f in range(4):
            for k in range(4):
                held = at(field, e, f, k)
                total = total + held * held
        return total

    return lax.fori_loop(0, 8, body, jnp.zeros((8, LANES), F32), unroll=8)


def sums_tile(gamma, delta):
    gamma = jnp.sum(gamma, axis=0, keepdims=True)
    delta = jnp.sum(delta, axis=0, keepdims=True)
    gamma, delta = gamma + pltpu.roll(gamma, 64, 1), delta + pltpu.roll(delta, 64, 1)
    return jnp.where(iota((1, LANES), 1) < 64, gamma, delta)


def read_sums(sum_ref):
    held, low = sum_ref[...], iota((1, LANES), 1) < 64
    return (
        jnp.sum(jnp.where(low, held, 0.0), axis=1, keepdims=True),
        jnp.sum(jnp.where(low, 0.0, held), axis=1, keepdims=True),
    )


def over_nodes(body):
    def step(e, _):
        body(e)
        return 0

    lax.fori_loop(0, 9, step, 0, unroll=9)


def cross_device(shift):
    role, gx, gy = place_of()
    target = lax.rem(2 * gx + role + shift, 16)
    return {"role": lax.rem(target, 2), "gx": lax.div(target, 2), "gy": gy}


def reduce_start(r, n):
    gy = lax.axis_index("gy")
    mine, slots, send, recv = r["tile", n], r["slots", n], r["rsend", n], r["rrecv", n]
    slots[gy] = mine[...]
    for k in range(1, GYN):
        remote(mine, slots.at[gy], send.at[0], recv.at[0], device_at(0, k)).start()


def reduce_middle(r, n):
    role, gx, gy = place_of()
    slots, half, send, recv = r["slots", n], r["half", n], r["rsend", n], r["rrecv", n]
    remote(slots.at[0:7], slots.at[0:7], send.at[0], recv.at[0], device_at(0, 0, True)).wait()
    part = jnp.sum(slots[0:8], axis=0)
    half[...] = part
    place = 8 + 2 * gx + role
    slots[place] = part
    for k in range(1, 16):
        remote(half, slots.at[place], send.at[1], recv.at[1], cross_device(k)).start()


def reduce_end(r, n):
    slots, send, recv = r["slots", n], r["rsend", n], r["rrecv", n]
    remote(slots.at[8:23], slots.at[8:23], send.at[1], recv.at[1], device_at(0, 0, True)).wait()
    r["sum", n][...] = jnp.sum(slots[8:24], axis=0)


FACE_MOVES = ((1, 0), (-1, 0), (0, 1), (0, -1), (1, 1), (1, -1), (-1, 1), (-1, -1))


def face_copies(r, n):
    image, corners = r["image", n], r["corners", n]
    ends = (
        (image.at[8, 0], r["xlo", n]),
        (image.at[0, 0], r["xhi", n]),
        (image.at[:, :, 64:72], r["ylo", n]),
        (image.at[:, :, 0:8], r["yhi", n]),
        (image.at[8, 0, 64:72], corners.at[0]),
        (image.at[8, 0, 0:8], corners.at[1]),
        (image.at[0, 0, 64:72], corners.at[2]),
        (image.at[0, 0, 0:8], corners.at[3]),
    )
    send, recv = r["fsend", n], r["frecv", n]
    return [
        remote(src, dst, send.at[k], recv.at[k], device_at(dx, dy))
        for k, ((dx, dy), (src, dst)) in enumerate(zip(FACE_MOVES, ends))
    ]


def plane_copies(r, n):
    lift, rows, send, recv = r["lift", n], r["trow", n], r["zsend", n], r["zrecv", n]
    tiles = (lift.at[16], lift.at[0], rows.at[1], rows.at[0], rows.at[1], rows.at[0], rows.at[1], rows.at[0])
    copies = [remote(r["packed", n], r["lifted", n], send.at[16], recv.at[16], device_at(0, 0, True))]
    for k, (dx, dy) in enumerate(FACE_MOVES):
        for other in range(2):
            m = 2 * k + other
            copies.append(
                remote(tiles[k], r["tface", n].at[m], send.at[m], recv.at[m], device_at(dx, dy, other == 1))
            )
    return copies


def face_stage(r, n):
    role = lax.axis_index("role")
    image, top, lift = r["image", n], r["imaget", n], r["lift", n]
    faces = face_copies(r, n)
    for copy in faces:
        copy.start()

    @pl.when(role == 0)
    def _():
        lift[...] = top[...]

    @pl.when(role == 1)
    def _():
        pack_bottom(image, lift)

    compress(lambda x: lift[x], r["packed", n])
    lane = iota((8, LANES), 1)
    below, above = jnp.zeros((8, LANES), F32), jnp.zeros((8, LANES), F32)
    for x in range(17):
        tile = lift[x]
        below = jnp.where(lane == x, pltpu.roll(tile, x, 1) if x else tile, below)
        above = jnp.where(lane == x, pltpu.roll(tile, 56 + x, 1), above)
    r["trow", n][0] = below
    r["trow", n][1] = above
    planes = plane_copies(r, n)
    for copy in planes:
        copy.start()
    reduce_middle(r, n)
    if n == 0:
        outer_stage(r)
    reduce_end(r, n)
    for copy in faces + planes:
        copy.wait()


def add_faces(r, n, work, workt):
    role, gx, gy = place_of()
    low_x, low_y = gx > 0, gy > 0
    image, corners = r["image", n], r["corners", n]
    lift, lifted, edges = r["lift", n], r["lifted", n], r["tface", n]
    tface = [edges[2 * k] + edges[2 * k + 1] for k in range(8)]
    xlo, xhi, ylo, yhi = (r[name, n] for name in ("xlo", "xhi", "ylo", "yhi"))
    low = low_lanes()

    def join(e, p, below, above):
        f0, f4 = work[e, p, 0:8], work[e, p, 64:72]
        below = jnp.where(low_y, below, 0.0)
        work[e, p, 0:8] = f0 + pltpu.roll(jnp.where(low, f4, below), 64, 1)
        work[e, p, 64:72] = f4 + pltpu.roll(jnp.where(low, above, f0), 64, 1)

    work[...] = image[...]
    work[0, 0] += jnp.where(low_x, xlo[...], 0.0)
    work[8, 0] += xhi[...]
    join(0, 0, ylo[0, 0] + jnp.where(low_x, corners[0], 0.0), yhi[0, 0] + jnp.where(low_x, corners[1], 0.0))
    join(8, 0, ylo[8, 0] + corners[2], yhi[8, 0] + corners[3])
    for e in range(8):
        for p in range(2):
            if e or p:
                join(e, p, ylo[e, p], yhi[e, p])

    lane = iota((8, LANES), 1)

    def row_of(face, first, last):
        first = jnp.where(low_x, first, 0.0)
        face = face + jnp.where(lane == 0, pltpu.roll(first, LANES - 16, 1), 0.0)
        return face + jnp.where(lane == 16, pltpu.roll(last, 16, 1), 0.0)

    below = jnp.where(low_y, row_of(tface[2], tface[4], tface[6]), 0.0)
    above = row_of(tface[3], tface[5], tface[7])
    for x in range(17):
        tile = lift[x] + expand(lifted, x)
        if x == 0:
            tile = tile + jnp.where(low_x, tface[0], 0.0)
        if x == 16:
            tile = tile + tface[1]
        total = tile + jnp.where(lane == 64, pltpu.roll(tile, 56, 1), 0.0)
        total = total + jnp.where(lane == 8, pltpu.roll(tile, 72, 1), 0.0)
        total = total + jnp.where(lane == 0, pltpu.roll(below, LANES - x, 1) if x else below, 0.0)
        total = total + jnp.where(lane == 72, pltpu.roll(above, 72 - x, 1), 0.0)
        workt[x] = total
    workt[17] = jnp.zeros((8, LANES), F32)

    @pl.when(role == 1)
    def _():
        set_bottom(work, workt)

    work[...] = work[...] * r.free[...]
    workt[...] = workt[...] * r.freet[...]


def spare(value):
    return value.reshape(1, 1, 1)


def first_stage(r):
    for e in range(8):
        r.rho[e] = r.dall[e]
    build_store(r.r0, r.r0t, r.store)
    apply_operator(r, 0, square_sum(r.r0))


def second_stage(r):
    add_faces(r, 0, r.s0, r.s0t)
    gamma, delta = read_sums(r["sum", 0])
    alpha = spare(gamma / delta)

    def update(e):
        r.r1[e] = r.r0[e] - alpha * r.s0[e]

    over_nodes(update)
    r.r1t[...] = r.r0t[...] - alpha * r.s0t[...]
    build_store(r.r1, r.r1t, r.store)
    apply_operator(r, 1, square_sum(r.r1))


def third_stage(r):
    add_faces(r, 1, r.work, r.workt)
    gamma0, delta0 = read_sums(r["sum", 0])
    gamma1, delta1 = read_sums(r["sum", 1])
    alpha0 = gamma0 / delta0
    beta1 = gamma1 / gamma0
    alpha1 = gamma1 / (delta1 - beta1 * gamma1 / alpha0)
    alpha0, alpha1, beta1 = spare(alpha0), spare(alpha1), spare(beta1)

    def update(e):
        p = r.r1[e] + beta1 * r.r0[e]
        r.p1[e] = p
        r.u1[e] = alpha0 * r.r0[e] + alpha1 * p
        r.r2[e] = r.r1[e] - alpha1 * (r.work[e] + beta1 * r.s0[e])

    over_nodes(update)
    p = r.r1t[...] + beta1 * r.r0t[...]
    r.p1t[...] = p
    r.u1t[...] = alpha0 * r.r0t[...] + alpha1 * p
    r.r2t[...] = r.r1t[...] - alpha1 * (r.workt[...] + beta1 * r.s0t[...])
    build_store(r.r2, r.r2t, r.store)
    delta = element_energy(r)
    r["tile", 2][...] = sums_tile(square_sum(r.r2), delta)


def reduce_stage(r):
    reduce_start(r, 2)
    reduce_middle(r, 2)
    reduce_end(r, 2)


def last_stage(r):
    gamma0, delta0 = read_sums(r["sum", 0])
    gamma1, delta1 = read_sums(r["sum", 1])
    gamma2, delta2 = read_sums(r["sum", 2])
    alpha0 = gamma0 / delta0
    beta1 = gamma1 / gamma0
    alpha1 = gamma1 / (delta1 - beta1 * gamma1 / alpha0)
    beta2 = gamma2 / gamma1
    alpha2 = spare(gamma2 / (delta2 - beta2 * gamma2 / alpha1))
    beta2 = spare(beta2)

    def update(e):
        r.u[e] = r.u1[e] + alpha2 * (r.r2[e] + beta2 * r.p1[e])

    over_nodes(update)
    r.ut[...] = r.u1t[...] + alpha2 * (r.r2t[...] + beta2 * r.p1t[...])
    build_store(r.u, r.ut, r.store)
    stiff = r.stiff[...]
    rows = iota((8, LANES), 0)

    def body(e, before):
        columns, products = element_product(r.store, stiff, e)
        rho = r.rho[e]
        energy = jnp.zeros((8, LANES), F32)
        for f in range(4):
            one = jnp.sum(chunk_sum(columns[f], products[f]), axis=0, keepdims=True)
            energy = jnp.where(rows == f, one, energy)
        layer = (-3.0 * (1.0 - floor_stiff) / 32.0) * (rho * rho) * energy
        r.grad[e] = before + pltpu.roll(layer, 4, 0)
        return layer

    r.grad[8] = lax.fori_loop(0, 8, body, jnp.zeros((8, LANES), F32), unroll=8)
    role, lane = lax.axis_index("role"), lax.rem(iota((8, LANES), 1), 64)
    rim = jnp.zeros((8, LANES), F32)
    for k in range(9):
        held = r.grad[k]
        held = jnp.where(role == 0, pltpu.roll(held, k + 65, 1), pltpu.roll(held, k, 1) if k else held)
        rim = jnp.where(lane == k, held, rim)
    r.zgrad[...] = rim


def edge_targets():
    role, gx, gy = place_of()
    up, down = lax.rem(gx + 1, GXN), lax.rem(gx + GXN - 1, GXN)
    return [
        {"role": role, "gx": up, "gy": 0},
        {"role": role, "gx": down, "gy": 7},
        {"role": 1 - role, "gx": up, "gy": 0},
        {"role": 1 - role, "gx": down, "gy": 7},
    ]


def gradient_copies(r):
    gy = lax.axis_index("gy")
    copies = []
    for k in range(GYN):
        target = lax.rem(gy + k, GYN)
        if k:
            copies.append(
                remote(r.grad.at[pl.ds(target, 2)], r.gall.at[gy], r.gsend.at[k], r.grecv.at[k], device_at(0, k))
            )
        copies.append(
            remote(r.zgrad, r.zall.at[gy], r.gsend.at[8 + k], r.grecv.at[8 + k], device_at(0, k, True))
        )
    return copies


def rim_copies(r):
    gy = lax.axis_index("gy")
    up, down, up_z, down_z = edge_targets()
    return [
        remote(r.grad.at[8], r.grim.at[gy], r.esend.at[0], r.erecv.at[gy], up),
        remote(r.grad.at[0], r.grim.at[gy], r.esend.at[1], r.erecv.at[gy], down),
        remote(r.zgrad, r.zrim.at[gy], r.esend.at[2], r.erecv.at[8 + gy], up_z),
        remote(r.zgrad, r.zrim.at[gy], r.esend.at[3], r.erecv.at[8 + gy], down_z),
    ]


def gradient_stage(r):
    gy = lax.axis_index("gy")
    for copy in gradient_copies(r) + rim_copies(r):
        copy.start()
    r.gall[gy] = r.grad[pl.ds(gy, 2)]


def gradient_end(r):
    gy = lax.axis_index("gy")
    for copy in gradient_copies(r):
        copy.wait()
    for copy in rim_copies(r):
        copy.wait_send()

    @pl.when(jnp.logical_or(gy == 0, gy == 7))
    def _():
        for k in range(GYN):
            remote(r.zgrad, r.grim.at[k], r.esend.at[0], r.erecv.at[k], device_at(0, 0, True)).wait_recv()
            remote(r.zgrad, r.zrim.at[k], r.esend.at[0], r.erecv.at[8 + k], device_at(0, 0, True)).wait_recv()


def unpack_stage(r):
    back = parity_back()
    for q in range(3):
        even = [r.u[x // 2, x % 2, pl.ds(q, 8, stride=8)] for x in range(16)]
        odd = [r.u[x // 2, x % 2, pl.ds(4 + q, 8, stride=8)] for x in range(16)]
        wide = jnp.concatenate([jnp.concatenate(even, axis=0), jnp.concatenate(odd, axis=0)], axis=1)
        total = None
        for part in pieces_of(wide, 3):
            one = mul(part, back)
            total = one if total is None else total + one
        r.disp[q, :, 0:8] = total[:, :LANES].reshape(16, 8, LANES)
        r.disp[q, :, 8:16] = total[:, LANES:].reshape(16, 8, LANES)


def final_stage(r):
    role, gx, gy = place_of()
    for k in range(GYN):
        rows = slice(8 * k, 8 * k + 8)
        r.layers[0, rows] = r.gall[k, 0]
        r.layers[1, rows] = r.gall[k, 0]
        r.layers[2, rows] = r.gall[k, 1]
        for layer in range(3):
            r.zlayers[layer, rows] = r.zall[k]

    @pl.when(gy == 0)
    def _():
        for k in range(GYN):
            r.layers[0, 8 * k : 8 * k + 8] = r.grim[k]
            r.zlayers[0, 8 * k : 8 * k + 8] = r.zrim[k]

    @pl.when(gy == 7)
    def _():
        for k in range(GYN):
            r.layers[2, 8 * k : 8 * k + 8] = r.grim[k]
            r.zlayers[2, 8 * k : 8 * k + 8] = r.zrim[k]

    pairs = (jnp.where(gy == 0, 8, gy), gy, jnp.where(gy == 7, 0, gy + 1))
    rows, cols = iota((LANES, 256), 0), iota((LANES, 256), 1)
    fine, beyond = cols < LANES, jnp.logical_and(cols >= LANES, cols < LANES + 2)

    def twice(chosen):
        chosen = chosen.astype(F32).astype(BF16)
        return jnp.concatenate([chosen, chosen], axis=0)

    widen = [twice(jnp.logical_and(fine, rows == 64 * h + lax.div(cols, 2))) for h in range(2)]
    rows_y, cols_y = iota((256, LANES), 0), iota((256, LANES), 1)
    wanted = lax.div(rows_y, 4) - 8 * lax.div(lax.rem(cols_y, 64), 8) - 4 * lax.div(cols_y, 64)
    spot = lax.rem(cols_y, 8)
    for k in range(3):
        wide = []
        main = jnp.concatenate(pieces_of(r.layers[k], 2), axis=1)
        side = jnp.concatenate(pieces_of(r.zlayers[k], 2), axis=1)
        for h in range(2):
            reach_out = twice(jnp.logical_and(beyond, rows == 64 * h + pairs[k]))
            wide.append(mul(main, widen[h]) + mul(side, reach_out))
        wide = jnp.concatenate(wide, axis=0)
        first = 4 if k else 0
        inside = jnp.logical_and(spot >= first, spot < first + 4)
        repeat = jnp.logical_and(inside, wanted == spot - first).astype(F32).astype(BF16)
        repeat = jnp.concatenate([repeat, repeat], axis=1)
        r.wide[k] = mul(repeat, jnp.concatenate(pieces_of(wide, 2), axis=0))
    band = hat_of(iota((256, LANES), 1) - column_z(role, (256, LANES), 0)).astype(BF16)
    bands = jnp.concatenate([band, band], axis=0)
    for o in range(4):
        r.zc[o, 0:8] = jnp.zeros((8, 256), F32)
        r.zc[o, 264:272] = jnp.zeros((8, 256), F32)
        for b in range(8):
            spot = slice(32 * b, 32 * b + 32)
            total = None
            for layer, planes in ((0, (0, 1)), (1, (2, 3, 4, 5)), (2, (6, 7))):
                part = None
                for i in planes:
                    if o <= i <= o + 4:
                        one = HAT[i - o] * r.m[i, spot]
                        part = one if part is None else part + one
                if part is not None:
                    part = part * r.wide[layer, spot]
                    total = part if total is None else total + part
            r.zc[o, 8 + 32 * b : 40 + 32 * b] = total
        for b in range(8):
            first = 32 * b
            total = (
                3.0 * r.zc[o, 8 + first : 40 + first]
                + 2.0 * (r.zc[o, 7 + first : 39 + first] + r.zc[o, 9 + first : 41 + first])
                + (r.zc[o, 6 + first : 38 + first] + r.zc[o, 10 + first : 42 + first])
            )
            r.sens[o, first : first + 32] = mul(jnp.concatenate(pieces_of(total, 2), axis=1), bands)


FIELD = (9, 2, 80, LANES)
TILE = (1, LANES)
TOP = (18, 8, LANES)


class Refs(dict):
    def __getattr__(self, name):
        return self[name]


def buffers():
    shapes = {
        "edge": (8, 512), "lo": (4, 256, LANES), "hi": (4, 256, LANES), "edges": (3, 8, 512),
        "m": (8, 256, 256), "zc": (8, 272, 256), "psum": (256, LANES),
        "dens": (GYN, 8, LANES), "vf": (2, 8, 2, 64, LANES), "nxhi": (2, 64, LANES), "nyhi": (2, 8, 2, 8, LANES),
        "ncorner": (2, 8, LANES), "bottom": (2,) + TOP, "packed": (3, 8, LANES), "npacked": (3, 8, LANES), "dall": (GYN, 8, LANES),
        "rho": (8, 8, LANES), "store": (9, 5, 7, 8, LANES), "acc": (9, 5, 7, 8, LANES), "grad": (9, 8, LANES),
        "zgrad": (8, LANES), "gall": (GYN, 2, 8, LANES), "grim": (GYN, 8, LANES), "zall": (GYN, 8, LANES),
        "zrim": (GYN, 8, LANES), "layers": (3, 64, LANES), "zlayers": (3, 64, LANES), "wide": (3, 256, 256),
    }
    for name in ("r0", "free", "s0", "r1", "p1", "u1", "r2", "u", "work"):
        shapes[name] = FIELD
        shapes[name + "t"] = TOP
    for n in range(3):
        shapes["tile", n] = shapes["sum", n] = shapes["half", n] = TILE
        shapes["slots", n] = (24, 1, LANES)
    for n in range(2):
        shapes["image", n] = FIELD
        shapes["imaget", n] = shapes["lift", n] = TOP
        shapes["packed", n] = shapes["lifted", n] = (3, 8, LANES)
        shapes["trow", n] = (2, 8, LANES)
        shapes["tface", n] = (16, 8, LANES)
        shapes["xlo", n] = shapes["xhi", n] = (80, LANES)
        shapes["ylo", n] = shapes["yhi", n] = (9, 2, 8, LANES)
        shapes["corners", n] = (4, 8, LANES)
    scratch = {name: pltpu.VMEM(shape, F32) for name, shape in shapes.items()}
    scratch["stiff"] = pltpu.VMEM((2 * ROWS, 2 * ROWS), BF16)
    counts = {"dsend": 7, "drecv": 7, "nsend": 12, "nrecv": 12, "gsend": 16, "grecv": 16, "esend": 4, "erecv": 16}
    for n in range(3):
        counts["rsend", n] = counts["rrecv", n] = 2
        counts["fsend", n] = counts["frecv", n] = 8
        counts["zsend", n] = counts["zrecv", n] = 17
    for name, count in counts.items():
        scratch[name] = pltpu.SemaphoreType.DMA((count,))
    return scratch


def greet_all():
    barrier = pltpu.get_barrier_semaphore()
    devices = [device_at(0, k) for k in range(1, GYN)]
    devices += [cross_device(k) for k in range(1, 16)]
    devices += [device_at(dx, dy) for dx, dy in FACE_MOVES[4:]]
    devices += [slab_device(shift, other) for shift, other in ((1, False), (-1, False), (1, True), (-1, True))]
    for device in devices:
        pl.semaphore_signal(barrier, inc=1, device_id=device, device_id_type=MESH)

    return len(devices)


def whole_kernel(names, *refs):
    r = Refs(zip(names, refs))
    count = greet_all()
    edge_stage(r)
    pack_stage(r)
    pl.semaphore_wait(pltpu.get_barrier_semaphore(), count)
    swap_stage(r)
    inner_stage(r)
    spread_stage(r)
    top_stage(r)
    first_stage(r)
    face_stage(r, 0)
    second_stage(r)
    face_stage(r, 1)
    third_stage(r)
    reduce_stage(r)
    last_stage(r)
    gradient_stage(r)
    unpack_stage(r)
    gradient_end(r)
    final_stage(r)


def on_device(design, force, clamped_dof_mask, stiffness):
    chosen = jnp.asarray(row_table())
    scratch = buffers()
    names = ["design", "force", "mask", "stiffness", "chosen", "sens", "disp"] + list(scratch)
    vmem = pl.BlockSpec(memory_space=pltpu.VMEM)
    return pl.pallas_call(
        functools.partial(whole_kernel, names),
        out_shape=(
            jax.ShapeDtypeStruct((4, 256, LANES), F32),
            jax.ShapeDtypeStruct((3, 16, 16, LANES), F32),
        ),
        in_specs=[vmem] * 5,
        out_specs=(vmem, vmem),
        scratch_shapes=list(scratch.values()),
        compiler_params=pltpu.CompilerParams(
            collective_id=0, has_side_effects=True, vmem_limit_bytes=36 * 1024 * 1024
        ),
        name="compliance",
    )(design, force, clamped_dof_mask, stiffness, chosen)


def solution(mesh):
    fine = P(("gx", "gy"), None, "role")
    nodes = P(None, "gx", "gy", "role")
    return jax.shard_map(
        on_device, mesh=mesh, in_specs=(fine, nodes, nodes, P()), out_specs=(fine, nodes), check_vma=False
    )
```
